256 devices in a mesh: gz: 4 (over y), gx: 16 (over x, z_hi), gy: 4 (over z_lo, core).
Axes of the slice: x: 4, y: 4, z: 8 (z_hi: 4, z_lo: 2; z = z_hi * 2 + z_lo), core: 2. Of those that a mesh axis runs over, the one named last changes fastest.
Arguments:
- potential: float32 [4, 32, 512, 1024], P(None, 'gz', 'gx', 'gy'), may hold values from -4 to 4
- labels: int32 [32, 512, 1024], P('gz', 'gx', 'gy'), may hold values from 0 to 15
- conductivity: float32 [16], replicated, may hold values from 0.1 to 10
- electrodes: int32 [4, 4], replicated, may hold values from 0 to 511
Outputs:
- relaxed: float32 [4, 32, 512, 1024], P(None, 'gz', 'gx', 'gy')
- coarse_residual: float32 [4, 32, 256, 512], P(None, 'gz', 'gx', 'gy')
The draws below stay inside these ranges and needn't reach their ends.
All inputs are finite; a program needn't handle non-finite values.
Results may differ from the reference program's by a relative error of at most 0.0003.
Values sent between devices are 32-bit elements; how exact they have to be, the bound alone decides.
A program may use at most 128 MiB of HBM per device.

```python
import math
import jax
import jax.numpy as jnp
from jax import lax

NSRC = 4
NLAB = 16
ASPECT = 128
NZ = 32
NX = 512
NY = 1024


def draw_potential(key, part):
    key = jax.random.fold_in(key, 7)
    full_shape = (NSRC, NZ, NX, NY)
    sample = jnp.clip(jax.random.normal(key, full_shape, jnp.float32), -4.0, 4.0)
    return sample


def set_ends(result, key, smallest, high):
    place = [jax.random.randint(jax.random.fold_in(key, axis), (), 0, length) for axis, length in enumerate(result.shape)]
    widest = result.shape.index(max(result.shape))
    beside = place[:widest] + [(place[widest] + 1) % result.shape[widest]] + place[widest + 1:]
    return result.at[tuple(place)].set(smallest).at[tuple(beside)].set(high)


def setup_inputs(seed: int = 0) -> dict:
    key_list = jax.random.split(jax.random.key(seed), 5)
    potential = draw_potential(jax.random.fold_in(key_list[4], 71), 0)
    labels = set_ends(jax.random.randint(key_list[1], (NZ, NX, NY), 0, NLAB), jax.random.fold_in(key_list[1], 1), 0, NLAB - 1).astype(jnp.int32)
    conductivity = jnp.clip(jnp.exp(jax.random.uniform(key_list[2], (NLAB,), jnp.float32, math.log(0.1), math.log(10.0))), 0.1, 10.0)
    electrodes = set_ends(jax.random.randint(key_list[3], (NSRC, 4), 0, min(NX, NY)), jax.random.fold_in(key_list[3], 1), 0, (min(NX, NY)) - 1).astype(jnp.int32)
    return dict(potential=potential, labels=labels, conductivity=conductivity, electrodes=electrodes)


def harmonic(first_value, second_value):
    summed = first_value + second_value
    return 2.0 * first_value * second_value / jnp.where(summed > 0, summed, 1.0)


def coefficients(sigma_cells):
    depth_weight = float(ASPECT * ASPECT)
    deeper = jnp.concatenate([jnp.zeros_like(sigma_cells[:1]), sigma_cells, sigma_cells[-1:]], 0)
    padded = jnp.pad(deeper, ((0, 0), (1, 1), (1, 1)))
    middle = padded[1:-1, 1:-1, 1:-1]
    link_shallow = depth_weight * harmonic(padded[:-2, 1:-1, 1:-1], middle)
    link_deep = depth_weight * harmonic(padded[2:, 1:-1, 1:-1], middle)
    link_west = harmonic(padded[1:-1, :-2, 1:-1], middle)
    link_east = harmonic(padded[1:-1, 2:, 1:-1], middle)
    link_south = harmonic(padded[1:-1, 1:-1, :-2], middle)
    link_north = harmonic(padded[1:-1, 1:-1, 2:], middle)
    diagonal = link_shallow + link_deep + link_west + link_east + link_south + link_north
    return link_shallow, link_deep, link_west, link_east, link_south, link_north, diagonal


def lateral(grid_field, link_west, link_east, link_south, link_north):
    padded = jnp.pad(grid_field, ((0, 0), (0, 0), (1, 1), (1, 1)))
    return (link_west * padded[:, :, :-2, 1:-1] + link_east * padded[:, :, 2:, 1:-1]) + (
        link_south * padded[:, :, 1:-1, :-2] + link_north * padded[:, :, 1:-1, 2:])


def line_solve(link_shallow, link_deep, diagonal, right_side):
    def forward(carry, inputs):
        ratio_before, value_before = carry
        shallow_now, deep_now, diagonal_now, right_now = inputs
        denominator = diagonal_now - shallow_now * ratio_before
        ratio_now = deep_now / denominator
        value_now = (right_now + shallow_now * value_before) / denominator
        return (ratio_now, value_now), (ratio_now, value_now)

    start_state = (jnp.zeros(diagonal.shape[1:], jnp.float32),
                   jnp.zeros((right_side.shape[0],) + diagonal.shape[1:], jnp.float32))
    ignored_state, (ratios, values) = lax.scan(
        forward, start_state, (link_shallow, link_deep, diagonal, jnp.moveaxis(right_side, 1, 0)))

    def backward(carry, inputs):
        ratio_now, value_now = inputs
        solved = value_now + ratio_now * carry
        return solved, solved

    ignored_last, solved_rows = lax.scan(backward, jnp.zeros_like(values[0]), (ratios, values), reverse=True)
    return jnp.moveaxis(solved_rows, 0, 1)


def surface_source(electrodes, x_cells, y_cells, depth_cells, on_surface):
    strength = 4.0 * ASPECT
    x_grid = x_cells[None, :, None]
    y_grid = y_cells[None, None, :]
    hit_first = ((x_grid == electrodes[:, 0, None, None]) & (y_grid == electrodes[:, 1, None, None])).astype(jnp.float32)
    hit_second = ((x_grid == electrodes[:, 2, None, None]) & (y_grid == electrodes[:, 3, None, None])).astype(jnp.float32)
    surface = strength * (hit_first - hit_second)
    surface = jnp.where(on_surface, surface, 0.0)
    below_rows = jnp.zeros((surface.shape[0], depth_cells - 1) + surface.shape[1:], jnp.float32)
    return jnp.concatenate([surface[:, None], below_rows], 1)


def reference(potential, labels, conductivity, electrodes):
    sigma_cells = conductivity[labels]
    link_shallow, link_deep, link_west, link_east, link_south, link_north, diagonal = coefficients(sigma_cells)
    sources = surface_source(electrodes, jnp.arange(NX, dtype=jnp.int32), jnp.arange(NY, dtype=jnp.int32), NZ, True)
    first_pass = line_solve(link_shallow, link_deep, diagonal,
                            sources + lateral(potential, link_west, link_east, link_south, link_north))
    relaxed = line_solve(link_shallow, link_deep, diagonal,
                         sources + lateral(first_pass, link_west, link_east, link_south, link_north))
    defect = lateral(relaxed - first_pass, link_west, link_east, link_south, link_north)
    coarse_residual = defect.reshape(NSRC, NZ, NX // 2, 2, NY // 2, 2).sum(axis=(3, 5))
    return relaxed, coarse_residual
```

```python
import functools

import jax
import jax.numpy as jnp
from jax import lax
from jax.experimental import pallas as pl
from jax.experimental.pallas import tpu as pltpu
from jax.sharding import PartitionSpec as P

ASPECT = 128
MESH = pl.DeviceIdType.MESH
F32 = jnp.float32
UNROLL = False


def roll(v, shift, axis):
    return pltpu.roll(v, shift, axis)


def recip(v):
    return pltpu.reciprocal(v, approx=True)


def loop(count, body, init):
    if UNROLL:
        for i in range(count):
            init = body(i, init)
        return init
    return lax.fori_loop(0, count, body, init)


def kernel(
    nz, nx, ny,
    pot, lab, cond, elec, out, coarse,
    p_nat, l_nat, sg, xp, xh, yp, yh, src,
    lw_r, le_r, ls_r, ln_r, inv_r, e_r, rt_r, g_r, r_r, ss,
    fw, fp, ch, on, df, co, ends, wab, km, tt,
    m1s, m1r, m2s, m2r, m3s, m3r,
    loc, zs, zr, xs, xr, ys, yr, ms, mr,
):
    p = lax.axis_index("gz")
    gx = lax.axis_index("gx")
    gy = lax.axis_index("gy")
    has_w, has_e = gx > 0, gx < nx - 1
    has_u, has_d = p > 0, p < nz - 1
    up = p < nz // 2
    is_end = (p == 0) | (p == nz - 1)
    is_mid = (p > 0) & (p < nz - 1)
    west, east = {"gx": gx - 1}, {"gx": gx + 1}
    south, north = {"gy": lax.rem(gy + ny - 1, ny)}, {"gy": lax.rem(gy + 1, ny)}
    above, below = {"gz": p - 1}, {"gz": p + 1}
    lane = lax.broadcasted_iota(jnp.int32, (16, 128), 1)
    lane32 = lax.broadcasted_iota(jnp.int32, (32, 128), 1)
    sub8 = lax.broadcasted_iota(jnp.int32, (8, 128), 0)
    row16 = lax.broadcasted_iota(jnp.int32, (16, 128), 0)

    lab_cp = [
        pltpu.make_async_copy(lab.at[:, :, c * 128:(c + 1) * 128], l_nat.at[:, c], loc.at[0, c])
        for c in range(2)
    ]
    pot_cp = [
        pltpu.make_async_copy(pot.at[:, :, :, c * 128:(c + 1) * 128], p_nat.at[:, :, c], loc.at[1, c])
        for c in range(2)
    ]
    for cp in lab_cp + pot_cp:
        cp.start()

    @pl.when(gx == 0)
    def _():
        xh[:, 0] = jnp.zeros((3, 2, 40, 128), F32)

    @pl.when(gx == nx - 1)
    def _():
        xh[:, 1] = jnp.zeros((3, 2, 40, 128), F32)

    barrier = pltpu.get_barrier_semaphore()

    def greet(device):
        pl.semaphore_signal(barrier, inc=1, device_id=device, device_id_type=MESH)

    greet(south)
    greet(north)
    for cond_here, device in ((has_w, west), (has_e, east), (has_u, above), (has_d, below)):
        pl.when(cond_here)(functools.partial(greet, device))

    for cp in lab_cp:
        cp.wait()
    table = [cond[i] for i in range(16)]

    def lookup(z, carry):
        for c in range(2):
            l = jnp.concatenate([l_nat[z, c, pl.ds(j, 8, stride=4), :] for j in range(4)], 0)
            level = table
            for bit in range(4):
                on_bit = (l & (1 << bit)) != 0
                level = [
                    jnp.where(on_bit, level[2 * i + 1], level[2 * i]) for i in range(len(level) // 2)
                ]
            sg[z + 1, c] = recip(level[0])
        return carry

    loop(8, lookup, 0)

    @pl.when(p == 0)
    def _():
        sg[0] = sg[1]

    @pl.when(p == nz - 1)
    def _():
        sg[9] = sg[8]

    pl.semaphore_wait(
        barrier,
        2 + has_w.astype(jnp.int32) + has_e.astype(jnp.int32)
        + has_u.astype(jnp.int32) + has_d.astype(jnp.int32),
    )

    def remote(src_ref, dst_ref, send, recv, device):
        return pltpu.make_async_remote_copy(
            src_ref=src_ref, dst_ref=dst_ref, send_sem=send, recv_sem=recv,
            device_id=device, device_id_type=MESH,
        )

    to_above = remote(sg.at[1], sg.at[9], zs.at[0], zr.at[1], above)
    to_below = remote(sg.at[8], sg.at[0], zs.at[1], zr.at[0], below)
    pl.when(has_u)(to_above.start)
    pl.when(has_d)(to_below.start)

    def lateral_copies(t):
        n = 40 if t == 0 else 32
        return (
            remote(xp.at[t, 0, :, 0:n], xh.at[t, 1, :, 0:n], xs.at[t, 0], xr.at[t, 1], west),
            remote(xp.at[t, 1, :, 0:n], xh.at[t, 0, :, 0:n], xs.at[t, 1], xr.at[t, 0], east),
            remote(yp.at[t, 0], yh.at[t, 1], ys.at[t, 0], yr.at[t, 1], south),
            remote(yp.at[t, 1], yh.at[t, 0], ys.at[t, 1], yr.at[t, 0], north),
        )

    lat = [lateral_copies(t) for t in range(3)]

    def send_x(t):
        pl.when(has_w)(lat[t][0].start)
        pl.when(has_e)(lat[t][1].start)

    def send_y(t):
        lat[t][2].start()
        lat[t][3].start()

    def wait_x(t):
        pl.when(has_e)(lat[t][0].wait_recv)
        pl.when(has_w)(lat[t][1].wait_recv)

    def wait_y(t):
        lat[t][2].wait_recv()
        lat[t][3].wait_recv()

    def pack_sigma(z, acc):
        acc_s, acc_n = acc
        v0, v1 = sg[z + 1, 0], sg[z + 1, 1]
        acc_s = jnp.where(lane32 == 32 + z, roll(v0, 32 + z, 1), acc_s)
        acc_n = jnp.where(lane32 == 32 + z, roll(v1, 33 + z, 1), acc_n)
        for c, v in ((0, v0), (1, v1)):
            xp[0, 0, c, pl.ds(32 + z, 1), :] = v[0:1]
            xp[0, 1, c, pl.ds(32 + z, 1), :] = v[31:32]
        return acc_s, acc_n

    zero32 = jnp.zeros((32, 128), F32)
    acc = loop(8, pack_sigma, (zero32, zero32))
    for cp in pot_cp:
        cp.wait()

    def pack_pot(z, acc):
        acc_s, acc_n = acc
        for s in range(4):
            k = s * 8 + z
            v0, v1 = (
                jnp.concatenate([p_nat[s, z, c, pl.ds(j, 8, stride=4), :] for j in range(4)], 0)
                for c in range(2)
            )
            acc_s = jnp.where(lane32 == k, roll(v0, k, 1), acc_s)
            acc_n = jnp.where(lane32 == k, roll(v1, k + 1, 1), acc_n)
            for c in range(2):
                xp[0, 0, c, pl.ds(k, 1), :] = p_nat[s, z, c, 0:1, :]
                xp[0, 1, c, pl.ds(k, 1), :] = p_nat[s, z, c, 31:32, :]
        return acc_s, acc_n

    acc = loop(8, pack_pot, acc)
    send_x(0)
    yp[0, 0], yp[0, 1] = acc
    send_y(0)

    here = jnp.where(p == 0, 4.0 * ASPECT, 0.0).astype(F32)
    row32 = lax.broadcasted_iota(jnp.int32, (32, 128), 0)
    x_cell = gx * 32 + 4 * (row32 % 8) + row32 // 8
    for c in range(2):
        y_cell = gy * 256 + c * 128 + lane32
        for s in range(4):
            first = jnp.where((x_cell == elec[s, 0]) & (y_cell == elec[s, 1]), here, 0.0)
            second = jnp.where((x_cell == elec[s, 2]) & (y_cell == elec[s, 3]), here, 0.0)
            src[s, c] = first - second

    def centre(g, v):
        return v[8:24] if g == 0 else jnp.concatenate([v[0:8], v[24:32]], 0)

    def west_east(g, v, halo_w, halo_e):
        if g == 0:
            return v[0:16], v[16:32]
        w0 = jnp.where(sub8 == 0, halo_w(), roll(v[24:32], 1, 0))
        e3 = jnp.where(sub8 == 7, halo_e(), roll(v[0:8], 7, 0))
        return jnp.concatenate([w0, v[16:24]], 0), jnp.concatenate([v[8:16], e3], 0)

    def south_north(v0, v1, halo_s, halo_n):
        r0, r1, q0, q1 = roll(v0, 1, 1), roll(v1, 1, 1), roll(v0, 127, 1), roll(v1, 127, 1)
        return (
            (jnp.where(lane == 0, halo_s, r0), jnp.where(lane == 127, q1, q0)),
            (jnp.where(lane == 0, r0, r1), jnp.where(lane == 127, halo_n, q1)),
        )

    def neighbours(g, t, k, v):
        halo_s = roll(centre(g, yh[t, 0]), lax.rem(128 - k, 128), 1)
        halo_n = roll(centre(g, yh[t, 1]), 127 - k, 1)
        ctr = [centre(g, v[c]) for c in range(2)]
        sn = south_north(ctr[0], ctr[1], halo_s, halo_n)
        res = []
        for c in range(2):
            w, e = west_east(
                g, v[c],
                lambda: xh[t, 0, c, pl.ds(k, 1), :],
                lambda: xh[t, 1, c, pl.ds(k, 1), :],
            )
            res.append((ctr[c], w, e) + sn[c])
        return res

    one = jnp.ones((16, 128), F32)
    mask_w = jnp.where(row16 == 0, jnp.where(has_w, 1.0, 0.0).astype(F32), one)
    mask_e = jnp.where(row16 == 15, jnp.where(has_e, 1.0, 0.0).astype(F32), one)
    mask_s = jnp.where(lane == 0, jnp.where(gy > 0, 1.0, 0.0).astype(F32), one)
    mask_n = jnp.where(lane == 127, jnp.where(gy < ny - 1, 1.0, 0.0).astype(F32), one)
    depth2 = 2.0 * ASPECT * ASPECT

    def setup(g):
        top = jnp.where(has_u, depth2, 0.0).astype(F32)
        zero = jnp.zeros((16, 128), F32)
        init = tuple(
            (
                top * recip(centre(g, sg[0, c]) + centre(g, sg[1, c])),
                zero, one, one, zero,
            )
            for c in range(2)
        )

        def body(z, carry):
            near = neighbours(g, 0, 32 + z, [sg[z + 1, c] for c in range(2)])
            res = []
            for c in range(2):
                sh, ratio, gg, rr, s00 = carry[c]
                here, w, e, s, n = near[c]
                lw, le = 2.0 * recip(here + w), 2.0 * recip(here + e)
                ls, ln = 2.0 * recip(here + s), 2.0 * recip(here + n)
                if g == 1:
                    lw, le = lw * mask_w, le * mask_e
                if c == 0:
                    ls = ls * mask_s
                else:
                    ln = ln * mask_n
                dp = depth2 * recip(here + centre(g, sg[z + 2, c]))
                diag = sh + dp + lw + le + ls + ln
                inv = recip(diag - sh * ratio)
                ee = sh * inv
                ratio = dp * inv
                gg = ee * gg
                s00 = s00 + rr * gg
                lw_r[g, z, c], le_r[g, z, c], ls_r[g, z, c], ln_r[g, z, c] = lw, le, ls, ln
                inv_r[g, z, c], rt_r[g, z, c], g_r[g, z, c], r_r[g, z, c] = inv, ratio, gg, rr
                e_r[g, z, c] = jnp.where(z == 0, inv, ee)
                res.append((dp, ratio, gg, rr * ratio, s00))
            return tuple(res)

        last = loop(8, body, init)
        for c in range(2):
            ss[g, 0, c], ss[g, 1, c], ss[g, 2, c], ss[g, 3, c] = (
                last[c][4], last[c][2], last[c][3], last[c][1],
            )

    def forward(g, t, load):
        for half in range(2):
            def body(z, carry):
                res = []
                for i in range(2):
                    s = 2 * half + i
                    near = neighbours(g, t, s * 8 + z, [load(s, z, c) for c in range(2)])
                    for c in range(2):
                        f, first = carry[2 * i + c]
                        here, w, e, so, no = near[c]
                        rhs = (lw_r[g, z, c] * w + le_r[g, z, c] * e) + (
                            ls_r[g, z, c] * so + ln_r[g, z, c] * no
                        )
                        f = rhs * inv_r[g, z, c] + e_r[g, z, c] * f
                        fw[g, s, z, c] = f
                        res.append((f, first + r_r[g, z, c] * f))
                return tuple(res)

            zero = jnp.zeros((16, 128), F32)
            init = tuple(
                (centre(g, src[2 * half + i, c]), zero) for i in range(2) for c in range(2)
            )
            last = loop(8, body, init)
            for i in range(2):
                for c in range(2):
                    ends[g, 1, 2 * half + i, c], ends[g, 0, 2 * half + i, c] = last[2 * i + c]

    i_out, i_in = jnp.where(up, 0, 1), jnp.where(up, 1, 0)
    i_oo, i_oi = jnp.where(up, 0, 3), jnp.where(up, 1, 2)
    i_io, i_ii = jnp.where(up, 2, 1), jnp.where(up, 3, 0)
    end_of = {"gz": jnp.where(up, 0, nz - 1)}
    mid_of = {"gz": jnp.where(up, 1, nz - 2)}
    twin = {"gz": nz - 1 - p}

    def hops(t, g):
        n = 5 if t == 0 else 4
        return (
            remote(m1s.at[t, g, 0:n], m1r.at[t, g, 0:n], ms.at[t, g, 0], mr.at[t, g, 0], mid_of),
            remote(m2s.at[t, g, 0:n], m2r.at[t, g, 0:n], ms.at[t, g, 1], mr.at[t, g, 1], twin),
            remote(m3s.at[t, g], m3r.at[t, g], ms.at[t, g, 2], mr.at[t, g, 2], end_of),
        )

    hop = [[hops(t, g) for g in range(2)] for t in range(2)]
    pairs = [(s, c) for s in range(4) for c in range(2)]

    def end_send(t, g):
        @pl.when(is_end)
        def _():
            for s, c in pairs:
                m1s[t, g, s, c] = ends[g, i_in, s, c]
            if t == 0:
                for c in range(2):
                    m1s[t, g, 4, c] = ss[g, i_ii, c]
            hop[t][g][0].start()

    def mid_forward(t, g):
        @pl.when(is_mid)
        def _():
            hop[t][g][0].wait_recv()
            for c in range(2):
                b_out = m1r[0, g, 4, c]
                if t == 0:
                    q = 1.0 / (1.0 - ss[g, i_oo, c] * b_out)
                    km[g, 0, c] = q
                    km[g, 1, c] = q * ss[g, i_io, c]
                    m2s[0, g, 4, c] = ss[g, i_ii, c] + ss[g, i_oi, c] * b_out * q * ss[g, i_io, c]
                for s in range(4):
                    a_out = m1r[t, g, s, c]
                    first = (ends[g, i_out, s, c] + ss[g, i_oo, c] * a_out) * km[g, 0, c]
                    tt[g, s, c] = first
                    m2s[t, g, s, c] = ends[g, i_in, s, c] + ss[g, i_oi, c] * (a_out + b_out * first)
            hop[t][g][1].start()

    def mid_solve(t, g):
        @pl.when(is_mid)
        def _():
            hop[t][g][1].wait_recv()
            for c in range(2):
                b_out, b_in, b_mine = m1r[0, g, 4, c], m2r[0, g, 4, c], m2s[0, g, 4, c]
                if t == 0:
                    km[g, 2, c] = 1.0 / (1.0 - b_in * b_mine)
                for s in range(4):
                    w_in = (m2r[t, g, s, c] + b_in * m2s[t, g, s, c]) * km[g, 2, c]
                    first = tt[g, s, c] + km[g, 1, c] * w_in
                    m3s[t, g, s, c] = first
                    wab[g, i_in, s, c] = w_in
                    wab[g, i_out, s, c] = m1r[t, g, s, c] + b_out * first
            hop[t][g][2].start()

    def end_solve(t, g):
        @pl.when(is_end)
        def _():
            hop[t][g][2].wait_recv()
            for s, c in pairs:
                wab[g, i_in, s, c] = m3r[t, g, s, c]
                wab[g, i_out, s, c] = jnp.zeros((16, 128), F32)

    def backward(t, g, emit):
        for half in range(2):
            def body(step, carry):
                z = 7 - step
                acc_s, acc_n, w_next = carry
                res = []
                for i in range(2):
                    s = 2 * half + i
                    k = s * 8 + z
                    both = []
                    for c in range(2):
                        w = fw[g, s, z, c] + g_r[g, z, c] * wab[g, 0, s, c] + (
                            rt_r[g, z, c] * w_next[2 * i + c]
                        )
                        res.append(w)
                        v = emit(s, z, c, w)
                        if g == 1:
                            xp[t + 1, 0, c, pl.ds(k, 1), :] = v[0:1]
                            xp[t + 1, 1, c, pl.ds(k, 1), :] = v[15:16]
                        both.append(v)
                    acc_s = jnp.where(lane == k, roll(both[0], k, 1), acc_s)
                    acc_n = jnp.where(lane == k, roll(both[1], k + 1, 1), acc_n)
                return acc_s, acc_n, tuple(res)

            if half == 0:
                zero = jnp.zeros((16, 128), F32)
                acc = (zero, zero)
            first = tuple(wab[g, 1, 2 * half + i, c] for i in range(2) for c in range(2))
            acc = loop(8, body, acc + (first,))[:2]
        for d in range(2):
            if g == 0:
                yp[t + 1, d, 8:24] = acc[d]
            else:
                yp[t + 1, d, 0:8] = acc[d][0:8]
                yp[t + 1, d, 24:32] = acc[d][8:16]

    def put(ref, g, s, z, c, v):
        if g == 0:
            ref[s, z, c, 8:24] = v
        else:
            ref[s, z, c, 0:8] = v[0:8]
            ref[s, z, c, 24:32] = v[8:16]

    def emit_first(g):
        def emit(s, z, c, w):
            put(fp, g, s, z, c, w)
            return w
        return emit

    def emit_relaxed(g):
        rows = (1, 2) if g == 0 else (0, 3)
        def emit(s, z, c, w):
            change = w - centre(g, fp[s, z, c])
            put(ch, g, s, z, c, change)
            for i in range(2):
                on[s, z, c, pl.ds(rows[i], 8, stride=4), :] = w[8 * i:8 * i + 8]
            return change
        return emit

    def load_pot(s, z, c):
        return jnp.concatenate([p_nat[s, z, c, pl.ds(j, 8, stride=4), :] for j in range(4)], 0)

    def load_first(s, z, c):
        return fp[s, z, c]

    def chain(t):
        for g in range(2):
            mid_forward(t, g)
        for g in range(2):
            mid_solve(t, g)
        for g in range(2):
            end_solve(t, g)
            backward(t, g, (emit_first if t == 0 else emit_relaxed)(g))

    wait_y(0)
    pl.when(has_d)(to_above.wait_recv)
    pl.when(has_u)(to_below.wait_recv)
    setup(0)
    forward(0, 0, load_pot)
    end_send(0, 0)
    wait_x(0)
    setup(1)
    forward(1, 0, load_pot)
    end_send(0, 1)
    chain(0)
    send_x(1)
    send_y(1)

    wait_y(1)
    forward(0, 1, load_first)
    end_send(1, 0)
    wait_x(1)
    forward(1, 1, load_first)
    end_send(1, 1)
    chain(1)
    send_x(2)
    send_y(2)
    out_cp = [
        pltpu.make_async_copy(on.at[:, :, c], out.at[:, :, :, c * 128:(c + 1) * 128], loc.at[0, c])
        for c in range(2)
    ]
    for cp in out_cp:
        cp.start()

    lane8 = lax.broadcasted_iota(jnp.int32, (8, 128), 1)
    even = (2 * lane8) % 128

    def squeeze(v):
        return jnp.take_along_axis(v + roll(v, 127, 1), even, axis=1)

    def defect(g):
        def body(z, carry):
            for s in range(4):
                near = neighbours(g, 2, s * 8 + z, [ch[s, z, c] for c in range(2)])
                low, high = [], []
                for c in range(2):
                    here, w, e, so, no = near[c]
                    d = (lw_r[g, z, c] * w + le_r[g, z, c] * e) + (
                        ls_r[g, z, c] * so + ln_r[g, z, c] * no
                    )
                    if g == 0:
                        df[s, z, c] = d
                    else:
                        d = d + df[s, z, c]
                        low.append(squeeze(d[0:8]))
                        high.append(squeeze(d[8:16]))
                if g == 1:
                    co[s, z, pl.ds(0, 8, stride=2), :] = jnp.where(lane8 < 64, low[0], low[1])
                    co[s, z, pl.ds(1, 8, stride=2), :] = jnp.where(lane8 < 64, high[0], high[1])
            return carry

        loop(8, body, 0)

    wait_y(2)
    defect(0)
    wait_x(2)
    defect(1)
    co_cp = pltpu.make_async_copy(co, coarse, loc.at[1, 0])
    co_cp.start()

    pl.when(has_u)(to_above.wait_send)
    pl.when(has_d)(to_below.wait_send)
    for t in range(3):
        pl.when(has_w)(lat[t][0].wait_send)
        pl.when(has_e)(lat[t][1].wait_send)
        lat[t][2].wait_send()
        lat[t][3].wait_send()
    for t in range(2):
        for g in range(2):
            pl.when(is_end)(hop[t][g][0].wait_send)
            pl.when(is_mid)(hop[t][g][1].wait_send)
            pl.when(is_mid)(hop[t][g][2].wait_send)
    for cp in out_cp:
        cp.wait()
    co_cp.wait()


def solution(mesh):
    nz, nx, ny = mesh.shape["gz"], mesh.shape["gx"], mesh.shape["gy"]

    def body(potential, labels, conductivity, electrodes):
        coef = pltpu.VMEM((2, 8, 2, 16, 128), F32)
        field = pltpu.VMEM((4, 8, 2, 32, 128), F32)
        msg5 = pltpu.VMEM((2, 2, 5, 2, 16, 128), F32)
        msg4 = pltpu.VMEM((2, 2, 4, 2, 16, 128), F32)
        dma = pltpu.SemaphoreType.DMA
        return pl.pallas_call(
            functools.partial(kernel, nz, nx, ny),
            out_shape=(
                jax.ShapeDtypeStruct((4, 8, 32, 256), F32),
                jax.ShapeDtypeStruct((4, 8, 16, 128), F32),
            ),
            in_specs=[
                pl.BlockSpec(memory_space=pl.ANY),
                pl.BlockSpec(memory_space=pl.ANY),
                pl.BlockSpec(memory_space=pltpu.SMEM),
                pl.BlockSpec(memory_space=pltpu.SMEM),
            ],
            out_specs=(pl.BlockSpec(memory_space=pl.ANY), pl.BlockSpec(memory_space=pl.ANY)),
            scratch_shapes=[
                field,
                pltpu.VMEM((8, 2, 32, 128), jnp.int32),
                pltpu.VMEM((10, 2, 32, 128), F32),
                pltpu.VMEM((3, 2, 2, 40, 128), F32),
                pltpu.VMEM((3, 2, 2, 40, 128), F32),
                pltpu.VMEM((3, 2, 32, 128), F32),
                pltpu.VMEM((3, 2, 32, 128), F32),
                pltpu.VMEM((4, 2, 32, 128), F32),
                coef, coef, coef, coef, coef, coef, coef, coef, coef,
                pltpu.VMEM((2, 4, 2, 16, 128), F32),
                pltpu.VMEM((2, 4, 8, 2, 16, 128), F32),
                field, field, field,
                pltpu.VMEM((4, 8, 2, 16, 128), F32),
                pltpu.VMEM((4, 8, 16, 128), F32),
                pltpu.VMEM((2, 2, 4, 2, 16, 128), F32),
                pltpu.VMEM((2, 2, 4, 2, 16, 128), F32),
                pltpu.VMEM((2, 3, 2, 16, 128), F32),
                pltpu.VMEM((2, 4, 2, 16, 128), F32),
                msg5, msg5, msg5, msg5, msg4, msg4,
                dma((2, 2)), dma((2,)), dma((2,)),
                dma((3, 2)), dma((3, 2)), dma((3, 2)), dma((3, 2)),
                dma((2, 2, 3)), dma((2, 2, 3)),
            ],
            compiler_params=pltpu.CompilerParams(
                collective_id=0, has_side_effects=True, vmem_limit_bytes=40 * 1024 * 1024,
            ),
        )(potential, labels, conductivity, electrodes)

    return jax.shard_map(
        body,
        mesh=mesh,
        in_specs=(P(None, "gz", "gx", "gy"), P("gz", "gx", "gy"), P(), P()),
        out_specs=(P(None, "gz", "gx", "gy"), P(None, "gz", "gx", "gy")),
        check_vma=False,
    )
```

```python
import functools

import jax
import jax.numpy as jnp
from jax import lax
from jax.experimental import pallas as pl
from jax.experimental.pallas import tpu as pltpu
from jax.sharding import PartitionSpec as P

ASPECT = 128
MESH = pl.DeviceIdType.MESH
F32 = jnp.float32
UNROLL = True


def roll(v, shift, axis):
    return pltpu.roll(v, shift, axis)


def recip(v):
    return pltpu.reciprocal(v, approx=True)


def loop(count, body, init):
    if UNROLL:
        for i in range(count):
            init = body(i, init)
        return init
    return lax.fori_loop(0, count, body, init)


def kernel(
    nz, nx, ny,
    pot, lab, cond, elec, out, coarse,
    p_nat, l_nat, sg, xp, xh, yp, yh, src,
    lw_r, le_r, ls_r, ln_r, inv_r, e_r, rt_r, g_r, r_r, ss,
    fw, fp, ch, on, df, co, ends, wab, km, tt,
    m1s, m1r, m2s, m2r, m3s, m3r,
    loc, zs, zr, xs, xr, ys, yr, ms, mr,
):
    p = lax.axis_index("gz")
    gx = lax.axis_index("gx")
    gy = lax.axis_index("gy")
    has_w, has_e = gx > 0, gx < nx - 1
    has_u, has_d = p > 0, p < nz - 1
    up = p < nz // 2
    is_end = (p == 0) | (p == nz - 1)
    is_mid = (p > 0) & (p < nz - 1)
    west, east = {"gx": gx - 1}, {"gx": gx + 1}
    south, north = {"gy": lax.rem(gy + ny - 1, ny)}, {"gy": lax.rem(gy + 1, ny)}
    above, below = {"gz": p - 1}, {"gz": p + 1}
    lane = lax.broadcasted_iota(jnp.int32, (16, 128), 1)
    lane32 = lax.broadcasted_iota(jnp.int32, (32, 128), 1)
    sub8 = lax.broadcasted_iota(jnp.int32, (8, 128), 0)
    row16 = lax.broadcasted_iota(jnp.int32, (16, 128), 0)

    lab_cp = [
        pltpu.make_async_copy(lab.at[:, :, c * 128:(c + 1) * 128], l_nat.at[:, c], loc.at[0, c])
        for c in range(2)
    ]
    pot_cp = [
        pltpu.make_async_copy(pot.at[:, :, :, c * 128:(c + 1) * 128], p_nat.at[:, :, c], loc.at[1, c])
        for c in range(2)
    ]
    for cp in lab_cp + pot_cp:
        cp.start()

    @pl.when(gx == 0)
    def _():
        xh[:, 0] = jnp.zeros((3, 2, 40, 128), F32)

    @pl.when(gx == nx - 1)
    def _():
        xh[:, 1] = jnp.zeros((3, 2, 40, 128), F32)

    barrier = pltpu.get_barrier_semaphore()

    def greet(device):
        pl.semaphore_signal(barrier, inc=1, device_id=device, device_id_type=MESH)

    greet(south)
    greet(north)
    for cond_here, device in ((has_w, west), (has_e, east), (has_u, above), (has_d, below)):
        pl.when(cond_here)(functools.partial(greet, device))

    for cp in lab_cp:
        cp.wait()
    table = [cond[i] for i in range(16)]

    def lookup(z, carry):
        for c in range(2):
            l = jnp.concatenate([l_nat[z, c, pl.ds(j, 8, stride=4), :] for j in range(4)], 0)
            level = table
            for bit in range(4):
                on_bit = (l & (1 << bit)) != 0
                level = [
                    jnp.where(on_bit, level[2 * i + 1], level[2 * i]) for i in range(len(level) // 2)
                ]
            sg[z + 1, c] = recip(level[0])
        return carry

    loop(8, lookup, 0)

    @pl.when(p == 0)
    def _():
        sg[0] = sg[1]

    @pl.when(p == nz - 1)
    def _():
        sg[9] = sg[8]

    def remote(src_ref, dst_ref, send, recv, device):
        return pltpu.make_async_remote_copy(
            src_ref=src_ref, dst_ref=dst_ref, send_sem=send, recv_sem=recv,
            device_id=device, device_id_type=MESH,
        )

    to_above = remote(sg.at[1], sg.at[9], zs.at[0], zr.at[1], above)
    to_below = remote(sg.at[8], sg.at[0], zs.at[1], zr.at[0], below)

    def lateral_copies(t):
        n = 40 if t == 0 else 32
        return (
            remote(xp.at[t, 0, :, 0:n], xh.at[t, 1, :, 0:n], xs.at[t, 0], xr.at[t, 1], west),
            remote(xp.at[t, 1, :, 0:n], xh.at[t, 0, :, 0:n], xs.at[t, 1], xr.at[t, 0], east),
            remote(yp.at[t, 0], yh.at[t, 1], ys.at[t, 0], yr.at[t, 1], south),
            remote(yp.at[t, 1], yh.at[t, 0], ys.at[t, 1], yr.at[t, 0], north),
        )

    lat = [lateral_copies(t) for t in range(3)]

    def send_x(t):
        pl.when(has_w)(lat[t][0].start)
        pl.when(has_e)(lat[t][1].start)

    def send_y(t):
        lat[t][2].start()
        lat[t][3].start()

    def wait_x(t):
        pl.when(has_e)(lat[t][0].wait_recv)
        pl.when(has_w)(lat[t][1].wait_recv)

    def wait_y(t):
        lat[t][2].wait_recv()
        lat[t][3].wait_recv()

    def pack_sigma(z, acc):
        acc_s, acc_n = acc
        v0, v1 = sg[z + 1, 0], sg[z + 1, 1]
        acc_s = jnp.where(lane32 == 32 + z, roll(v0, 32 + z, 1), acc_s)
        acc_n = jnp.where(lane32 == 32 + z, roll(v1, 33 + z, 1), acc_n)
        for c, v in ((0, v0), (1, v1)):
            xp[0, 0, c, pl.ds(32 + z, 1), :] = v[0:1]
            xp[0, 1, c, pl.ds(32 + z, 1), :] = v[31:32]
        return acc_s, acc_n

    zero32 = jnp.zeros((32, 128), F32)
    acc = loop(8, pack_sigma, (zero32, zero32))
    for cp in pot_cp:
        cp.wait()

    def pack_pot(z, acc):
        acc_s, acc_n = acc
        for s in range(4):
            k = s * 8 + z
            v0, v1 = (
                jnp.concatenate([p_nat[s, z, c, pl.ds(j, 8, stride=4), :] for j in range(4)], 0)
                for c in range(2)
            )
            acc_s = jnp.where(lane32 == k, roll(v0, k, 1), acc_s)
            acc_n = jnp.where(lane32 == k, roll(v1, k + 1, 1), acc_n)
            for c in range(2):
                xp[0, 0, c, pl.ds(k, 1), :] = p_nat[s, z, c, 0:1, :]
                xp[0, 1, c, pl.ds(k, 1), :] = p_nat[s, z, c, 31:32, :]
        return acc_s, acc_n

    acc = loop(8, pack_pot, acc)
    yp[0, 0], yp[0, 1] = acc
    pl.semaphore_wait(
        barrier,
        2 + has_w.astype(jnp.int32) + has_e.astype(jnp.int32)
        + has_u.astype(jnp.int32) + has_d.astype(jnp.int32),
    )

    send_x(0)
    pl.when(has_u)(to_above.start)
    pl.when(has_d)(to_below.start)
    send_y(0)

    here = jnp.where(p == 0, 4.0 * ASPECT, 0.0).astype(F32)
    row32 = lax.broadcasted_iota(jnp.int32, (32, 128), 0)
    x_cell = gx * 32 + 4 * (row32 % 8) + row32 // 8
    for c in range(2):
        y_cell = gy * 256 + c * 128 + lane32
        for s in range(4):
            first = jnp.where((x_cell == elec[s, 0]) & (y_cell == elec[s, 1]), here, 0.0)
            second = jnp.where((x_cell == elec[s, 2]) & (y_cell == elec[s, 3]), here, 0.0)
            src[s, c] = first - second

    def centre(g, v):
        return v[8:24] if g == 0 else jnp.concatenate([v[0:8], v[24:32]], 0)

    def west_east(g, v, halo_w, halo_e):
        if g == 0:
            return v[0:16], v[16:32]
        w0 = jnp.where(sub8 == 0, halo_w(), roll(v[24:32], 1, 0))
        e3 = jnp.where(sub8 == 7, halo_e(), roll(v[0:8], 7, 0))
        return jnp.concatenate([w0, v[16:24]], 0), jnp.concatenate([v[8:16], e3], 0)

    def south_north(v0, v1, halo_s, halo_n):
        r0, r1, q0, q1 = roll(v0, 1, 1), roll(v1, 1, 1), roll(v0, 127, 1), roll(v1, 127, 1)
        return (
            (jnp.where(lane == 0, halo_s, r0), jnp.where(lane == 127, q1, q0)),
            (jnp.where(lane == 0, r0, r1), jnp.where(lane == 127, halo_n, q1)),
        )

    def neighbours(g, t, k, v):
        halo_s = roll(centre(g, yh[t, 0]), lax.rem(128 - k, 128), 1)
        halo_n = roll(centre(g, yh[t, 1]), 127 - k, 1)
        ctr = [centre(g, v[c]) for c in range(2)]
        sn = south_north(ctr[0], ctr[1], halo_s, halo_n)
        res = []
        for c in range(2):
            w, e = west_east(
                g, v[c],
                lambda: xh[t, 0, c, pl.ds(k, 1), :],
                lambda: xh[t, 1, c, pl.ds(k, 1), :],
            )
            res.append((ctr[c], w, e) + sn[c])
        return res

    one = jnp.ones((16, 128), F32)
    mask_w = jnp.where(row16 == 0, jnp.where(has_w, 1.0, 0.0).astype(F32), one)
    mask_e = jnp.where(row16 == 15, jnp.where(has_e, 1.0, 0.0).astype(F32), one)
    mask_s = jnp.where(lane == 0, jnp.where(gy > 0, 1.0, 0.0).astype(F32), one)
    mask_n = jnp.where(lane == 127, jnp.where(gy < ny - 1, 1.0, 0.0).astype(F32), one)
    depth2 = 2.0 * ASPECT * ASPECT

    def setup(g):
        top = jnp.where(has_u, depth2, 0.0).astype(F32)
        zero = jnp.zeros((16, 128), F32)
        init = tuple(
            (
                top * recip(centre(g, sg[0, c]) + centre(g, sg[1, c])),
                zero, one, one, zero,
            )
            for c in range(2)
        )

        def body(z, carry):
            near = neighbours(g, 0, 32 + z, [sg[z + 1, c] for c in range(2)])
            res = []
            for c in range(2):
                sh, ratio, gg, rr, s00 = carry[c]
                here, w, e, s, n = near[c]
                lw, le = 2.0 * recip(here + w), 2.0 * recip(here + e)
                ls, ln = 2.0 * recip(here + s), 2.0 * recip(here + n)
                if g == 1:
                    lw, le = lw * mask_w, le * mask_e
                if c == 0:
                    ls = ls * mask_s
                else:
                    ln = ln * mask_n
                dp = depth2 * recip(here + centre(g, sg[z + 2, c]))
                diag = sh + dp + lw + le + ls + ln
                inv = recip(diag - sh * ratio)
                ee = sh * inv
                ratio = dp * inv
                gg = ee * gg
                s00 = s00 + rr * gg
                lw_r[g, z, c], le_r[g, z, c], ls_r[g, z, c], ln_r[g, z, c] = lw, le, ls, ln
                inv_r[g, z, c], rt_r[g, z, c], g_r[g, z, c], r_r[g, z, c] = inv, ratio, gg, rr
                e_r[g, z, c] = jnp.where(z == 0, inv, ee)
                res.append((dp, ratio, gg, rr * ratio, s00))
            return tuple(res)

        last = loop(8, body, init)
        for c in range(2):
            ss[g, 0, c], ss[g, 1, c], ss[g, 2, c], ss[g, 3, c] = (
                last[c][4], last[c][2], last[c][3], last[c][1],
            )

    def forward(g, t, load):
        for half in range(2):
            def body(z, carry):
                res = []
                for i in range(2):
                    s = 2 * half + i
                    near = neighbours(g, t, s * 8 + z, [load(s, z, c) for c in range(2)])
                    for c in range(2):
                        f, first = carry[2 * i + c]
                        here, w, e, so, no = near[c]
                        rhs = (lw_r[g, z, c] * w + le_r[g, z, c] * e) + (
                            ls_r[g, z, c] * so + ln_r[g, z, c] * no
                        )
                        f = rhs * inv_r[g, z, c] + e_r[g, z, c] * f
                        fw[g, s, z, c] = f
                        res.append((f, first + r_r[g, z, c] * f))
                return tuple(res)

            zero = jnp.zeros((16, 128), F32)
            init = tuple(
                (centre(g, src[2 * half + i, c]), zero) for i in range(2) for c in range(2)
            )
            last = loop(8, body, init)
            for i in range(2):
                for c in range(2):
                    ends[g, 1, 2 * half + i, c], ends[g, 0, 2 * half + i, c] = last[2 * i + c]

    i_out, i_in = jnp.where(up, 0, 1), jnp.where(up, 1, 0)
    i_oo, i_oi = jnp.where(up, 0, 3), jnp.where(up, 1, 2)
    i_io, i_ii = jnp.where(up, 2, 1), jnp.where(up, 3, 0)
    end_of = {"gz": jnp.where(up, 0, nz - 1)}
    mid_of = {"gz": jnp.where(up, 1, nz - 2)}
    twin = {"gz": nz - 1 - p}

    def hops(t, g):
        n = 5 if t == 0 else 4
        return (
            remote(m1s.at[t, g, 0:n], m1r.at[t, g, 0:n], ms.at[t, g, 0], mr.at[t, g, 0], mid_of),
            remote(m2s.at[t, g, 0:n], m2r.at[t, g, 0:n], ms.at[t, g, 1], mr.at[t, g, 1], twin),
            remote(m3s.at[t, g], m3r.at[t, g], ms.at[t, g, 2], mr.at[t, g, 2], end_of),
        )

    hop = [[hops(t, g) for g in range(2)] for t in range(2)]
    pairs = [(s, c) for s in range(4) for c in range(2)]

    def end_send(t, g):
        @pl.when(is_end)
        def _():
            for s, c in pairs:
                m1s[t, g, s, c] = ends[g, i_in, s, c]
            if t == 0:
                for c in range(2):
                    m1s[t, g, 4, c] = ss[g, i_ii, c]
            hop[t][g][0].start()

    def mid_forward(t, g):
        @pl.when(is_mid)
        def _():
            hop[t][g][0].wait_recv()
            for c in range(2):
                b_out = m1r[0, g, 4, c]
                if t == 0:
                    q = 1.0 / (1.0 - ss[g, i_oo, c] * b_out)
                    km[g, 0, c] = q
                    km[g, 1, c] = q * ss[g, i_io, c]
                    m2s[0, g, 4, c] = ss[g, i_ii, c] + ss[g, i_oi, c] * b_out * q * ss[g, i_io, c]
                for s in range(4):
                    a_out = m1r[t, g, s, c]
                    first = (ends[g, i_out, s, c] + ss[g, i_oo, c] * a_out) * km[g, 0, c]
                    tt[g, s, c] = first
                    m2s[t, g, s, c] = ends[g, i_in, s, c] + ss[g, i_oi, c] * (a_out + b_out * first)
            hop[t][g][1].start()

    def mid_solve(t, g):
        @pl.when(is_mid)
        def _():
            hop[t][g][1].wait_recv()
            for c in range(2):
                b_out, b_in, b_mine = m1r[0, g, 4, c], m2r[0, g, 4, c], m2s[0, g, 4, c]
                if t == 0:
                    km[g, 2, c] = 1.0 / (1.0 - b_in * b_mine)
                for s in range(4):
                    w_in = (m2r[t, g, s, c] + b_in * m2s[t, g, s, c]) * km[g, 2, c]
                    first = tt[g, s, c] + km[g, 1, c] * w_in
                    m3s[t, g, s, c] = first
                    wab[g, i_in, s, c] = w_in
                    wab[g, i_out, s, c] = m1r[t, g, s, c] + b_out * first
            hop[t][g][2].start()

    def end_solve(t, g):
        @pl.when(is_end)
        def _():
            hop[t][g][2].wait_recv()
            for s, c in pairs:
                wab[g, i_in, s, c] = m3r[t, g, s, c]
                wab[g, i_out, s, c] = jnp.zeros((16, 128), F32)

    def backward(t, g, emit):
        for half in range(2):
            def body(step, carry):
                z = 7 - step
                acc_s, acc_n, w_next = carry
                res = []
                for i in range(2):
                    s = 2 * half + i
                    k = s * 8 + z
                    both = []
                    for c in range(2):
                        w = fw[g, s, z, c] + g_r[g, z, c] * wab[g, 0, s, c] + (
                            rt_r[g, z, c] * w_next[2 * i + c]
                        )
                        res.append(w)
                        v = emit(s, z, c, w)
                        if g == 1:
                            xp[t + 1, 0, c, pl.ds(k, 1), :] = v[0:1]
                            xp[t + 1, 1, c, pl.ds(k, 1), :] = v[15:16]
                        both.append(v)
                    acc_s = jnp.where(lane == k, roll(both[0], k, 1), acc_s)
                    acc_n = jnp.where(lane == k, roll(both[1], k + 1, 1), acc_n)
                return acc_s, acc_n, tuple(res)

            if half == 0:
                zero = jnp.zeros((16, 128), F32)
                acc = (zero, zero)
            first = tuple(wab[g, 1, 2 * half + i, c] for i in range(2) for c in range(2))
            acc = loop(8, body, acc + (first,))[:2]
        for d in range(2):
            if g == 0:
                yp[t + 1, d, 8:24] = acc[d]
            else:
                yp[t + 1, d, 0:8] = acc[d][0:8]
                yp[t + 1, d, 24:32] = acc[d][8:16]

    def put(ref, g, s, z, c, v):
        if g == 0:
            ref[s, z, c, 8:24] = v
        else:
            ref[s, z, c, 0:8] = v[0:8]
            ref[s, z, c, 24:32] = v[8:16]

    def emit_first(g):
        def emit(s, z, c, w):
            put(fp, g, s, z, c, w)
            return w
        return emit

    def emit_relaxed(g):
        rows = (1, 2) if g == 0 else (0, 3)
        def emit(s, z, c, w):
            change = w - centre(g, fp[s, z, c])
            put(ch, g, s, z, c, change)
            for i in range(2):
                on[s, z, c, pl.ds(rows[i], 8, stride=4), :] = w[8 * i:8 * i + 8]
            return change
        return emit

    def load_pot(s, z, c):
        return jnp.concatenate([p_nat[s, z, c, pl.ds(j, 8, stride=4), :] for j in range(4)], 0)

    def load_first(s, z, c):
        return fp[s, z, c]

    def chain(t):
        for g in range(2):
            mid_forward(t, g)
        for g in range(2):
            mid_solve(t, g)
        for g in range(2):
            end_solve(t, g)
            backward(t, g, (emit_first if t == 0 else emit_relaxed)(g))

    wait_y(0)
    pl.when(has_d)(to_above.wait_recv)
    pl.when(has_u)(to_below.wait_recv)
    setup(0)
    forward(0, 0, load_pot)
    end_send(0, 0)
    wait_x(0)
    setup(1)
    forward(1, 0, load_pot)
    end_send(0, 1)
    chain(0)
    send_x(1)
    send_y(1)

    wait_y(1)
    forward(0, 1, load_first)
    end_send(1, 0)
    wait_x(1)
    forward(1, 1, load_first)
    end_send(1, 1)
    chain(1)
    send_x(2)
    send_y(2)
    out_cp = [
        pltpu.make_async_copy(on.at[:, :, c], out.at[:, :, :, c * 128:(c + 1) * 128], loc.at[0, c])
        for c in range(2)
    ]
    for cp in out_cp:
        cp.start()

    lane8 = lax.broadcasted_iota(jnp.int32, (8, 128), 1)
    even = (2 * lane8) % 128

    def squeeze(v):
        return jnp.take_along_axis(v + roll(v, 127, 1), even, axis=1)

    def defect(g):
        def body(z, carry):
            for s in range(4):
                near = neighbours(g, 2, s * 8 + z, [ch[s, z, c] for c in range(2)])
                low, high = [], []
                for c in range(2):
                    here, w, e, so, no = near[c]
                    d = (lw_r[g, z, c] * w + le_r[g, z, c] * e) + (
                        ls_r[g, z, c] * so + ln_r[g, z, c] * no
                    )
                    if g == 0:
                        df[s, z, c] = d
                    else:
                        d = d + df[s, z, c]
                        low.append(squeeze(d[0:8]))
                        high.append(squeeze(d[8:16]))
                if g == 1:
                    co[s, z, pl.ds(0, 8, stride=2), :] = jnp.where(lane8 < 64, low[0], low[1])
                    co[s, z, pl.ds(1, 8, stride=2), :] = jnp.where(lane8 < 64, high[0], high[1])
            return carry

        loop(8, body, 0)

    wait_y(2)
    defect(0)
    wait_x(2)
    defect(1)
    co_cp = pltpu.make_async_copy(co, coarse, loc.at[1, 0])
    co_cp.start()

    pl.when(has_u)(to_above.wait_send)
    pl.when(has_d)(to_below.wait_send)
    for t in range(3):
        pl.when(has_w)(lat[t][0].wait_send)
        pl.when(has_e)(lat[t][1].wait_send)
        lat[t][2].wait_send()
        lat[t][3].wait_send()
    for t in range(2):
        for g in range(2):
            pl.when(is_end)(hop[t][g][0].wait_send)
            pl.when(is_mid)(hop[t][g][1].wait_send)
            pl.when(is_mid)(hop[t][g][2].wait_send)
    for cp in out_cp:
        cp.wait()
    co_cp.wait()


def solution(mesh):
    nz, nx, ny = mesh.shape["gz"], mesh.shape["gx"], mesh.shape["gy"]

    def body(potential, labels, conductivity, electrodes):
        coef = pltpu.VMEM((2, 8, 2, 16, 128), F32)
        field = pltpu.VMEM((4, 8, 2, 32, 128), F32)
        msg5 = pltpu.VMEM((2, 2, 5, 2, 16, 128), F32)
        msg4 = pltpu.VMEM((2, 2, 4, 2, 16, 128), F32)
        dma = pltpu.SemaphoreType.DMA
        return pl.pallas_call(
            functools.partial(kernel, nz, nx, ny),
            out_shape=(
                jax.ShapeDtypeStruct((4, 8, 32, 256), F32),
                jax.ShapeDtypeStruct((4, 8, 16, 128), F32),
            ),
            in_specs=[
                pl.BlockSpec(memory_space=pl.ANY),
                pl.BlockSpec(memory_space=pl.ANY),
                pl.BlockSpec(memory_space=pltpu.SMEM),
                pl.BlockSpec(memory_space=pltpu.SMEM),
            ],
            out_specs=(pl.BlockSpec(memory_space=pl.ANY), pl.BlockSpec(memory_space=pl.ANY)),
            scratch_shapes=[
                field,
                pltpu.VMEM((8, 2, 32, 128), jnp.int32),
                pltpu.VMEM((10, 2, 32, 128), F32),
                pltpu.VMEM((3, 2, 2, 40, 128), F32),
                pltpu.VMEM((3, 2, 2, 40, 128), F32),
                pltpu.VMEM((3, 2, 32, 128), F32),
                pltpu.VMEM((3, 2, 32, 128), F32),
                pltpu.VMEM((4, 2, 32, 128), F32),
                coef, coef, coef, coef, coef, coef, coef, coef, coef,
                pltpu.VMEM((2, 4, 2, 16, 128), F32),
                pltpu.VMEM((2, 4, 8, 2, 16, 128), F32),
                field, field, field,
                pltpu.VMEM((4, 8, 2, 16, 128), F32),
                pltpu.VMEM((4, 8, 16, 128), F32),
                pltpu.VMEM((2, 2, 4, 2, 16, 128), F32),
                pltpu.VMEM((2, 2, 4, 2, 16, 128), F32),
                pltpu.VMEM((2, 3, 2, 16, 128), F32),
                pltpu.VMEM((2, 4, 2, 16, 128), F32),
                msg5, msg5, msg5, msg5, msg4, msg4,
                dma((2, 2)), dma((2,)), dma((2,)),
                dma((3, 2)), dma((3, 2)), dma((3, 2)), dma((3, 2)),
                dma((2, 2, 3)), dma((2, 2, 3)),
            ],
            compiler_params=pltpu.CompilerParams(
                collective_id=0, has_side_effects=True, vmem_limit_bytes=60 * 1024 * 1024,
            ),
        )(potential, labels, conductivity, electrodes)

    return jax.shard_map(
        body,
        mesh=mesh,
        in_specs=(P(None, "gz", "gx", "gy"), P("gz", "gx", "gy"), P(), P()),
        out_specs=(P(None, "gz", "gx", "gy"), P(None, "gz", "gx", "gy")),
        check_vma=False,
    )
```

```python
import functools

import jax
import jax.numpy as jnp
from jax import lax
from jax.experimental import pallas as pl
from jax.experimental.pallas import tpu as pltpu
from jax.sharding import PartitionSpec as P

ASPECT = 128
MESH = pl.DeviceIdType.MESH
F32 = jnp.float32
UNROLL = True


def roll(v, shift, axis):
    return pltpu.roll(v, shift, axis)


def recip(v):
    return pltpu.reciprocal(v, approx=True)


def loop(count, body, init):
    if UNROLL:
        for i in range(count):
            init = body(i, init)
        return init
    return lax.fori_loop(0, count, body, init)


def kernel(
    nz, nx, ny,
    pot, lab, cond, elec, out, coarse,
    p_nat, l_nat, sg, xp, xh, yp, yh, src,
    lw_r, le_r, ls_r, ln_r, inv_r, e_r, rt_r, g_r, r_r, ss,
    fw, fp, ch, on, df, co, ends, wab, km, tt,
    m0s, m0r, m1s, m1r, m2s, m2r, b2s, b2r, m3s, m3r, b3s, b3r, ods, ids, xin, kx,
    loc, zs, zr, xs, xr, ys, yr, ms, mr, bs, br, qs, qr,
):
    p = lax.axis_index("gz")
    gx = lax.axis_index("gx")
    gy = lax.axis_index("gy")
    has_w, has_e = gx > 0, gx < nx - 1
    has_u, has_d = p > 0, p < nz - 1
    up = p < nz // 2
    is_end = (p == 0) | (p == nz - 1)
    is_mid = (p > 0) & (p < nz - 1)
    west, east = {"gx": gx - 1}, {"gx": gx + 1}
    south, north = {"gy": lax.rem(gy + ny - 1, ny)}, {"gy": lax.rem(gy + 1, ny)}
    above, below = {"gz": p - 1}, {"gz": p + 1}
    lane = lax.broadcasted_iota(jnp.int32, (16, 128), 1)
    lane32 = lax.broadcasted_iota(jnp.int32, (32, 128), 1)
    sub8 = lax.broadcasted_iota(jnp.int32, (8, 128), 0)
    row16 = lax.broadcasted_iota(jnp.int32, (16, 128), 0)

    lab_cp = [
        pltpu.make_async_copy(lab.at[:, :, c * 128:(c + 1) * 128], l_nat.at[:, c], loc.at[0, c])
        for c in range(2)
    ]
    pot_cp = [
        pltpu.make_async_copy(pot.at[:, :, :, c * 128:(c + 1) * 128], p_nat.at[:, :, c], loc.at[1, c])
        for c in range(2)
    ]
    for cp in lab_cp + pot_cp:
        cp.start()

    @pl.when(gx == 0)
    def _():
        xh[:, 0] = jnp.zeros((3, 2, 40, 128), F32)

    @pl.when(gx == nx - 1)
    def _():
        xh[:, 1] = jnp.zeros((3, 2, 40, 128), F32)

    barrier = pltpu.get_barrier_semaphore()

    def greet(device):
        pl.semaphore_signal(barrier, inc=1, device_id=device, device_id_type=MESH)

    greet(south)
    greet(north)
    for step in range(1, nz):
        greet({"gz": lax.rem(p + step, nz)})
    for cond_here, device in ((has_w, west), (has_e, east)):
        pl.when(cond_here)(functools.partial(greet, device))

    for cp in lab_cp:
        cp.wait()
    table = [cond[i] for i in range(16)]

    def lookup(z, carry):
        for c in range(2):
            l = jnp.concatenate([l_nat[z, c, pl.ds(j, 8, stride=4), :] for j in range(4)], 0)
            level = table
            for bit in range(4):
                on_bit = (l & (1 << bit)) != 0
                level = [
                    jnp.where(on_bit, level[2 * i + 1], level[2 * i]) for i in range(len(level) // 2)
                ]
            sg[z + 1, c] = recip(level[0])
        return carry

    loop(8, lookup, 0)

    @pl.when(p == 0)
    def _():
        sg[0] = sg[1]

    @pl.when(p == nz - 1)
    def _():
        sg[9] = sg[8]

    def remote(src_ref, dst_ref, send, recv, device):
        return pltpu.make_async_remote_copy(
            src_ref=src_ref, dst_ref=dst_ref, send_sem=send, recv_sem=recv,
            device_id=device, device_id_type=MESH,
        )

    started = []

    def start(copy, where=None):
        started.append((copy, where))
        if where is None:
            copy.start()
        else:
            pl.when(where)(copy.start)

    to_above = remote(sg.at[1], sg.at[9], zs.at[0], zr.at[1], above)
    to_below = remote(sg.at[8], sg.at[0], zs.at[1], zr.at[0], below)

    def lateral_copies(t):
        n = 40 if t == 0 else 32
        return (
            remote(xp.at[t, 0, :, 0:n], xh.at[t, 1, :, 0:n], xs.at[t, 0], xr.at[t, 1], west),
            remote(xp.at[t, 1, :, 0:n], xh.at[t, 0, :, 0:n], xs.at[t, 1], xr.at[t, 0], east),
            remote(yp.at[t, 0], yh.at[t, 1], ys.at[t, 0], yr.at[t, 1], south),
            remote(yp.at[t, 1], yh.at[t, 0], ys.at[t, 1], yr.at[t, 0], north),
        )

    lat = [lateral_copies(t) for t in range(3)]

    def send_x(t):
        start(lat[t][0], has_w)
        start(lat[t][1], has_e)

    def send_y(t):
        start(lat[t][2])
        start(lat[t][3])

    def wait_x(t):
        pl.when(has_e)(lat[t][0].wait_recv)
        pl.when(has_w)(lat[t][1].wait_recv)

    def wait_y(t):
        lat[t][2].wait_recv()
        lat[t][3].wait_recv()

    def pack_sigma(z, acc):
        acc_s, acc_n = acc
        v0, v1 = sg[z + 1, 0], sg[z + 1, 1]
        acc_s = jnp.where(lane32 == 32 + z, roll(v0, 32 + z, 1), acc_s)
        acc_n = jnp.where(lane32 == 32 + z, roll(v1, 33 + z, 1), acc_n)
        for c, v in ((0, v0), (1, v1)):
            xp[0, 0, c, pl.ds(32 + z, 1), :] = v[0:1]
            xp[0, 1, c, pl.ds(32 + z, 1), :] = v[31:32]
        return acc_s, acc_n

    zero32 = jnp.zeros((32, 128), F32)
    acc = loop(8, pack_sigma, (zero32, zero32))
    for cp in pot_cp:
        cp.wait()

    def pack_pot(z, acc):
        acc_s, acc_n = acc
        for s in range(4):
            k = s * 8 + z
            v0, v1 = (
                jnp.concatenate([p_nat[s, z, c, pl.ds(j, 8, stride=4), :] for j in range(4)], 0)
                for c in range(2)
            )
            acc_s = jnp.where(lane32 == k, roll(v0, k, 1), acc_s)
            acc_n = jnp.where(lane32 == k, roll(v1, k + 1, 1), acc_n)
            for c in range(2):
                xp[0, 0, c, pl.ds(k, 1), :] = p_nat[s, z, c, 0:1, :]
                xp[0, 1, c, pl.ds(k, 1), :] = p_nat[s, z, c, 31:32, :]
        return acc_s, acc_n

    acc = loop(8, pack_pot, acc)
    yp[0, 0], yp[0, 1] = acc
    pl.semaphore_wait(
        barrier,
        nz + 1 + has_w.astype(jnp.int32) + has_e.astype(jnp.int32),
    )

    send_x(0)
    start(to_above, has_u)
    start(to_below, has_d)
    send_y(0)

    here = jnp.where(p == 0, 4.0 * ASPECT, 0.0).astype(F32)
    row32 = lax.broadcasted_iota(jnp.int32, (32, 128), 0)
    x_cell = gx * 32 + 4 * (row32 % 8) + row32 // 8
    for c in range(2):
        y_cell = gy * 256 + c * 128 + lane32
        for s in range(4):
            first = jnp.where((x_cell == elec[s, 0]) & (y_cell == elec[s, 1]), here, 0.0)
            second = jnp.where((x_cell == elec[s, 2]) & (y_cell == elec[s, 3]), here, 0.0)
            src[s, c] = first - second

    def centre(g, v):
        return v[8:24] if g == 0 else jnp.concatenate([v[0:8], v[24:32]], 0)

    def west_east(g, v, halo_w, halo_e):
        if g == 0:
            return v[0:16], v[16:32]
        w0 = jnp.where(sub8 == 0, halo_w(), roll(v[24:32], 1, 0))
        e3 = jnp.where(sub8 == 7, halo_e(), roll(v[0:8], 7, 0))
        return jnp.concatenate([w0, v[16:24]], 0), jnp.concatenate([v[8:16], e3], 0)

    def south_north(v0, v1, halo_s, halo_n):
        r0, r1, q0, q1 = roll(v0, 1, 1), roll(v1, 1, 1), roll(v0, 127, 1), roll(v1, 127, 1)
        return (
            (jnp.where(lane == 0, halo_s, r0), jnp.where(lane == 127, q1, q0)),
            (jnp.where(lane == 0, r0, r1), jnp.where(lane == 127, halo_n, q1)),
        )

    def neighbours(g, t, k, v):
        halo_s = roll(centre(g, yh[t, 0]), lax.rem(128 - k, 128), 1)
        halo_n = roll(centre(g, yh[t, 1]), 127 - k, 1)
        ctr = [centre(g, v[c]) for c in range(2)]
        sn = south_north(ctr[0], ctr[1], halo_s, halo_n)
        res = []
        for c in range(2):
            w, e = west_east(
                g, v[c],
                lambda: xh[t, 0, c, pl.ds(k, 1), :],
                lambda: xh[t, 1, c, pl.ds(k, 1), :],
            )
            res.append((ctr[c], w, e) + sn[c])
        return res

    one = jnp.ones((16, 128), F32)
    mask_w = jnp.where(row16 == 0, jnp.where(has_w, 1.0, 0.0).astype(F32), one)
    mask_e = jnp.where(row16 == 15, jnp.where(has_e, 1.0, 0.0).astype(F32), one)
    mask_s = jnp.where(lane == 0, jnp.where(gy > 0, 1.0, 0.0).astype(F32), one)
    mask_n = jnp.where(lane == 127, jnp.where(gy < ny - 1, 1.0, 0.0).astype(F32), one)
    depth2 = 2.0 * ASPECT * ASPECT

    def setup(g):
        top = jnp.where(has_u, depth2, 0.0).astype(F32)
        zero = jnp.zeros((16, 128), F32)
        init = tuple(
            (
                top * recip(centre(g, sg[0, c]) + centre(g, sg[1, c])),
                zero, one, one, zero,
            )
            for c in range(2)
        )

        def body(z, carry):
            near = neighbours(g, 0, 32 + z, [sg[z + 1, c] for c in range(2)])
            res = []
            for c in range(2):
                sh, ratio, gg, rr, s00 = carry[c]
                here, w, e, s, n = near[c]
                lw, le = 2.0 * recip(here + w), 2.0 * recip(here + e)
                ls, ln = 2.0 * recip(here + s), 2.0 * recip(here + n)
                if g == 1:
                    lw, le = lw * mask_w, le * mask_e
                if c == 0:
                    ls = ls * mask_s
                else:
                    ln = ln * mask_n
                dp = depth2 * recip(here + centre(g, sg[z + 2, c]))
                diag = sh + dp + lw + le + ls + ln
                inv = recip(diag - sh * ratio)
                ee = sh * inv
                ratio = dp * inv
                gg = ee * gg
                s00 = s00 + rr * gg
                lw_r[g, z, c], le_r[g, z, c], ls_r[g, z, c], ln_r[g, z, c] = lw, le, ls, ln
                inv_r[g, z, c], rt_r[g, z, c], g_r[g, z, c], r_r[g, z, c] = inv, ratio, gg, rr
                e_r[g, z, c] = jnp.where(z == 0, inv, ee)
                res.append((dp, ratio, gg, rr * ratio, s00))
            return tuple(res)

        last = loop(8, body, init)
        for c in range(2):
            ss[g, 0, c], ss[g, 1, c], ss[g, 2, c], ss[g, 3, c] = (
                last[c][4], last[c][2], last[c][3], last[c][1],
            )

    def forward(g, t, half, load):
        if True:
            def body(z, carry):
                res = []
                for i in range(2):
                    s = 2 * half + i
                    near = neighbours(g, t, s * 8 + z, [load(s, z, c) for c in range(2)])
                    for c in range(2):
                        f, first = carry[2 * i + c]
                        here, w, e, so, no = near[c]
                        rhs = (lw_r[g, z, c] * w + le_r[g, z, c] * e) + (
                            ls_r[g, z, c] * so + ln_r[g, z, c] * no
                        )
                        f = rhs * inv_r[g, z, c] + e_r[g, z, c] * f
                        fw[g, s, z, c] = f
                        res.append((f, first + r_r[g, z, c] * f))
                return tuple(res)

            zero = jnp.zeros((16, 128), F32)
            init = tuple(
                (centre(g, src[2 * half + i, c]), zero) for i in range(2) for c in range(2)
            )
            last = loop(8, body, init)
            for i in range(2):
                for c in range(2):
                    ends[g, 1, 2 * half + i, c], ends[g, 0, 2 * half + i, c] = last[2 * i + c]

    i_out, i_in = jnp.where(up, 0, 1), jnp.where(up, 1, 0)
    i_oo, i_oi = jnp.where(up, 0, 3), jnp.where(up, 1, 2)
    i_io, i_ii = jnp.where(up, 2, 1), jnp.where(up, 3, 0)
    end_of = {"gz": jnp.where(up, 0, nz - 1)}
    mid_of = {"gz": jnp.where(up, 1, nz - 2)}
    twin = {"gz": nz - 1 - p}
    mate = {"gz": jnp.where(lax.rem(p, 2) == 0, p + 1, p - 1)}
    far_mid = {"gz": jnp.where(up, nz - 2, 1)}
    far_end = {"gz": jnp.where(up, nz - 1, 0)}
    i_od = jnp.where(is_end, i_in, i_out)
    slot = jnp.where(is_end, 2, 1)

    def hops(g, h):
        return (
            remote(m1s.at[g, h], m1r.at[g, h], ms.at[g, h, 0], mr.at[g, h, 0], mid_of),
            remote(m2s.at[g, h], m2r.at[g, h], ms.at[g, h, 1], mr.at[g, h, 1], twin),
            remote(m3s.at[g, h], m3r.at[g, h], ms.at[g, h, 2], mr.at[g, h, 2], end_of),
        )

    def factor_hops(g):
        return (
            remote(m0s.at[g], m0r.at[g], bs.at[g, 0], br.at[g, 0], mid_of),
            remote(b2s.at[g], b2r.at[g], bs.at[g, 1], br.at[g, 1], twin),
            remote(b3s.at[g], b3r.at[g], bs.at[g, 2], br.at[g, 2], end_of),
        )

    def cross(g, h):
        def one_of(src_ref, at, i, device):
            return remote(src_ref.at[g, h], xin.at[g, h, at], qs.at[g, h, i], qr.at[g, h, at], device)
        return (
            one_of(ids, slot, 0, far_mid), one_of(ids, slot, 1, far_end), one_of(ods, 0, 2, mate),
        )

    hop = [[hops(g, h) for h in range(2)] for g in range(2)]
    fhop = [factor_hops(g) for g in range(2)]
    pairs = [(i, c) for i in range(2) for c in range(2)]

    def end_factor(g):
        @pl.when(is_end)
        def _():
            m0s[g] = ss[g, i_ii]
        start(fhop[g][0], is_end)

    def end_send(g, h):
        @pl.when(is_end)
        def _():
            for i, c in pairs:
                m1s[g, h, i, c] = ends[g, i_in, 2 * h + i, c]
        start(hop[g][h][0], is_end)

    def mid_factor(g):
        @pl.when(is_mid)
        def _():
            fhop[g][0].wait_recv()
            for c in range(2):
                b_out = m0r[g, c]
                q = 1.0 / (1.0 - ss[g, i_oo, c] * b_out)
                km[g, 0, c] = q
                km[g, 1, c] = q * ss[g, i_io, c]
                b2s[g, 0, c] = ss[g, i_ii, c] + ss[g, i_oi, c] * b_out * q * ss[g, i_io, c]
                b2s[g, 1, c] = ss[g, i_oi, c] * q
        start(fhop[g][1], is_mid)

    def mid_forward(g, h):
        @pl.when(is_mid)
        def _():
            hop[g][h][0].wait_recv()
            for i, c in pairs:
                s = 2 * h + i
                a_out = m1r[g, h, i, c]
                first = (ends[g, i_out, s, c] + ss[g, i_oo, c] * a_out) * km[g, 0, c]
                tt[g, s, c] = first
                m2s[g, h, i, c] = ends[g, i_in, s, c] + ss[g, i_oi, c] * (a_out + m0r[g, c] * first)
        start(hop[g][h][1], is_mid)

    def mid_match(g):
        @pl.when(is_mid)
        def _():
            fhop[g][1].wait_recv()
            for c in range(2):
                km[g, 2, c] = 1.0 / (1.0 - b2r[g, 0, c] * b2s[g, 0, c])

    def mid_solve(g, h):
        @pl.when(is_mid)
        def _():
            hop[g][h][1].wait_recv()
            for i, c in pairs:
                s = 2 * h + i
                w_in = (m2r[g, h, i, c] + b2r[g, 0, c] * m2s[g, h, i, c]) * km[g, 2, c]
                first = tt[g, s, c] + km[g, 1, c] * w_in
                m3s[g, h, i, c] = first
                wab[g, i_in, s, c] = w_in
                wab[g, i_out, s, c] = m1r[g, h, i, c] + m0r[g, c] * first
        start(hop[g][h][2], is_mid)

    def end_solve(g, h):
        @pl.when(is_end)
        def _():
            hop[g][h][2].wait_recv()
            for i, c in pairs:
                wab[g, i_in, 2 * h + i, c] = m3r[g, h, i, c]
                wab[g, i_out, 2 * h + i, c] = jnp.zeros((16, 128), F32)

    def mid_extra(g):
        @pl.when(is_mid)
        def _():
            for c in range(2):
                b_out, b_in, q = m0r[g, c], b2r[g, 0, c], km[g, 0, c]
                s_oo, s_oi, s_io, s_ii = ss[g, i_oo, c], ss[g, i_oi, c], ss[g, i_io, c], ss[g, i_ii, c]
                g_mine, g_in, match = b2s[g, 1, c], b2r[g, 1, c], km[g, 2, c]
                r = 1.0 / (1.0 - s_ii * b_in)
                h = s_io * r
                b3s[g, 0, c] = s_oo + h * b_in * s_oi
                b3s[g, 1, c] = h
                b3s[g, 2, c] = h * g_in
                kx[g, 0, c] = match * b_in
                kx[g, 1, c] = match * b_in * g_mine
                kx[g, 2, c] = match
                kx[g, 3, c] = match * g_in
                kx[g, 4, c] = q
                kx[g, 5, c] = b_out * q
                kx[g, 6, c] = b_out * q * s_io
                kx[g, 7, c] = s_oi * b_out * q
                kx[g, 8, c] = h * b_in
        start(fhop[g][2], is_mid)

    def end_extra(g):
        @pl.when(is_end)
        def _():
            fhop[g][2].wait_recv()
            for c in range(2):
                c_in = b3r[g, 0, c]
                k = 1.0 / (1.0 - c_in * ss[g, i_ii, c])
                kx[g, 0, c] = k * c_in
                kx[g, 1, c] = k
                kx[g, 2, c] = k * b3r[g, 1, c]
                kx[g, 3, c] = k * b3r[g, 2, c]
                for i in range(4, 9):
                    kx[g, i, c] = jnp.zeros((16, 128), F32)

    def cross_send(g, h):
        for i, c in pairs:
            s = 2 * h + i
            ids[g, h, i, c] = ends[g, i_in, s, c] + kx[g, 7, c] * ends[g, i_out, s, c]
            ods[g, h, i, c] = ends[g, i_od, s, c] + kx[g, 8, c] * ends[g, i_in, s, c]
        for copy in cross(g, h):
            start(copy)

    def cross_solve(g, h):
        for at in range(3):
            remote(
                ids.at[g, h], xin.at[g, h, at], qs.at[g, h, 0], qr.at[g, h, at], far_mid
            ).wait_recv()
        for i, c in pairs:
            s = 2 * h + i
            near, r1, r2 = xin[g, h, 0, i, c], xin[g, h, 1, i, c], xin[g, h, 2, i, c]
            w_in = (kx[g, 0, c] * ids[g, h, i, c] + kx[g, 1, c] * near) + (
                kx[g, 2, c] * r1 + kx[g, 3, c] * r2
            )
            wab[g, i_in, s, c] = w_in
            wab[g, i_out, s, c] = (
                kx[g, 4, c] * near + kx[g, 5, c] * ends[g, i_out, s, c] + kx[g, 6, c] * w_in
            )

    def backward(t, g, h, emit, acc):
        def body(step, carry):
            z = 7 - step
            acc_s, acc_n, w_next = carry
            res = []
            for i in range(2):
                s = 2 * h + i
                k = s * 8 + z
                both = []
                for c in range(2):
                    w = fw[g, s, z, c] + g_r[g, z, c] * wab[g, 0, s, c] + (
                        rt_r[g, z, c] * w_next[2 * i + c]
                    )
                    res.append(w)
                    v = emit(s, z, c, w)
                    if g == 1:
                        xp[t + 1, 0, c, pl.ds(k, 1), :] = v[0:1]
                        xp[t + 1, 1, c, pl.ds(k, 1), :] = v[15:16]
                    both.append(v)
                acc_s = jnp.where(lane == k, roll(both[0], k, 1), acc_s)
                acc_n = jnp.where(lane == k, roll(both[1], k + 1, 1), acc_n)
            return acc_s, acc_n, tuple(res)

        first = tuple(wab[g, 1, 2 * h + i, c] for i in range(2) for c in range(2))
        return loop(8, body, acc + (first,))[:2]

    def pack_y(t, g, acc):
        for d in range(2):
            if g == 0:
                yp[t + 1, d, 8:24] = acc[d]
            else:
                yp[t + 1, d, 0:8] = acc[d][0:8]
                yp[t + 1, d, 24:32] = acc[d][8:16]

    def put(ref, g, s, z, c, v):
        if g == 0:
            ref[s, z, c, 8:24] = v
        else:
            ref[s, z, c, 0:8] = v[0:8]
            ref[s, z, c, 24:32] = v[8:16]

    def emit_first(g):
        def emit(s, z, c, w):
            put(fp, g, s, z, c, w)
            return w
        return emit

    def emit_relaxed(g):
        rows = (1, 2) if g == 0 else (0, 3)
        def emit(s, z, c, w):
            change = w - centre(g, fp[s, z, c])
            put(ch, g, s, z, c, change)
            for i in range(2):
                on[s, z, c, pl.ds(rows[i], 8, stride=4), :] = w[8 * i:8 * i + 8]
            return change
        return emit

    def load_pot(s, z, c):
        return jnp.concatenate([p_nat[s, z, c, pl.ds(j, 8, stride=4), :] for j in range(4)], 0)

    def load_first(s, z, c):
        return fp[s, z, c]

    empty = (jnp.zeros((16, 128), F32),) * 2

    wait_y(0)
    pl.when(has_d)(to_above.wait_recv)
    pl.when(has_u)(to_below.wait_recv)
    setup(0)
    end_factor(0)
    for h in range(2):
        forward(0, 0, h, load_pot)
        end_send(0, h)
    wait_x(0)
    setup(1)
    end_factor(1)
    for h in range(2):
        forward(1, 0, h, load_pot)
        end_send(1, h)
    for g in range(2):
        mid_factor(g)
        for h in range(2):
            mid_forward(g, h)
    for g in range(2):
        mid_match(g)
        acc = empty
        for h in range(2):
            mid_solve(g, h)
        for h in range(2):
            end_solve(g, h)
            acc = backward(0, g, h, emit_first(g), acc)
        pack_y(0, g, acc)
    send_x(1)
    send_y(1)
    for g in range(2):
        mid_extra(g)
    for g in range(2):
        end_extra(g)

    wait_y(1)
    for h in range(2):
        forward(0, 1, h, load_first)
        cross_send(0, h)
    wait_x(1)
    for h in range(2):
        forward(1, 1, h, load_first)
        cross_send(1, h)
    for g in range(2):
        acc = empty
        for h in range(2):
            cross_solve(g, h)
            acc = backward(1, g, h, emit_relaxed(g), acc)
        pack_y(1, g, acc)
    send_x(2)
    send_y(2)
    out_cp = [
        pltpu.make_async_copy(on.at[:, :, c], out.at[:, :, :, c * 128:(c + 1) * 128], loc.at[0, c])
        for c in range(2)
    ]
    for cp in out_cp:
        cp.start()

    lane8 = lax.broadcasted_iota(jnp.int32, (8, 128), 1)
    even = (2 * lane8) % 128

    def squeeze(v):
        return jnp.take_along_axis(v + roll(v, 127, 1), even, axis=1)

    def defect(g):
        def body(z, carry):
            for s in range(4):
                near = neighbours(g, 2, s * 8 + z, [ch[s, z, c] for c in range(2)])
                low, high = [], []
                for c in range(2):
                    here, w, e, so, no = near[c]
                    d = (lw_r[g, z, c] * w + le_r[g, z, c] * e) + (
                        ls_r[g, z, c] * so + ln_r[g, z, c] * no
                    )
                    if g == 0:
                        df[s, z, c] = d
                    else:
                        d = d + df[s, z, c]
                        low.append(squeeze(d[0:8]))
                        high.append(squeeze(d[8:16]))
                if g == 1:
                    co[s, z, pl.ds(0, 8, stride=2), :] = jnp.where(lane8 < 64, low[0], low[1])
                    co[s, z, pl.ds(1, 8, stride=2), :] = jnp.where(lane8 < 64, high[0], high[1])
            return carry

        loop(8, body, 0)

    wait_y(2)
    defect(0)
    wait_x(2)
    defect(1)
    co_cp = pltpu.make_async_copy(co, coarse, loc.at[1, 0])
    co_cp.start()

    for copy, where in started:
        if where is None:
            copy.wait_send()
        else:
            pl.when(where)(copy.wait_send)
    for cp in out_cp:
        cp.wait()
    co_cp.wait()


def solution(mesh):
    nz, nx, ny = mesh.shape["gz"], mesh.shape["gx"], mesh.shape["gy"]

    def body(potential, labels, conductivity, electrodes):
        coef = pltpu.VMEM((2, 8, 2, 16, 128), F32)
        field = pltpu.VMEM((4, 8, 2, 32, 128), F32)
        msg = pltpu.VMEM((2, 2, 2, 2, 16, 128), F32)
        part1 = pltpu.VMEM((2, 2, 16, 128), F32)
        part2 = pltpu.VMEM((2, 2, 2, 16, 128), F32)
        part3 = pltpu.VMEM((2, 3, 2, 16, 128), F32)
        dma = pltpu.SemaphoreType.DMA
        return pl.pallas_call(
            functools.partial(kernel, nz, nx, ny),
            out_shape=(
                jax.ShapeDtypeStruct((4, 8, 32, 256), F32),
                jax.ShapeDtypeStruct((4, 8, 16, 128), F32),
            ),
            in_specs=[
                pl.BlockSpec(memory_space=pl.ANY),
                pl.BlockSpec(memory_space=pl.ANY),
                pl.BlockSpec(memory_space=pltpu.SMEM),
                pl.BlockSpec(memory_space=pltpu.SMEM),
            ],
            out_specs=(pl.BlockSpec(memory_space=pl.ANY), pl.BlockSpec(memory_space=pl.ANY)),
            scratch_shapes=[
                field,
                pltpu.VMEM((8, 2, 32, 128), jnp.int32),
                pltpu.VMEM((10, 2, 32, 128), F32),
                pltpu.VMEM((3, 2, 2, 40, 128), F32),
                pltpu.VMEM((3, 2, 2, 40, 128), F32),
                pltpu.VMEM((3, 2, 32, 128), F32),
                pltpu.VMEM((3, 2, 32, 128), F32),
                pltpu.VMEM((4, 2, 32, 128), F32),
                coef, coef, coef, coef, coef, coef, coef, coef, coef,
                pltpu.VMEM((2, 4, 2, 16, 128), F32),
                pltpu.VMEM((2, 4, 8, 2, 16, 128), F32),
                field, field, field,
                pltpu.VMEM((4, 8, 2, 16, 128), F32),
                pltpu.VMEM((4, 8, 16, 128), F32),
                pltpu.VMEM((2, 2, 4, 2, 16, 128), F32),
                pltpu.VMEM((2, 2, 4, 2, 16, 128), F32),
                pltpu.VMEM((2, 3, 2, 16, 128), F32),
                pltpu.VMEM((2, 4, 2, 16, 128), F32),
                part1, part1, msg, msg, msg, msg, part2, part2, msg, msg, part3, part3, msg, msg,
                pltpu.VMEM((2, 2, 3, 2, 2, 16, 128), F32),
                pltpu.VMEM((2, 9, 2, 16, 128), F32),
                dma((2, 2)), dma((2,)), dma((2,)),
                dma((3, 2)), dma((3, 2)), dma((3, 2)), dma((3, 2)),
                dma((2, 2, 3)), dma((2, 2, 3)), dma((2, 3)), dma((2, 3)),
                dma((2, 2, 3)), dma((2, 2, 3)),
            ],
            compiler_params=pltpu.CompilerParams(
                collective_id=0, has_side_effects=True, vmem_limit_bytes=60 * 1024 * 1024,
            ),
        )(potential, labels, conductivity, electrodes)

    return jax.shard_map(
        body,
        mesh=mesh,
        in_specs=(P(None, "gz", "gx", "gy"), P("gz", "gx", "gy"), P(), P()),
        out_specs=(P(None, "gz", "gx", "gy"), P(None, "gz", "gx", "gy")),
        check_vma=False,
    )
```

```python
import functools

import jax
import jax.numpy as jnp
from jax import lax
from jax.experimental import pallas as pl
from jax.experimental.pallas import tpu as pltpu
from jax.sharding import PartitionSpec as P

ASPECT = 128
MESH = pl.DeviceIdType.MESH
F32 = jnp.float32
UNROLL = True


def roll(v, shift, axis):
    return pltpu.roll(v, shift, axis)


def recip(v):
    return pltpu.reciprocal(v, approx=True)


def loop(count, body, init):
    if UNROLL:
        for i in range(count):
            init = body(i, init)
        return init
    return lax.fori_loop(0, count, body, init)


def kernel(
    nz, nx, ny,
    pot, lab, cond, elec, out, coarse,
    p_nat, l_nat, sg, xp, xh, yp, yh, src,
    lw_r, le_r, ls_r, ln_r, inv_r, e_r, rt_r, g_r, r_r, ss,
    fw, fp, ch, on, df, co, ends, wab, km, tt,
    m0s, m0r, m1s, m1r, m2s, m2r, b2s, b2r, m3s, m3r, b3s, b3r, ods, ids, xin, kx,
    loc, zs, zr, xs, xr, ys, yr, ms, mr, bs, br, qs, qr,
):
    p = lax.axis_index("gz")
    gx = lax.axis_index("gx")
    gy = lax.axis_index("gy")
    has_w, has_e = gx > 0, gx < nx - 1
    has_u, has_d = p > 0, p < nz - 1
    up = p < nz // 2
    is_end = (p == 0) | (p == nz - 1)
    is_mid = (p > 0) & (p < nz - 1)
    west, east = {"gx": gx - 1}, {"gx": gx + 1}
    south, north = {"gy": lax.rem(gy + ny - 1, ny)}, {"gy": lax.rem(gy + 1, ny)}
    above, below = {"gz": p - 1}, {"gz": p + 1}
    lane = lax.broadcasted_iota(jnp.int32, (16, 128), 1)
    lane32 = lax.broadcasted_iota(jnp.int32, (32, 128), 1)
    sub8 = lax.broadcasted_iota(jnp.int32, (8, 128), 0)
    row16 = lax.broadcasted_iota(jnp.int32, (16, 128), 0)

    lab_cp = [
        pltpu.make_async_copy(lab.at[:, :, c * 128:(c + 1) * 128], l_nat.at[:, c], loc.at[0, c])
        for c in range(2)
    ]
    pot_cp = [
        pltpu.make_async_copy(pot.at[:, :, :, c * 128:(c + 1) * 128], p_nat.at[:, :, c], loc.at[1, c])
        for c in range(2)
    ]
    for cp in lab_cp + pot_cp:
        cp.start()

    @pl.when(gx == 0)
    def _():
        xh[:, 0] = jnp.zeros((3, 2, 40, 128), F32)

    @pl.when(gx == nx - 1)
    def _():
        xh[:, 1] = jnp.zeros((3, 2, 40, 128), F32)

    barrier = pltpu.get_barrier_semaphore()

    def greet(device):
        pl.semaphore_signal(barrier, inc=1, device_id=device, device_id_type=MESH)

    greet(south)
    greet(north)
    for step in range(1, nz):
        greet({"gz": lax.rem(p + step, nz)})
    for cond_here, device in ((has_w, west), (has_e, east)):
        pl.when(cond_here)(functools.partial(greet, device))

    for cp in lab_cp:
        cp.wait()
    table = [cond[i] for i in range(16)]

    def lookup(z, carry):
        for c in range(2):
            l = jnp.concatenate([l_nat[z, c, pl.ds(j, 8, stride=4), :] for j in range(4)], 0)
            level = table
            for bit in range(4):
                on_bit = (l & (1 << bit)) != 0
                level = [
                    jnp.where(on_bit, level[2 * i + 1], level[2 * i]) for i in range(len(level) // 2)
                ]
            sg[z + 1, c] = recip(level[0])
        return carry

    loop(8, lookup, 0)

    @pl.when(p == 0)
    def _():
        sg[0] = sg[1]

    @pl.when(p == nz - 1)
    def _():
        sg[9] = sg[8]

    def remote(src_ref, dst_ref, send, recv, device):
        return pltpu.make_async_remote_copy(
            src_ref=src_ref, dst_ref=dst_ref, send_sem=send, recv_sem=recv,
            device_id=device, device_id_type=MESH,
        )

    started = []

    def start(copy, where=None):
        started.append((copy, where))
        if where is None:
            copy.start()
        else:
            pl.when(where)(copy.start)

    to_above = remote(sg.at[1], sg.at[9], zs.at[0], zr.at[1], above)
    to_below = remote(sg.at[8], sg.at[0], zs.at[1], zr.at[0], below)

    def lateral_copies(t):
        n = 40 if t == 0 else 32
        return (
            remote(xp.at[t, 0, :, 0:n], xh.at[t, 1, :, 0:n], xs.at[t, 0], xr.at[t, 1], west),
            remote(xp.at[t, 1, :, 0:n], xh.at[t, 0, :, 0:n], xs.at[t, 1], xr.at[t, 0], east),
            remote(yp.at[t, 0], yh.at[t, 1], ys.at[t, 0], yr.at[t, 1], south),
            remote(yp.at[t, 1], yh.at[t, 0], ys.at[t, 1], yr.at[t, 0], north),
        )

    lat = [lateral_copies(t) for t in range(3)]

    def send_x(t):
        start(lat[t][0], has_w)
        start(lat[t][1], has_e)

    def send_y(t):
        start(lat[t][2])
        start(lat[t][3])

    def wait_x(t):
        pl.when(has_e)(lat[t][0].wait_recv)
        pl.when(has_w)(lat[t][1].wait_recv)

    def wait_y(t):
        lat[t][2].wait_recv()
        lat[t][3].wait_recv()

    def pack_sigma(z, acc):
        acc_s, acc_n = acc
        v0, v1 = sg[z + 1, 0], sg[z + 1, 1]
        acc_s = jnp.where(lane32 == 32 + z, roll(v0, 32 + z, 1), acc_s)
        acc_n = jnp.where(lane32 == 32 + z, roll(v1, 33 + z, 1), acc_n)
        for c, v in ((0, v0), (1, v1)):
            xp[0, 0, c, pl.ds(32 + z, 1), :] = v[0:1]
            xp[0, 1, c, pl.ds(32 + z, 1), :] = v[31:32]
        return acc_s, acc_n

    zero32 = jnp.zeros((32, 128), F32)
    acc = loop(8, pack_sigma, (zero32, zero32))
    for cp in pot_cp:
        cp.wait()

    def pack_pot(z, acc):
        acc_s, acc_n = acc
        for s in range(4):
            k = s * 8 + z
            v0, v1 = (
                jnp.concatenate([p_nat[s, z, c, pl.ds(j, 8, stride=4), :] for j in range(4)], 0)
                for c in range(2)
            )
            acc_s = jnp.where(lane32 == k, roll(v0, k, 1), acc_s)
            acc_n = jnp.where(lane32 == k, roll(v1, k + 1, 1), acc_n)
            for c in range(2):
                xp[0, 0, c, pl.ds(k, 1), :] = p_nat[s, z, c, 0:1, :]
                xp[0, 1, c, pl.ds(k, 1), :] = p_nat[s, z, c, 31:32, :]
        return acc_s, acc_n

    acc = loop(8, pack_pot, acc)
    yp[0, 0], yp[0, 1] = acc
    pl.semaphore_wait(
        barrier,
        nz + 1 + has_w.astype(jnp.int32) + has_e.astype(jnp.int32),
    )

    send_x(0)
    start(to_above, has_u)
    start(to_below, has_d)
    send_y(0)

    here = jnp.where(p == 0, 4.0 * ASPECT, 0.0).astype(F32)
    row32 = lax.broadcasted_iota(jnp.int32, (32, 128), 0)
    x_cell = gx * 32 + 4 * (row32 % 8) + row32 // 8
    for c in range(2):
        y_cell = gy * 256 + c * 128 + lane32
        for s in range(4):
            first = jnp.where((x_cell == elec[s, 0]) & (y_cell == elec[s, 1]), here, 0.0)
            second = jnp.where((x_cell == elec[s, 2]) & (y_cell == elec[s, 3]), here, 0.0)
            src[s, c] = first - second

    def centre(g, v):
        return v[8:24] if g == 0 else jnp.concatenate([v[0:8], v[24:32]], 0)

    def west_east(g, v, halo_w, halo_e):
        if g == 0:
            return v[0:16], v[16:32]
        w0 = jnp.where(sub8 == 0, halo_w(), roll(v[24:32], 1, 0))
        e3 = jnp.where(sub8 == 7, halo_e(), roll(v[0:8], 7, 0))
        return jnp.concatenate([w0, v[16:24]], 0), jnp.concatenate([v[8:16], e3], 0)

    def south_north(v0, v1, halo_s, halo_n):
        r0, r1, q0, q1 = roll(v0, 1, 1), roll(v1, 1, 1), roll(v0, 127, 1), roll(v1, 127, 1)
        return (
            (jnp.where(lane == 0, halo_s, r0), jnp.where(lane == 127, q1, q0)),
            (jnp.where(lane == 0, r0, r1), jnp.where(lane == 127, halo_n, q1)),
        )

    def neighbours(g, t, k, v):
        halo_s = roll(centre(g, yh[t, 0]), lax.rem(128 - k, 128), 1)
        halo_n = roll(centre(g, yh[t, 1]), 127 - k, 1)
        ctr = [centre(g, v[c]) for c in range(2)]
        sn = south_north(ctr[0], ctr[1], halo_s, halo_n)
        res = []
        for c in range(2):
            w, e = west_east(
                g, v[c],
                lambda: xh[t, 0, c, pl.ds(k, 1), :],
                lambda: xh[t, 1, c, pl.ds(k, 1), :],
            )
            res.append((ctr[c], w, e) + sn[c])
        return res

    one = jnp.ones((16, 128), F32)
    mask_w = jnp.where(row16 == 0, jnp.where(has_w, 1.0, 0.0).astype(F32), one)
    mask_e = jnp.where(row16 == 15, jnp.where(has_e, 1.0, 0.0).astype(F32), one)
    mask_s = jnp.where(lane == 0, jnp.where(gy > 0, 1.0, 0.0).astype(F32), one)
    mask_n = jnp.where(lane == 127, jnp.where(gy < ny - 1, 1.0, 0.0).astype(F32), one)
    depth2 = 2.0 * ASPECT * ASPECT

    def setup(g):
        top = jnp.where(has_u, depth2, 0.0).astype(F32)
        zero = jnp.zeros((16, 128), F32)
        init = tuple(
            (
                top * recip(centre(g, sg[0, c]) + centre(g, sg[1, c])),
                zero, one, one, zero,
            )
            for c in range(2)
        )

        def body(z, carry):
            near = neighbours(g, 0, 32 + z, [sg[z + 1, c] for c in range(2)])
            res = []
            for c in range(2):
                sh, ratio, gg, rr, s00 = carry[c]
                here, w, e, s, n = near[c]
                lw, le = 2.0 * recip(here + w), 2.0 * recip(here + e)
                ls, ln = 2.0 * recip(here + s), 2.0 * recip(here + n)
                if g == 1:
                    lw, le = lw * mask_w, le * mask_e
                if c == 0:
                    ls = ls * mask_s
                else:
                    ln = ln * mask_n
                dp = depth2 * recip(here + centre(g, sg[z + 2, c]))
                diag = sh + dp + lw + le + ls + ln
                inv = recip(diag - sh * ratio)
                ee = sh * inv
                ratio = dp * inv
                gg = ee * gg
                s00 = s00 + rr * gg
                lw_r[g, z, c], le_r[g, z, c], ls_r[g, z, c], ln_r[g, z, c] = lw, le, ls, ln
                inv_r[g, z, c], rt_r[g, z, c], g_r[g, z, c], r_r[g, z, c] = inv, ratio, gg, rr
                e_r[g, z, c] = jnp.where(z == 0, inv, ee)
                res.append((dp, ratio, gg, rr * ratio, s00))
            return tuple(res)

        last = loop(8, body, init)
        for c in range(2):
            ss[g, 0, c], ss[g, 1, c], ss[g, 2, c], ss[g, 3, c] = (
                last[c][4], last[c][2], last[c][3], last[c][1],
            )

    def forward(g, t, half, load):
        if True:
            def body(z, carry):
                res = []
                for i in range(2):
                    s = 2 * half + i
                    near = neighbours(g, t, s * 8 + z, [load(s, z, c) for c in range(2)])
                    for c in range(2):
                        f, first = carry[2 * i + c]
                        here, w, e, so, no = near[c]
                        rhs = (lw_r[g, z, c] * w + le_r[g, z, c] * e) + (
                            ls_r[g, z, c] * so + ln_r[g, z, c] * no
                        )
                        f = rhs * inv_r[g, z, c] + e_r[g, z, c] * f
                        fw[g, s, z, c] = f
                        res.append((f, first + r_r[g, z, c] * f))
                return tuple(res)

            zero = jnp.zeros((16, 128), F32)
            init = tuple(
                (centre(g, src[2 * half + i, c]), zero) for i in range(2) for c in range(2)
            )
            last = loop(8, body, init)
            for i in range(2):
                for c in range(2):
                    ends[g, 1, 2 * half + i, c], ends[g, 0, 2 * half + i, c] = last[2 * i + c]

    i_out, i_in = jnp.where(up, 0, 1), jnp.where(up, 1, 0)
    i_oo, i_oi = jnp.where(up, 0, 3), jnp.where(up, 1, 2)
    i_io, i_ii = jnp.where(up, 2, 1), jnp.where(up, 3, 0)
    end_of = {"gz": jnp.where(up, 0, nz - 1)}
    mid_of = {"gz": jnp.where(up, 1, nz - 2)}
    twin = {"gz": nz - 1 - p}
    mate = {"gz": jnp.where(lax.rem(p, 2) == 0, p + 1, p - 1)}
    far_mid = {"gz": jnp.where(up, nz - 2, 1)}
    far_end = {"gz": jnp.where(up, nz - 1, 0)}
    i_od = jnp.where(is_end, i_in, i_out)
    slot = jnp.where(is_end, 2, 1)

    def hops(g, h):
        return (
            remote(m1s.at[g, h], m1r.at[g, h], ms.at[g, h, 0], mr.at[g, h, 0], mid_of),
            remote(m2s.at[g, h], m2r.at[g, h], ms.at[g, h, 1], mr.at[g, h, 1], twin),
            remote(m3s.at[g, h], m3r.at[g, h], ms.at[g, h, 2], mr.at[g, h, 2], end_of),
        )

    def factor_hops(g):
        return (
            remote(m0s.at[g], m0r.at[g], bs.at[g, 0], br.at[g, 0], mid_of),
            remote(b2s.at[g], b2r.at[g], bs.at[g, 1], br.at[g, 1], twin),
            remote(b3s.at[g], b3r.at[g], bs.at[g, 2], br.at[g, 2], end_of),
        )

    def cross(g, h):
        def one_of(src_ref, at, i, device):
            return remote(src_ref.at[g, h], xin.at[g, h, at], qs.at[g, h, i], qr.at[g, h, at], device)
        return (
            one_of(ids, slot, 0, far_mid), one_of(ids, slot, 1, far_end), one_of(ods, 0, 2, mate),
        )

    hop = [[hops(g, h) for h in range(2)] for g in range(2)]
    fhop = [factor_hops(g) for g in range(2)]
    pairs = [(i, c) for i in range(2) for c in range(2)]

    def end_factor(g):
        @pl.when(is_end)
        def _():
            m0s[g] = ss[g, i_ii]
        start(fhop[g][0], is_end)

    def end_send(g, h):
        @pl.when(is_end)
        def _():
            for i, c in pairs:
                m1s[g, h, i, c] = ends[g, i_in, 2 * h + i, c]
        start(hop[g][h][0], is_end)

    def mid_factor(g):
        @pl.when(is_mid)
        def _():
            fhop[g][0].wait_recv()
            for c in range(2):
                b_out = m0r[g, c]
                q = 1.0 / (1.0 - ss[g, i_oo, c] * b_out)
                km[g, 0, c] = q
                km[g, 1, c] = q * ss[g, i_io, c]
                b2s[g, 0, c] = ss[g, i_ii, c] + ss[g, i_oi, c] * b_out * q * ss[g, i_io, c]
                b2s[g, 1, c] = ss[g, i_oi, c] * q
        start(fhop[g][1], is_mid)

    def mid_forward(g, h):
        @pl.when(is_mid)
        def _():
            hop[g][h][0].wait_recv()
            for i, c in pairs:
                s = 2 * h + i
                a_out = m1r[g, h, i, c]
                first = (ends[g, i_out, s, c] + ss[g, i_oo, c] * a_out) * km[g, 0, c]
                tt[g, s, c] = first
                m2s[g, h, i, c] = ends[g, i_in, s, c] + ss[g, i_oi, c] * (a_out + m0r[g, c] * first)
        start(hop[g][h][1], is_mid)

    def mid_match(g):
        @pl.when(is_mid)
        def _():
            fhop[g][1].wait_recv()
            for c in range(2):
                km[g, 2, c] = 1.0 / (1.0 - b2r[g, 0, c] * b2s[g, 0, c])

    def mid_solve(g, h):
        @pl.when(is_mid)
        def _():
            hop[g][h][1].wait_recv()
            for i, c in pairs:
                s = 2 * h + i
                w_in = (m2r[g, h, i, c] + b2r[g, 0, c] * m2s[g, h, i, c]) * km[g, 2, c]
                first = tt[g, s, c] + km[g, 1, c] * w_in
                m3s[g, h, i, c] = first
                wab[g, i_in, s, c] = w_in
                wab[g, i_out, s, c] = m1r[g, h, i, c] + m0r[g, c] * first
        start(hop[g][h][2], is_mid)

    def end_solve(g, h):
        @pl.when(is_end)
        def _():
            hop[g][h][2].wait_recv()
            for i, c in pairs:
                wab[g, i_in, 2 * h + i, c] = m3r[g, h, i, c]
                wab[g, i_out, 2 * h + i, c] = jnp.zeros((16, 128), F32)

    def mid_extra(g):
        @pl.when(is_mid)
        def _():
            for c in range(2):
                b_out, b_in, q = m0r[g, c], b2r[g, 0, c], km[g, 0, c]
                s_oo, s_oi, s_io, s_ii = ss[g, i_oo, c], ss[g, i_oi, c], ss[g, i_io, c], ss[g, i_ii, c]
                g_mine, g_in, match = b2s[g, 1, c], b2r[g, 1, c], km[g, 2, c]
                r = 1.0 / (1.0 - s_ii * b_in)
                h = s_io * r
                b3s[g, 0, c] = s_oo + h * b_in * s_oi
                b3s[g, 1, c] = h
                b3s[g, 2, c] = h * g_in
                kx[g, 0, c] = match * b_in
                kx[g, 1, c] = match * b_in * g_mine
                kx[g, 2, c] = match
                kx[g, 3, c] = match * g_in
                kx[g, 4, c] = q
                kx[g, 5, c] = b_out * q
                kx[g, 6, c] = b_out * q * s_io
                kx[g, 7, c] = s_oi * b_out * q
                kx[g, 8, c] = h * b_in
        start(fhop[g][2], is_mid)

    def end_extra(g):
        @pl.when(is_end)
        def _():
            fhop[g][2].wait_recv()
            for c in range(2):
                c_in = b3r[g, 0, c]
                k = 1.0 / (1.0 - c_in * ss[g, i_ii, c])
                kx[g, 0, c] = k * c_in
                kx[g, 1, c] = k
                kx[g, 2, c] = k * b3r[g, 1, c]
                kx[g, 3, c] = k * b3r[g, 2, c]
                for i in range(4, 9):
                    kx[g, i, c] = jnp.zeros((16, 128), F32)

    def cross_send(g, h):
        for i, c in pairs:
            s = 2 * h + i
            ids[g, h, i, c] = ends[g, i_in, s, c] + kx[g, 7, c] * ends[g, i_out, s, c]
            ods[g, h, i, c] = ends[g, i_od, s, c] + kx[g, 8, c] * ends[g, i_in, s, c]
        for copy in cross(g, h):
            start(copy)

    def cross_solve(g, h):
        for at in range(3):
            remote(
                ids.at[g, h], xin.at[g, h, at], qs.at[g, h, 0], qr.at[g, h, at], far_mid
            ).wait_recv()
        for i, c in pairs:
            s = 2 * h + i
            near, r1, r2 = xin[g, h, 0, i, c], xin[g, h, 1, i, c], xin[g, h, 2, i, c]
            w_in = (kx[g, 0, c] * ids[g, h, i, c] + kx[g, 1, c] * near) + (
                kx[g, 2, c] * r1 + kx[g, 3, c] * r2
            )
            wab[g, i_in, s, c] = w_in
            wab[g, i_out, s, c] = (
                kx[g, 4, c] * near + kx[g, 5, c] * ends[g, i_out, s, c] + kx[g, 6, c] * w_in
            )

    def backward(t, g, h, emit, acc):
        def body(step, carry):
            z = 7 - step
            acc_s, acc_n, w_next = carry
            res = []
            for i in range(2):
                s = 2 * h + i
                k = s * 8 + z
                both = []
                for c in range(2):
                    w = fw[g, s, z, c] + g_r[g, z, c] * wab[g, 0, s, c] + (
                        rt_r[g, z, c] * w_next[2 * i + c]
                    )
                    res.append(w)
                    v = emit(s, z, c, w)
                    if g == 1:
                        xp[t + 1, 0, c, pl.ds(k, 1), :] = v[0:1]
                        xp[t + 1, 1, c, pl.ds(k, 1), :] = v[15:16]
                    both.append(v)
                acc_s = jnp.where(lane == k, roll(both[0], k, 1), acc_s)
                acc_n = jnp.where(lane == k, roll(both[1], k + 1, 1), acc_n)
            return acc_s, acc_n, tuple(res)

        first = tuple(wab[g, 1, 2 * h + i, c] for i in range(2) for c in range(2))
        return loop(8, body, acc + (first,))[:2]

    def pack_y(t, g, acc):
        for d in range(2):
            if g == 0:
                yp[t + 1, d, 8:24] = acc[d]
            else:
                yp[t + 1, d, 0:8] = acc[d][0:8]
                yp[t + 1, d, 24:32] = acc[d][8:16]

    def put(ref, g, s, z, c, v):
        if g == 0:
            ref[s, z, c, 8:24] = v
        else:
            ref[s, z, c, 0:8] = v[0:8]
            ref[s, z, c, 24:32] = v[8:16]

    def emit_first(g):
        def emit(s, z, c, w):
            put(fp, g, s, z, c, w)
            return w
        return emit

    def emit_relaxed(g):
        rows = (1, 2) if g == 0 else (0, 3)
        def emit(s, z, c, w):
            change = w - centre(g, fp[s, z, c])
            put(ch, g, s, z, c, change)
            for i in range(2):
                on[s, z, c, pl.ds(rows[i], 8, stride=4), :] = w[8 * i:8 * i + 8]
            return change
        return emit

    def load_pot(s, z, c):
        return jnp.concatenate([p_nat[s, z, c, pl.ds(j, 8, stride=4), :] for j in range(4)], 0)

    def load_first(s, z, c):
        return fp[s, z, c]

    empty = (jnp.zeros((16, 128), F32),) * 2

    wait_y(0)
    pl.when(has_d)(to_above.wait_recv)
    pl.when(has_u)(to_below.wait_recv)
    setup(0)
    end_factor(0)
    for h in range(2):
        forward(0, 0, h, load_pot)
        end_send(0, h)
    wait_x(0)
    setup(1)
    end_factor(1)
    for h in range(2):
        forward(1, 0, h, load_pot)
        end_send(1, h)
    for g in range(2):
        mid_factor(g)
        for h in range(2):
            mid_forward(g, h)
    for g in range(2):
        mid_match(g)
        acc = empty
        for h in range(2):
            mid_solve(g, h)
        for h in range(2):
            end_solve(g, h)
            acc = backward(0, g, h, emit_first(g), acc)
        pack_y(0, g, acc)
    send_x(1)
    send_y(1)
    for g in range(2):
        mid_extra(g)
    for g in range(2):
        end_extra(g)

    wait_y(1)
    for h in range(2):
        forward(0, 1, h, load_first)
        cross_send(0, h)
    wait_x(1)
    for h in range(2):
        forward(1, 1, h, load_first)
        cross_send(1, h)
    for g in range(2):
        acc = empty
        for h in range(2):
            cross_solve(g, h)
            acc = backward(1, g, h, emit_relaxed(g), acc)
        pack_y(1, g, acc)
    send_x(2)
    send_y(2)
    out_cp = [
        pltpu.make_async_copy(on.at[:, :, c], out.at[:, :, :, c * 128:(c + 1) * 128], loc.at[0, c])
        for c in range(2)
    ]
    for cp in out_cp:
        cp.start()

    pick = (
        lax.broadcasted_iota(jnp.int32, (256, 128), 0) // 2
        == lax.broadcasted_iota(jnp.int32, (256, 128), 1)
    ).astype(F32)

    def defect(g):
        def body(z, carry):
            rows = []
            for s in range(4):
                near = neighbours(g, 2, s * 8 + z, [ch[s, z, c] for c in range(2)])
                both = []
                for c in range(2):
                    here, w, e, so, no = near[c]
                    d = (lw_r[g, z, c] * w + le_r[g, z, c] * e) + (
                        ls_r[g, z, c] * so + ln_r[g, z, c] * no
                    )
                    if g == 0:
                        df[s, z, c] = d
                    else:
                        both.append(d + df[s, z, c])
                if g == 1:
                    rows.append(jnp.concatenate(both, 1))
            if g == 1:
                d = jnp.dot(
                    jnp.concatenate(rows, 0), pick,
                    precision=lax.Precision.HIGHEST, preferred_element_type=F32,
                )
                for s in range(4):
                    co[s, z, pl.ds(0, 8, stride=2), :] = d[16 * s:16 * s + 8]
                    co[s, z, pl.ds(1, 8, stride=2), :] = d[16 * s + 8:16 * s + 16]
            return carry

        loop(8, body, 0)

    wait_y(2)
    defect(0)
    wait_x(2)
    defect(1)
    co_cp = pltpu.make_async_copy(co, coarse, loc.at[1, 0])
    co_cp.start()

    for copy, where in started:
        if where is None:
            copy.wait_send()
        else:
            pl.when(where)(copy.wait_send)
    for cp in out_cp:
        cp.wait()
    co_cp.wait()


def solution(mesh):
    nz, nx, ny = mesh.shape["gz"], mesh.shape["gx"], mesh.shape["gy"]

    def body(potential, labels, conductivity, electrodes):
        coef = pltpu.VMEM((2, 8, 2, 16, 128), F32)
        field = pltpu.VMEM((4, 8, 2, 32, 128), F32)
        msg = pltpu.VMEM((2, 2, 2, 2, 16, 128), F32)
        part1 = pltpu.VMEM((2, 2, 16, 128), F32)
        part2 = pltpu.VMEM((2, 2, 2, 16, 128), F32)
        part3 = pltpu.VMEM((2, 3, 2, 16, 128), F32)
        dma = pltpu.SemaphoreType.DMA
        return pl.pallas_call(
            functools.partial(kernel, nz, nx, ny),
            out_shape=(
                jax.ShapeDtypeStruct((4, 8, 32, 256), F32),
                jax.ShapeDtypeStruct((4, 8, 16, 128), F32),
            ),
            in_specs=[
                pl.BlockSpec(memory_space=pl.ANY),
                pl.BlockSpec(memory_space=pl.ANY),
                pl.BlockSpec(memory_space=pltpu.SMEM),
                pl.BlockSpec(memory_space=pltpu.SMEM),
            ],
            out_specs=(pl.BlockSpec(memory_space=pl.ANY), pl.BlockSpec(memory_space=pl.ANY)),
            scratch_shapes=[
                field,
                pltpu.VMEM((8, 2, 32, 128), jnp.int32),
                pltpu.VMEM((10, 2, 32, 128), F32),
                pltpu.VMEM((3, 2, 2, 40, 128), F32),
                pltpu.VMEM((3, 2, 2, 40, 128), F32),
                pltpu.VMEM((3, 2, 32, 128), F32),
                pltpu.VMEM((3, 2, 32, 128), F32),
                pltpu.VMEM((4, 2, 32, 128), F32),
                coef, coef, coef, coef, coef, coef, coef, coef, coef,
                pltpu.VMEM((2, 4, 2, 16, 128), F32),
                pltpu.VMEM((2, 4, 8, 2, 16, 128), F32),
                field, field, field,
                pltpu.VMEM((4, 8, 2, 16, 128), F32),
                pltpu.VMEM((4, 8, 16, 128), F32),
                pltpu.VMEM((2, 2, 4, 2, 16, 128), F32),
                pltpu.VMEM((2, 2, 4, 2, 16, 128), F32),
                pltpu.VMEM((2, 3, 2, 16, 128), F32),
                pltpu.VMEM((2, 4, 2, 16, 128), F32),
                part1, part1, msg, msg, msg, msg, part2, part2, msg, msg, part3, part3, msg, msg,
                pltpu.VMEM((2, 2, 3, 2, 2, 16, 128), F32),
                pltpu.VMEM((2, 9, 2, 16, 128), F32),
                dma((2, 2)), dma((2,)), dma((2,)),
                dma((3, 2)), dma((3, 2)), dma((3, 2)), dma((3, 2)),
                dma((2, 2, 3)), dma((2, 2, 3)), dma((2, 3)), dma((2, 3)),
                dma((2, 2, 3)), dma((2, 2, 3)),
            ],
            compiler_params=pltpu.CompilerParams(
                collective_id=0, has_side_effects=True, vmem_limit_bytes=60 * 1024 * 1024,
            ),
        )(potential, labels, conductivity, electrodes)

    return jax.shard_map(
        body,
        mesh=mesh,
        in_specs=(P(None, "gz", "gx", "gy"), P("gz", "gx", "gy"), P(), P()),
        out_specs=(P(None, "gz", "gx", "gy"), P(None, "gz", "gx", "gy")),
        check_vma=False,
    )
```

```python
import functools

import jax
import jax.numpy as jnp
from jax import lax
from jax.experimental import pallas as pl
from jax.experimental.pallas import tpu as pltpu
from jax.sharding import PartitionSpec as P

ASPECT = 128
MESH = pl.DeviceIdType.MESH
F32 = jnp.float32
UNROLL = True


def roll(v, shift, axis):
    return pltpu.roll(v, shift, axis)


def recip(v):
    return pltpu.reciprocal(v, approx=True)


def loop(count, body, init):
    if UNROLL:
        for i in range(count):
            init = body(i, init)
        return init
    return lax.fori_loop(0, count, body, init)


def kernel(
    nz, nx, ny,
    pot, lab, cond, elec, out, coarse,
    p_nat, l_nat, sg, xp, xh, yp, yh, src,
    lw_r, le_r, ls_r, ln_r, inv_r, e_r, rt_r, g_r, r_r, ss,
    fw, fp, ch, on, df, co, ends, wab, km, tt,
    m0s, m0r, m1s, m1r, m2s, m2r, b2s, b2r, m3s, m3r, b3s, b3r, ods, ids, xin, kx,
    loc, zs, zr, xs, xr, ys, yr, ms, mr, bs, br, qs, qr,
):
    p = lax.axis_index("gz")
    gx = lax.axis_index("gx")
    gy = lax.axis_index("gy")
    has_w, has_e = gx > 0, gx < nx - 1
    has_u, has_d = p > 0, p < nz - 1
    up = p < nz // 2
    is_end = (p == 0) | (p == nz - 1)
    is_mid = (p > 0) & (p < nz - 1)
    west, east = {"gx": gx - 1}, {"gx": gx + 1}
    south, north = {"gy": lax.rem(gy + ny - 1, ny)}, {"gy": lax.rem(gy + 1, ny)}
    above, below = {"gz": p - 1}, {"gz": p + 1}
    lane = lax.broadcasted_iota(jnp.int32, (16, 128), 1)
    lane32 = lax.broadcasted_iota(jnp.int32, (32, 128), 1)
    sub8 = lax.broadcasted_iota(jnp.int32, (8, 128), 0)
    row16 = lax.broadcasted_iota(jnp.int32, (16, 128), 0)

    lab_cp = [
        pltpu.make_async_copy(lab.at[:, :, c * 128:(c + 1) * 128], l_nat.at[:, c], loc.at[0, c])
        for c in range(2)
    ]
    pot_cp = [
        pltpu.make_async_copy(pot.at[:, :, :, c * 128:(c + 1) * 128], p_nat.at[:, :, c], loc.at[1, c])
        for c in range(2)
    ]
    for cp in lab_cp + pot_cp:
        cp.start()

    @pl.when(gx == 0)
    def _():
        xh[:, 0] = jnp.zeros((3, 2, 40, 128), F32)

    @pl.when(gx == nx - 1)
    def _():
        xh[:, 1] = jnp.zeros((3, 2, 40, 128), F32)

    barrier = pltpu.get_barrier_semaphore()

    def greet(device):
        pl.semaphore_signal(barrier, inc=1, device_id=device, device_id_type=MESH)

    greet(south)
    greet(north)
    for step in range(1, nz):
        greet({"gz": lax.rem(p + step, nz)})
    for cond_here, device in ((has_w, west), (has_e, east)):
        pl.when(cond_here)(functools.partial(greet, device))

    for cp in lab_cp:
        cp.wait()
    table = [cond[i] for i in range(16)]

    def lookup(z, carry):
        for c in range(2):
            l = jnp.concatenate([l_nat[z, c, pl.ds(j, 8, stride=4), :] for j in range(4)], 0)
            level = table
            for bit in range(4):
                on_bit = (l & (1 << bit)) != 0
                level = [
                    jnp.where(on_bit, level[2 * i + 1], level[2 * i]) for i in range(len(level) // 2)
                ]
            sg[z + 1, c] = recip(level[0])
        return carry

    loop(8, lookup, 0)

    @pl.when(p == 0)
    def _():
        sg[0] = sg[1]

    @pl.when(p == nz - 1)
    def _():
        sg[9] = sg[8]

    def remote(src_ref, dst_ref, send, recv, device):
        return pltpu.make_async_remote_copy(
            src_ref=src_ref, dst_ref=dst_ref, send_sem=send, recv_sem=recv,
            device_id=device, device_id_type=MESH,
        )

    started = []

    def start(copy, where=None):
        started.append((copy, where))
        if where is None:
            copy.start()
        else:
            pl.when(where)(copy.start)

    to_above = remote(sg.at[1], sg.at[9], zs.at[0], zr.at[1], above)
    to_below = remote(sg.at[8], sg.at[0], zs.at[1], zr.at[0], below)

    def lateral_copies(t):
        n = 40 if t == 0 else 32
        return (
            remote(xp.at[t, 0, :, 0:n], xh.at[t, 1, :, 0:n], xs.at[t, 0], xr.at[t, 1], west),
            remote(xp.at[t, 1, :, 0:n], xh.at[t, 0, :, 0:n], xs.at[t, 1], xr.at[t, 0], east),
            remote(yp.at[t, 0], yh.at[t, 1], ys.at[t, 0], yr.at[t, 1], south),
            remote(yp.at[t, 1], yh.at[t, 0], ys.at[t, 1], yr.at[t, 0], north),
        )

    lat = [lateral_copies(t) for t in range(3)]

    def send_x(t):
        start(lat[t][0], has_w)
        start(lat[t][1], has_e)

    def send_y(t):
        start(lat[t][2])
        start(lat[t][3])

    def wait_x(t):
        pl.when(has_e)(lat[t][0].wait_recv)
        pl.when(has_w)(lat[t][1].wait_recv)

    def wait_y(t):
        lat[t][2].wait_recv()
        lat[t][3].wait_recv()

    def pack_sigma(z, acc):
        acc_s, acc_n = acc
        v0, v1 = sg[z + 1, 0], sg[z + 1, 1]
        acc_s = jnp.where(lane32 == 32 + z, roll(v0, 32 + z, 1), acc_s)
        acc_n = jnp.where(lane32 == 32 + z, roll(v1, 33 + z, 1), acc_n)
        for c, v in ((0, v0), (1, v1)):
            xp[0, 0, c, pl.ds(32 + z, 1), :] = v[0:1]
            xp[0, 1, c, pl.ds(32 + z, 1), :] = v[31:32]
        return acc_s, acc_n

    zero32 = jnp.zeros((32, 128), F32)
    acc = loop(8, pack_sigma, (zero32, zero32))
    for cp in pot_cp:
        cp.wait()

    def pack_pot(z, acc):
        acc_s, acc_n = acc
        for s in range(4):
            k = s * 8 + z
            v0, v1 = (
                jnp.concatenate([p_nat[s, z, c, pl.ds(j, 8, stride=4), :] for j in range(4)], 0)
                for c in range(2)
            )
            acc_s = jnp.where(lane32 == k, roll(v0, k, 1), acc_s)
            acc_n = jnp.where(lane32 == k, roll(v1, k + 1, 1), acc_n)
            for c in range(2):
                xp[0, 0, c, pl.ds(k, 1), :] = p_nat[s, z, c, 0:1, :]
                xp[0, 1, c, pl.ds(k, 1), :] = p_nat[s, z, c, 31:32, :]
        return acc_s, acc_n

    acc = loop(8, pack_pot, acc)
    yp[0, 0], yp[0, 1] = acc
    pl.semaphore_wait(
        barrier,
        nz + 1 + has_w.astype(jnp.int32) + has_e.astype(jnp.int32),
    )

    send_x(0)
    start(to_above, has_u)
    start(to_below, has_d)
    send_y(0)

    here = jnp.where(p == 0, 4.0 * ASPECT, 0.0).astype(F32)
    row32 = lax.broadcasted_iota(jnp.int32, (32, 128), 0)
    x_cell = gx * 32 + 4 * (row32 % 8) + row32 // 8
    for c in range(2):
        y_cell = gy * 256 + c * 128 + lane32
        for s in range(4):
            first = jnp.where((x_cell == elec[s, 0]) & (y_cell == elec[s, 1]), here, 0.0)
            second = jnp.where((x_cell == elec[s, 2]) & (y_cell == elec[s, 3]), here, 0.0)
            src[s, c] = first - second

    def centre(g, v):
        return v[8:24] if g == 0 else jnp.concatenate([v[0:8], v[24:32]], 0)

    def west_east(g, v, halo_w, halo_e):
        if g == 0:
            return v[0:16], v[16:32]
        w0 = jnp.where(sub8 == 0, halo_w(), roll(v[24:32], 1, 0))
        e3 = jnp.where(sub8 == 7, halo_e(), roll(v[0:8], 7, 0))
        return jnp.concatenate([w0, v[16:24]], 0), jnp.concatenate([v[8:16], e3], 0)

    def south_north(v0, v1, halo_s, halo_n):
        r0, r1, q0, q1 = roll(v0, 1, 1), roll(v1, 1, 1), roll(v0, 127, 1), roll(v1, 127, 1)
        return (
            (jnp.where(lane == 0, halo_s, r0), jnp.where(lane == 127, q1, q0)),
            (jnp.where(lane == 0, r0, r1), jnp.where(lane == 127, halo_n, q1)),
        )

    def neighbours(g, t, k, v):
        halo_s = roll(centre(g, yh[t, 0]), lax.rem(128 - k, 128), 1)
        halo_n = roll(centre(g, yh[t, 1]), 127 - k, 1)
        ctr = [centre(g, v[c]) for c in range(2)]
        sn = south_north(ctr[0], ctr[1], halo_s, halo_n)
        res = []
        for c in range(2):
            w, e = west_east(
                g, v[c],
                lambda: xh[t, 0, c, pl.ds(k, 1), :],
                lambda: xh[t, 1, c, pl.ds(k, 1), :],
            )
            res.append((ctr[c], w, e) + sn[c])
        return res

    one = jnp.ones((16, 128), F32)
    mask_w = jnp.where(row16 == 0, jnp.where(has_w, 1.0, 0.0).astype(F32), one)
    mask_e = jnp.where(row16 == 15, jnp.where(has_e, 1.0, 0.0).astype(F32), one)
    mask_s = jnp.where(lane == 0, jnp.where(gy > 0, 1.0, 0.0).astype(F32), one)
    mask_n = jnp.where(lane == 127, jnp.where(gy < ny - 1, 1.0, 0.0).astype(F32), one)
    depth2 = 2.0 * ASPECT * ASPECT

    def setup(g):
        top = jnp.where(has_u, depth2, 0.0).astype(F32)
        zero = jnp.zeros((16, 128), F32)
        init = tuple(
            (
                top * recip(centre(g, sg[0, c]) + centre(g, sg[1, c])),
                zero, one, one, zero,
            )
            for c in range(2)
        )

        def body(z, carry):
            near = neighbours(g, 0, 32 + z, [sg[z + 1, c] for c in range(2)])
            res = []
            for c in range(2):
                sh, ratio, gg, rr, s00 = carry[c]
                here, w, e, s, n = near[c]
                lw, le = 2.0 * recip(here + w), 2.0 * recip(here + e)
                ls, ln = 2.0 * recip(here + s), 2.0 * recip(here + n)
                if g == 1:
                    lw, le = lw * mask_w, le * mask_e
                if c == 0:
                    ls = ls * mask_s
                else:
                    ln = ln * mask_n
                dp = depth2 * recip(here + centre(g, sg[z + 2, c]))
                diag = sh + dp + lw + le + ls + ln
                inv = recip(diag - sh * ratio)
                ee = sh * inv
                ratio = dp * inv
                gg = ee * gg
                s00 = s00 + rr * gg
                lw_r[g, z, c], le_r[g, z, c], ls_r[g, z, c], ln_r[g, z, c] = lw, le, ls, ln
                inv_r[g, z, c], rt_r[g, z, c], g_r[g, z, c], r_r[g, z, c] = inv, ratio, gg, rr
                e_r[g, z, c] = jnp.where(z == 0, inv, ee)
                res.append((dp, ratio, gg, rr * ratio, s00))
            return tuple(res)

        last = loop(8, body, init)
        for c in range(2):
            ss[g, 0, c], ss[g, 1, c], ss[g, 2, c], ss[g, 3, c] = (
                last[c][4], last[c][2], last[c][3], last[c][1],
            )

    def forward(g, t, half, load):
        if True:
            def body(z, carry):
                res = []
                for i in range(2):
                    s = 2 * half + i
                    near = neighbours(g, t, s * 8 + z, [load(s, z, c) for c in range(2)])
                    for c in range(2):
                        f, first = carry[2 * i + c]
                        here, w, e, so, no = near[c]
                        rhs = (lw_r[g, z, c] * w + le_r[g, z, c] * e) + (
                            ls_r[g, z, c] * so + ln_r[g, z, c] * no
                        )
                        f = rhs * inv_r[g, z, c] + e_r[g, z, c] * f
                        fw[g, s, z, c] = f
                        res.append((f, first + r_r[g, z, c] * f))
                return tuple(res)

            zero = jnp.zeros((16, 128), F32)
            init = tuple(
                (centre(g, src[2 * half + i, c]), zero) for i in range(2) for c in range(2)
            )
            last = loop(8, body, init)
            for i in range(2):
                for c in range(2):
                    ends[g, 1, 2 * half + i, c], ends[g, 0, 2 * half + i, c] = last[2 * i + c]

    i_out, i_in = jnp.where(up, 0, 1), jnp.where(up, 1, 0)
    i_oo, i_oi = jnp.where(up, 0, 3), jnp.where(up, 1, 2)
    i_io, i_ii = jnp.where(up, 2, 1), jnp.where(up, 3, 0)
    end_of = {"gz": jnp.where(up, 0, nz - 1)}
    mid_of = {"gz": jnp.where(up, 1, nz - 2)}
    twin = {"gz": nz - 1 - p}
    mate = {"gz": jnp.where(lax.rem(p, 2) == 0, p + 1, p - 1)}
    far_mid = {"gz": jnp.where(up, nz - 2, 1)}
    far_end = {"gz": jnp.where(up, nz - 1, 0)}
    i_od = jnp.where(is_end, i_in, i_out)
    slot = jnp.where(is_end, 2, 1)

    def hops(g, h):
        return (
            remote(m1s.at[g, h], m1r.at[g, h], ms.at[g, h, 0], mr.at[g, h, 0], mid_of),
            remote(m2s.at[g, h], m2r.at[g, h], ms.at[g, h, 1], mr.at[g, h, 1], twin),
            remote(m3s.at[g, h], m3r.at[g, h], ms.at[g, h, 2], mr.at[g, h, 2], end_of),
        )

    def factor_hops(g):
        return (
            remote(m0s.at[g], m0r.at[g], bs.at[g, 0], br.at[g, 0], mid_of),
            remote(b2s.at[g], b2r.at[g], bs.at[g, 1], br.at[g, 1], twin),
            remote(b3s.at[g], b3r.at[g], bs.at[g, 2], br.at[g, 2], end_of),
        )

    def cross(g, h):
        def one_of(src_ref, at, i, device):
            return remote(src_ref.at[g, h], xin.at[g, h, at], qs.at[g, h, i], qr.at[g, h, at], device)
        return (
            one_of(ids, slot, 0, far_mid), one_of(ids, slot, 1, far_end), one_of(ods, 0, 2, mate),
        )

    hop = [[hops(g, h) for h in range(2)] for g in range(2)]
    fhop = [factor_hops(g) for g in range(2)]
    pairs = [(i, c) for i in range(2) for c in range(2)]

    def end_factor(g):
        @pl.when(is_end)
        def _():
            m0s[g] = ss[g, i_ii]
        start(fhop[g][0], is_end)

    def end_send(g, h):
        @pl.when(is_end)
        def _():
            for i, c in pairs:
                m1s[g, h, i, c] = ends[g, i_in, 2 * h + i, c]
        start(hop[g][h][0], is_end)

    def mid_factor(g):
        @pl.when(is_mid)
        def _():
            fhop[g][0].wait_recv()
            for c in range(2):
                b_out = m0r[g, c]
                q = 1.0 / (1.0 - ss[g, i_oo, c] * b_out)
                km[g, 0, c] = q
                km[g, 1, c] = q * ss[g, i_io, c]
                b2s[g, 0, c] = ss[g, i_ii, c] + ss[g, i_oi, c] * b_out * q * ss[g, i_io, c]
                b2s[g, 1, c] = ss[g, i_oi, c] * q
        start(fhop[g][1], is_mid)

    def mid_forward(g, h):
        @pl.when(is_mid)
        def _():
            hop[g][h][0].wait_recv()
            for i, c in pairs:
                s = 2 * h + i
                a_out = m1r[g, h, i, c]
                first = (ends[g, i_out, s, c] + ss[g, i_oo, c] * a_out) * km[g, 0, c]
                tt[g, s, c] = first
                m2s[g, h, i, c] = ends[g, i_in, s, c] + ss[g, i_oi, c] * (a_out + m0r[g, c] * first)
        start(hop[g][h][1], is_mid)

    def mid_match(g):
        @pl.when(is_mid)
        def _():
            fhop[g][1].wait_recv()
            for c in range(2):
                km[g, 2, c] = 1.0 / (1.0 - b2r[g, 0, c] * b2s[g, 0, c])

    def mid_solve(g, h):
        @pl.when(is_mid)
        def _():
            hop[g][h][1].wait_recv()
            for i, c in pairs:
                s = 2 * h + i
                w_in = (m2r[g, h, i, c] + b2r[g, 0, c] * m2s[g, h, i, c]) * km[g, 2, c]
                first = tt[g, s, c] + km[g, 1, c] * w_in
                m3s[g, h, i, c] = first
                wab[g, i_in, s, c] = w_in
                wab[g, i_out, s, c] = m1r[g, h, i, c] + m0r[g, c] * first
        start(hop[g][h][2], is_mid)

    def end_solve(g, h):
        @pl.when(is_end)
        def _():
            hop[g][h][2].wait_recv()
            for i, c in pairs:
                wab[g, i_in, 2 * h + i, c] = m3r[g, h, i, c]
                wab[g, i_out, 2 * h + i, c] = jnp.zeros((16, 128), F32)

    def mid_extra(g):
        @pl.when(is_mid)
        def _():
            for c in range(2):
                b_out, b_in, q = m0r[g, c], b2r[g, 0, c], km[g, 0, c]
                s_oo, s_oi, s_io, s_ii = ss[g, i_oo, c], ss[g, i_oi, c], ss[g, i_io, c], ss[g, i_ii, c]
                g_mine, g_in, match = b2s[g, 1, c], b2r[g, 1, c], km[g, 2, c]
                r = 1.0 / (1.0 - s_ii * b_in)
                h = s_io * r
                b3s[g, 0, c] = s_oo + h * b_in * s_oi
                b3s[g, 1, c] = h
                b3s[g, 2, c] = h * g_in
                kx[g, 0, c] = match * b_in
                kx[g, 1, c] = match * b_in * g_mine
                kx[g, 2, c] = match
                kx[g, 3, c] = match * g_in
                kx[g, 4, c] = q
                kx[g, 5, c] = b_out * q
                kx[g, 6, c] = b_out * q * s_io
                kx[g, 7, c] = s_oi * b_out * q
                kx[g, 8, c] = h * b_in
        start(fhop[g][2], is_mid)

    def end_extra(g):
        @pl.when(is_end)
        def _():
            fhop[g][2].wait_recv()
            for c in range(2):
                c_in = b3r[g, 0, c]
                k = 1.0 / (1.0 - c_in * ss[g, i_ii, c])
                kx[g, 0, c] = k * c_in
                kx[g, 1, c] = k
                kx[g, 2, c] = k * b3r[g, 1, c]
                kx[g, 3, c] = k * b3r[g, 2, c]
                for i in range(4, 9):
                    kx[g, i, c] = jnp.zeros((16, 128), F32)

    def cross_send(g, h):
        for i, c in pairs:
            s = 2 * h + i
            ids[g, h, i, c] = ends[g, i_in, s, c] + kx[g, 7, c] * ends[g, i_out, s, c]
            ods[g, h, i, c] = ends[g, i_od, s, c] + kx[g, 8, c] * ends[g, i_in, s, c]
        for copy in cross(g, h):
            start(copy)

    def cross_solve(g, h):
        for at in range(3):
            remote(
                ids.at[g, h], xin.at[g, h, at], qs.at[g, h, 0], qr.at[g, h, at], far_mid
            ).wait_recv()
        for i, c in pairs:
            s = 2 * h + i
            near, r1, r2 = xin[g, h, 0, i, c], xin[g, h, 1, i, c], xin[g, h, 2, i, c]
            w_in = (kx[g, 0, c] * ids[g, h, i, c] + kx[g, 1, c] * near) + (
                kx[g, 2, c] * r1 + kx[g, 3, c] * r2
            )
            wab[g, i_in, s, c] = w_in
            wab[g, i_out, s, c] = (
                kx[g, 4, c] * near + kx[g, 5, c] * ends[g, i_out, s, c] + kx[g, 6, c] * w_in
            )

    def backward(t, g, h, emit, acc):
        def body(step, carry):
            z = 7 - step
            acc_s, acc_n, w_next = carry
            res = []
            for i in range(2):
                s = 2 * h + i
                k = s * 8 + z
                both = []
                for c in range(2):
                    w = fw[g, s, z, c] + g_r[g, z, c] * wab[g, 0, s, c] + (
                        rt_r[g, z, c] * w_next[2 * i + c]
                    )
                    res.append(w)
                    v = emit(s, z, c, w)
                    if g == 1:
                        xp[t + 1, 0, c, pl.ds(k, 1), :] = v[0:1]
                        xp[t + 1, 1, c, pl.ds(k, 1), :] = v[15:16]
                    both.append(v)
                acc_s = jnp.where(lane == k, roll(both[0], k, 1), acc_s)
                acc_n = jnp.where(lane == k, roll(both[1], k + 1, 1), acc_n)
            return acc_s, acc_n, tuple(res)

        first = tuple(wab[g, 1, 2 * h + i, c] for i in range(2) for c in range(2))
        return loop(8, body, acc + (first,))[:2]

    def pack_y(t, g, acc):
        for d in range(2):
            if g == 0:
                yp[t + 1, d, 8:24] = acc[d]
            else:
                yp[t + 1, d, 0:8] = acc[d][0:8]
                yp[t + 1, d, 24:32] = acc[d][8:16]

    def put(ref, g, s, z, c, v):
        if g == 0:
            ref[s, z, c, 8:24] = v
        else:
            ref[s, z, c, 0:8] = v[0:8]
            ref[s, z, c, 24:32] = v[8:16]

    def emit_first(g):
        def emit(s, z, c, w):
            put(fp, g, s, z, c, w)
            return w
        return emit

    def emit_relaxed(g):
        rows = (1, 2) if g == 0 else (0, 3)
        def emit(s, z, c, w):
            change = w - centre(g, fp[s, z, c])
            put(ch, g, s, z, c, change)
            for i in range(2):
                on[s, z, c, pl.ds(rows[i], 8, stride=4), :] = w[8 * i:8 * i + 8]
            return change
        return emit

    def load_pot(s, z, c):
        return jnp.concatenate([p_nat[s, z, c, pl.ds(j, 8, stride=4), :] for j in range(4)], 0)

    def load_first(s, z, c):
        return fp[s, z, c]

    empty = (jnp.zeros((16, 128), F32),) * 2

    wait_y(0)
    pl.when(has_d)(to_above.wait_recv)
    pl.when(has_u)(to_below.wait_recv)
    setup(0)
    end_factor(0)
    for h in range(2):
        forward(0, 0, h, load_pot)
        end_send(0, h)
    wait_x(0)
    setup(1)
    end_factor(1)
    for h in range(2):
        forward(1, 0, h, load_pot)
        end_send(1, h)
    for g in range(2):
        mid_factor(g)
        for h in range(2):
            mid_forward(g, h)
    for g in range(2):
        mid_match(g)
        acc = empty
        for h in range(2):
            mid_solve(g, h)
        for h in range(2):
            end_solve(g, h)
            acc = backward(0, g, h, emit_first(g), acc)
        pack_y(0, g, acc)
    send_x(1)
    send_y(1)
    for g in range(2):
        mid_extra(g)
    for g in range(2):
        end_extra(g)

    wait_y(1)
    for h in range(2):
        forward(0, 1, h, load_first)
        cross_send(0, h)
    wait_x(1)
    for h in range(2):
        forward(1, 1, h, load_first)
        cross_send(1, h)
    for g in range(2):
        acc = empty
        for h in range(2):
            cross_solve(g, h)
            acc = backward(1, g, h, emit_relaxed(g), acc)
        pack_y(1, g, acc)
    send_x(2)
    send_y(2)
    out_cp = [
        pltpu.make_async_copy(on.at[:, :, c], out.at[:, :, :, c * 128:(c + 1) * 128], loc.at[0, c])
        for c in range(2)
    ]
    for cp in out_cp:
        cp.start()

    pick = (
        lax.broadcasted_iota(jnp.int32, (256, 128), 0) // 2
        == lax.broadcasted_iota(jnp.int32, (256, 128), 1)
    ).astype(F32)

    def defect(g):
        def body(z, carry):
            rows = []
            for s in range(4):
                near = neighbours(g, 2, s * 8 + z, [ch[s, z, c] for c in range(2)])
                both = []
                for c in range(2):
                    here, w, e, so, no = near[c]
                    d = (lw_r[g, z, c] * w + le_r[g, z, c] * e) + (
                        ls_r[g, z, c] * so + ln_r[g, z, c] * no
                    )
                    if g == 0:
                        df[s, z, c] = d
                    else:
                        both.append(d + df[s, z, c])
                if g == 1:
                    rows.append(jnp.concatenate(both, 1))
            if g == 1:
                d = jnp.dot(
                    jnp.concatenate(rows, 0), pick,
                    precision=lax.Precision.HIGHEST, preferred_element_type=F32,
                )
                for s in range(4):
                    co[s, z, pl.ds(0, 8, stride=2), :] = d[16 * s:16 * s + 8]
                    co[s, z, pl.ds(1, 8, stride=2), :] = d[16 * s + 8:16 * s + 16]
            return carry

        loop(8, body, 0)

    wait_y(2)
    defect(0)
    wait_x(2)
    defect(1)
    co_cp = pltpu.make_async_copy(co, coarse, loc.at[1, 0])
    co_cp.start()

    for copy, where in started:
        if where is None:
            copy.wait_send()
        else:
            pl.when(where)(copy.wait_send)
    for cp in out_cp:
        cp.wait()
    co_cp.wait()


def store_kernel(relaxed, restricted, out, coarse, held, held_coarse, sems):
    fetch = [pltpu.make_async_copy(restricted, held_coarse, sems.at[0, 4])] + [
        pltpu.make_async_copy(relaxed.at[s], held.at[s], sems.at[0, s]) for s in range(4)
    ]
    store = [pltpu.make_async_copy(held_coarse, coarse, sems.at[1, 4])] + [
        pltpu.make_async_copy(held.at[s], out.at[s], sems.at[1, s]) for s in range(4)
    ]
    for cp in fetch:
        cp.start()
    for cp, then in zip(fetch, store):
        cp.wait()
        then.start()
    for cp in store:
        cp.wait()


def solution(mesh):
    nz, nx, ny = mesh.shape["gz"], mesh.shape["gx"], mesh.shape["gy"]

    def body(potential, labels, conductivity, electrodes):
        coef = pltpu.VMEM((2, 8, 2, 16, 128), F32)
        field = pltpu.VMEM((4, 8, 2, 32, 128), F32)
        msg = pltpu.VMEM((2, 2, 2, 2, 16, 128), F32)
        part1 = pltpu.VMEM((2, 2, 16, 128), F32)
        part2 = pltpu.VMEM((2, 2, 2, 16, 128), F32)
        part3 = pltpu.VMEM((2, 3, 2, 16, 128), F32)
        dma = pltpu.SemaphoreType.DMA
        shapes = (
            jax.ShapeDtypeStruct((4, 8, 32, 256), F32),
            jax.ShapeDtypeStruct((4, 8, 16, 128), F32),
        )
        anywhere = pl.BlockSpec(memory_space=pl.ANY)
        results = pl.pallas_call(
            functools.partial(kernel, nz, nx, ny),
            out_shape=shapes,
            in_specs=[
                pl.BlockSpec(memory_space=pl.ANY),
                pl.BlockSpec(memory_space=pl.ANY),
                pl.BlockSpec(memory_space=pltpu.SMEM),
                pl.BlockSpec(memory_space=pltpu.SMEM),
            ],
            out_specs=(pl.BlockSpec(memory_space=pl.ANY), pl.BlockSpec(memory_space=pl.ANY)),
            scratch_shapes=[
                field,
                pltpu.VMEM((8, 2, 32, 128), jnp.int32),
                pltpu.VMEM((10, 2, 32, 128), F32),
                pltpu.VMEM((3, 2, 2, 40, 128), F32),
                pltpu.VMEM((3, 2, 2, 40, 128), F32),
                pltpu.VMEM((3, 2, 32, 128), F32),
                pltpu.VMEM((3, 2, 32, 128), F32),
                pltpu.VMEM((4, 2, 32, 128), F32),
                coef, coef, coef, coef, coef, coef, coef, coef, coef,
                pltpu.VMEM((2, 4, 2, 16, 128), F32),
                pltpu.VMEM((2, 4, 8, 2, 16, 128), F32),
                field, field, field,
                pltpu.VMEM((4, 8, 2, 16, 128), F32),
                pltpu.VMEM((4, 8, 16, 128), F32),
                pltpu.VMEM((2, 2, 4, 2, 16, 128), F32),
                pltpu.VMEM((2, 2, 4, 2, 16, 128), F32),
                pltpu.VMEM((2, 3, 2, 16, 128), F32),
                pltpu.VMEM((2, 4, 2, 16, 128), F32),
                part1, part1, msg, msg, msg, msg, part2, part2, msg, msg, part3, part3, msg, msg,
                pltpu.VMEM((2, 2, 3, 2, 2, 16, 128), F32),
                pltpu.VMEM((2, 9, 2, 16, 128), F32),
                dma((2, 2)), dma((2,)), dma((2,)),
                dma((3, 2)), dma((3, 2)), dma((3, 2)), dma((3, 2)),
                dma((2, 2, 3)), dma((2, 2, 3)), dma((2, 3)), dma((2, 3)),
                dma((2, 2, 3)), dma((2, 2, 3)),
            ],
            compiler_params=pltpu.CompilerParams(
                collective_id=0, has_side_effects=True, vmem_limit_bytes=60 * 1024 * 1024,
            ),
        )(potential, labels, conductivity, electrodes)
        return pl.pallas_call(
            store_kernel,
            out_shape=shapes,
            in_specs=[anywhere, anywhere],
            out_specs=(anywhere, anywhere),
            scratch_shapes=[
                pltpu.VMEM((4, 8, 32, 256), F32),
                pltpu.VMEM((4, 8, 16, 128), F32),
                pltpu.SemaphoreType.DMA((2, 5)),
            ],
        )(*results)

    return jax.shard_map(
        body,
        mesh=mesh,
        in_specs=(P(None, "gz", "gx", "gy"), P("gz", "gx", "gy"), P(), P()),
        out_specs=(P(None, "gz", "gx", "gy"), P(None, "gz", "gx", "gy")),
        check_vma=False,
    )
```

```python
import functools

import jax
import jax.numpy as jnp
from jax import lax
from jax.experimental import pallas as pl
from jax.experimental.pallas import tpu as pltpu
from jax.sharding import PartitionSpec as P

ASPECT = 128
MESH = pl.DeviceIdType.MESH
F32 = jnp.float32
UNROLL = True


def roll(v, shift, axis):
    return pltpu.roll(v, shift, axis)


def recip(v):
    return pltpu.reciprocal(v, approx=True)


def loop(count, body, init):
    if UNROLL:
        for i in range(count):
            init = body(i, init)
        return init
    return lax.fori_loop(0, count, body, init)


def kernel(
    nz, nx, ny,
    pot, lab, cond, elec, out, coarse,
    p_nat, l_nat, sg, xp, xh, yp, yh, src,
    lw_r, le_r, ls_r, ln_r, inv_r, e_r, rt_r, g_r, r_r, ss,
    fw, fp, ch, on, df, co, ends, wab, km, tt,
    m0s, m0r, m1s, m1r, m2s, m2r, b2s, b2r, m3s, m3r, b3s, b3r, ods, ids, xin, kx,
    loc, zs, zr, xs, xr, ys, yr, ms, mr, bs, br, qs, qr,
):
    p = lax.axis_index("gz")
    gx = lax.axis_index("gx")
    gy = lax.axis_index("gy")
    has_w, has_e = gx > 0, gx < nx - 1
    has_u, has_d = p > 0, p < nz - 1
    up = p < nz // 2
    is_end = (p == 0) | (p == nz - 1)
    is_mid = (p > 0) & (p < nz - 1)
    west, east = {"gx": gx - 1}, {"gx": gx + 1}
    south, north = {"gy": lax.rem(gy + ny - 1, ny)}, {"gy": lax.rem(gy + 1, ny)}
    above, below = {"gz": p - 1}, {"gz": p + 1}
    lane = lax.broadcasted_iota(jnp.int32, (16, 128), 1)
    lane32 = lax.broadcasted_iota(jnp.int32, (32, 128), 1)
    sub8 = lax.broadcasted_iota(jnp.int32, (8, 128), 0)
    row16 = lax.broadcasted_iota(jnp.int32, (16, 128), 0)

    lab_cp = [
        pltpu.make_async_copy(lab.at[:, :, c * 128:(c + 1) * 128], l_nat.at[:, c], loc.at[0, c])
        for c in range(2)
    ]
    pot_cp = [
        pltpu.make_async_copy(pot.at[:, :, :, c * 128:(c + 1) * 128], p_nat.at[:, :, c], loc.at[1, c])
        for c in range(2)
    ]
    for cp in lab_cp + pot_cp:
        cp.start()

    @pl.when(gx == 0)
    def _():
        xh[:, 0] = jnp.zeros((3, 2, 40, 128), F32)

    @pl.when(gx == nx - 1)
    def _():
        xh[:, 1] = jnp.zeros((3, 2, 40, 128), F32)

    barrier = pltpu.get_barrier_semaphore()

    def greet(device):
        pl.semaphore_signal(barrier, inc=1, device_id=device, device_id_type=MESH)

    greet(south)
    greet(north)
    for step in range(1, nz):
        greet({"gz": lax.rem(p + step, nz)})
    for cond_here, device in ((has_w, west), (has_e, east)):
        pl.when(cond_here)(functools.partial(greet, device))

    for cp in lab_cp:
        cp.wait()
    table = [cond[i] for i in range(16)]

    def lookup(z, carry):
        for c in range(2):
            l = jnp.concatenate([l_nat[z, c, pl.ds(j, 8, stride=4), :] for j in range(4)], 0)
            level = table
            for bit in range(4):
                on_bit = (l & (1 << bit)) != 0
                level = [
                    jnp.where(on_bit, level[2 * i + 1], level[2 * i]) for i in range(len(level) // 2)
                ]
            sg[z + 1, c] = recip(level[0])
        return carry

    loop(8, lookup, 0)

    @pl.when(p == 0)
    def _():
        sg[0] = sg[1]

    @pl.when(p == nz - 1)
    def _():
        sg[9] = sg[8]

    def remote(src_ref, dst_ref, send, recv, device):
        return pltpu.make_async_remote_copy(
            src_ref=src_ref, dst_ref=dst_ref, send_sem=send, recv_sem=recv,
            device_id=device, device_id_type=MESH,
        )

    started = []

    def start(copy, where=None):
        started.append((copy, where))
        if where is None:
            copy.start()
        else:
            pl.when(where)(copy.start)

    to_above = remote(sg.at[1], sg.at[9], zs.at[0], zr.at[1], above)
    to_below = remote(sg.at[8], sg.at[0], zs.at[1], zr.at[0], below)

    def lateral_copies(t):
        n = 40 if t == 0 else 32
        return (
            remote(xp.at[t, 0, :, 0:n], xh.at[t, 1, :, 0:n], xs.at[t, 0], xr.at[t, 1], west),
            remote(xp.at[t, 1, :, 0:n], xh.at[t, 0, :, 0:n], xs.at[t, 1], xr.at[t, 0], east),
        )

    def y_copies(t, g):
        return (
            remote(yp.at[t, g, 0], yh.at[t, g, 1], ys.at[t, g, 0], yr.at[t, g, 1], south),
            remote(yp.at[t, g, 1], yh.at[t, g, 0], ys.at[t, g, 1], yr.at[t, g, 0], north),
        )

    lat = [lateral_copies(t) for t in range(3)]
    laty = [[y_copies(t, g) for g in range(2)] for t in range(3)]

    def send_x(t):
        start(lat[t][0], has_w)
        start(lat[t][1], has_e)

    def send_y(t, g):
        for copy in laty[t][g]:
            start(copy)

    def wait_x(t):
        pl.when(has_e)(lat[t][0].wait_recv)
        pl.when(has_w)(lat[t][1].wait_recv)

    def wait_y(t, g):
        for copy in laty[t][g]:
            copy.wait_recv()

    def pack_sigma(z, acc):
        acc_s, acc_n = acc
        v0, v1 = sg[z + 1, 0], sg[z + 1, 1]
        acc_s = jnp.where(lane32 == 32 + z, roll(v0, 32 + z, 1), acc_s)
        acc_n = jnp.where(lane32 == 32 + z, roll(v1, 33 + z, 1), acc_n)
        for c, v in ((0, v0), (1, v1)):
            xp[0, 0, c, pl.ds(32 + z, 1), :] = v[0:1]
            xp[0, 1, c, pl.ds(32 + z, 1), :] = v[31:32]
        return acc_s, acc_n

    zero32 = jnp.zeros((32, 128), F32)
    acc = loop(8, pack_sigma, (zero32, zero32))
    for cp in pot_cp:
        cp.wait()

    def pack_pot(z, acc):
        acc_s, acc_n = acc
        for s in range(4):
            k = s * 8 + z
            v0, v1 = (
                jnp.concatenate([p_nat[s, z, c, pl.ds(j, 8, stride=4), :] for j in range(4)], 0)
                for c in range(2)
            )
            acc_s = jnp.where(lane32 == k, roll(v0, k, 1), acc_s)
            acc_n = jnp.where(lane32 == k, roll(v1, k + 1, 1), acc_n)
            for c in range(2):
                xp[0, 0, c, pl.ds(k, 1), :] = p_nat[s, z, c, 0:1, :]
                xp[0, 1, c, pl.ds(k, 1), :] = p_nat[s, z, c, 31:32, :]
        return acc_s, acc_n

    acc = loop(8, pack_pot, acc)
    for d in range(2):
        yp[0, 0, d] = acc[d][8:24]
        yp[0, 1, d] = jnp.concatenate([acc[d][0:8], acc[d][24:32]], 0)
    pl.semaphore_wait(
        barrier,
        nz + 1 + has_w.astype(jnp.int32) + has_e.astype(jnp.int32),
    )

    start(to_above, has_u)
    start(to_below, has_d)
    send_y(0, 0)
    send_y(0, 1)
    send_x(0)

    here = jnp.where(p == 0, 4.0 * ASPECT, 0.0).astype(F32)
    row32 = lax.broadcasted_iota(jnp.int32, (32, 128), 0)
    x_cell = gx * 32 + 4 * (row32 % 8) + row32 // 8
    for c in range(2):
        y_cell = gy * 256 + c * 128 + lane32
        for s in range(4):
            first = jnp.where((x_cell == elec[s, 0]) & (y_cell == elec[s, 1]), here, 0.0)
            second = jnp.where((x_cell == elec[s, 2]) & (y_cell == elec[s, 3]), here, 0.0)
            src[s, c] = first - second

    def centre(g, v):
        return v[8:24] if g == 0 else jnp.concatenate([v[0:8], v[24:32]], 0)

    def west_east(g, v, halo_w, halo_e):
        if g == 0:
            return v[0:16], v[16:32]
        w0 = jnp.where(sub8 == 0, halo_w(), roll(v[24:32], 1, 0))
        e3 = jnp.where(sub8 == 7, halo_e(), roll(v[0:8], 7, 0))
        return jnp.concatenate([w0, v[16:24]], 0), jnp.concatenate([v[8:16], e3], 0)

    def south_north(v0, v1, halo_s, halo_n):
        r0, r1, q0, q1 = roll(v0, 1, 1), roll(v1, 1, 1), roll(v0, 127, 1), roll(v1, 127, 1)
        return (
            (jnp.where(lane == 0, halo_s, r0), jnp.where(lane == 127, q1, q0)),
            (jnp.where(lane == 0, r0, r1), jnp.where(lane == 127, halo_n, q1)),
        )

    def neighbours(g, t, k, v):
        halo_s = roll(yh[t, g, 0], lax.rem(128 - k, 128), 1)
        halo_n = roll(yh[t, g, 1], 127 - k, 1)
        ctr = [centre(g, v[c]) for c in range(2)]
        sn = south_north(ctr[0], ctr[1], halo_s, halo_n)
        res = []
        for c in range(2):
            w, e = west_east(
                g, v[c],
                lambda: xh[t, 0, c, pl.ds(k, 1), :],
                lambda: xh[t, 1, c, pl.ds(k, 1), :],
            )
            res.append((ctr[c], w, e) + sn[c])
        return res

    one = jnp.ones((16, 128), F32)
    mask_w = jnp.where(row16 == 0, jnp.where(has_w, 1.0, 0.0).astype(F32), one)
    mask_e = jnp.where(row16 == 15, jnp.where(has_e, 1.0, 0.0).astype(F32), one)
    mask_s = jnp.where(lane == 0, jnp.where(gy > 0, 1.0, 0.0).astype(F32), one)
    mask_n = jnp.where(lane == 127, jnp.where(gy < ny - 1, 1.0, 0.0).astype(F32), one)
    depth2 = 2.0 * ASPECT * ASPECT

    def setup(g):
        top = jnp.where(has_u, depth2, 0.0).astype(F32)
        zero = jnp.zeros((16, 128), F32)
        init = tuple(
            (
                top * recip(centre(g, sg[0, c]) + centre(g, sg[1, c])),
                zero, one, one, zero,
            )
            for c in range(2)
        )

        def body(z, carry):
            near = neighbours(g, 0, 32 + z, [sg[z + 1, c] for c in range(2)])
            res = []
            for c in range(2):
                sh, ratio, gg, rr, s00 = carry[c]
                here, w, e, s, n = near[c]
                lw, le = 2.0 * recip(here + w), 2.0 * recip(here + e)
                ls, ln = 2.0 * recip(here + s), 2.0 * recip(here + n)
                if g == 1:
                    lw, le = lw * mask_w, le * mask_e
                if c == 0:
                    ls = ls * mask_s
                else:
                    ln = ln * mask_n
                dp = depth2 * recip(here + centre(g, sg[z + 2, c]))
                diag = sh + dp + lw + le + ls + ln
                inv = recip(diag - sh * ratio)
                ee = sh * inv
                ratio = dp * inv
                gg = ee * gg
                s00 = s00 + rr * gg
                lw_r[g, z, c], le_r[g, z, c], ls_r[g, z, c], ln_r[g, z, c] = lw, le, ls, ln
                inv_r[g, z, c], rt_r[g, z, c], g_r[g, z, c], r_r[g, z, c] = inv, ratio, gg, rr
                e_r[g, z, c] = jnp.where(z == 0, inv, ee)
                res.append((dp, ratio, gg, rr * ratio, s00))
            return tuple(res)

        last = loop(8, body, init)
        for c in range(2):
            ss[g, 0, c], ss[g, 1, c], ss[g, 2, c], ss[g, 3, c] = (
                last[c][4], last[c][2], last[c][3], last[c][1],
            )

    def forward(g, t, half, load):
        if True:
            def body(z, carry):
                res = []
                for i in range(2):
                    s = 2 * half + i
                    near = neighbours(g, t, s * 8 + z, [load(s, z, c) for c in range(2)])
                    for c in range(2):
                        f, first = carry[2 * i + c]
                        here, w, e, so, no = near[c]
                        rhs = (lw_r[g, z, c] * w + le_r[g, z, c] * e) + (
                            ls_r[g, z, c] * so + ln_r[g, z, c] * no
                        )
                        f = rhs * inv_r[g, z, c] + e_r[g, z, c] * f
                        fw[g, s, z, c] = f
                        res.append((f, first + r_r[g, z, c] * f))
                return tuple(res)

            zero = jnp.zeros((16, 128), F32)
            init = tuple(
                (centre(g, src[2 * half + i, c]), zero) for i in range(2) for c in range(2)
            )
            last = loop(8, body, init)
            for i in range(2):
                for c in range(2):
                    ends[g, 1, 2 * half + i, c], ends[g, 0, 2 * half + i, c] = last[2 * i + c]

    i_out, i_in = jnp.where(up, 0, 1), jnp.where(up, 1, 0)
    i_oo, i_oi = jnp.where(up, 0, 3), jnp.where(up, 1, 2)
    i_io, i_ii = jnp.where(up, 2, 1), jnp.where(up, 3, 0)
    end_of = {"gz": jnp.where(up, 0, nz - 1)}
    mid_of = {"gz": jnp.where(up, 1, nz - 2)}
    twin = {"gz": nz - 1 - p}
    mate = {"gz": jnp.where(lax.rem(p, 2) == 0, p + 1, p - 1)}
    far_mid = {"gz": jnp.where(up, nz - 2, 1)}
    far_end = {"gz": jnp.where(up, nz - 1, 0)}
    i_od = jnp.where(is_end, i_in, i_out)
    slot = jnp.where(is_end, 2, 1)

    def hops(g, h):
        return (
            remote(m1s.at[g, h], m1r.at[g, h], ms.at[g, h, 0], mr.at[g, h, 0], mid_of),
            remote(m2s.at[g, h], m2r.at[g, h], ms.at[g, h, 1], mr.at[g, h, 1], twin),
            remote(m3s.at[g, h], m3r.at[g, h], ms.at[g, h, 2], mr.at[g, h, 2], end_of),
        )

    def factor_hops(g):
        return (
            remote(m0s.at[g], m0r.at[g], bs.at[g, 0], br.at[g, 0], mid_of),
            remote(b2s.at[g], b2r.at[g], bs.at[g, 1], br.at[g, 1], twin),
            remote(b3s.at[g], b3r.at[g], bs.at[g, 2], br.at[g, 2], end_of),
        )

    def cross(g, h):
        def one_of(src_ref, at, i, device):
            return remote(src_ref.at[g, h], xin.at[g, h, at], qs.at[g, h, i], qr.at[g, h, at], device)
        return (
            one_of(ids, slot, 0, far_mid), one_of(ids, slot, 1, far_end), one_of(ods, 0, 2, mate),
        )

    hop = [[hops(g, h) for h in range(2)] for g in range(2)]
    fhop = [factor_hops(g) for g in range(2)]
    pairs = [(i, c) for i in range(2) for c in range(2)]

    def end_factor(g):
        @pl.when(is_end)
        def _():
            m0s[g] = ss[g, i_ii]
        start(fhop[g][0], is_end)

    def end_send(g, h):
        @pl.when(is_end)
        def _():
            for i, c in pairs:
                m1s[g, h, i, c] = ends[g, i_in, 2 * h + i, c]
        start(hop[g][h][0], is_end)

    def mid_factor(g):
        @pl.when(is_mid)
        def _():
            fhop[g][0].wait_recv()
            for c in range(2):
                b_out = m0r[g, c]
                q = 1.0 / (1.0 - ss[g, i_oo, c] * b_out)
                km[g, 0, c] = q
                km[g, 1, c] = q * ss[g, i_io, c]
                b2s[g, 0, c] = ss[g, i_ii, c] + ss[g, i_oi, c] * b_out * q * ss[g, i_io, c]
                b2s[g, 1, c] = ss[g, i_oi, c] * q
        start(fhop[g][1], is_mid)

    def mid_forward(g, h):
        @pl.when(is_mid)
        def _():
            hop[g][h][0].wait_recv()
            for i, c in pairs:
                s = 2 * h + i
                a_out = m1r[g, h, i, c]
                first = (ends[g, i_out, s, c] + ss[g, i_oo, c] * a_out) * km[g, 0, c]
                tt[g, s, c] = first
                m2s[g, h, i, c] = ends[g, i_in, s, c] + ss[g, i_oi, c] * (a_out + m0r[g, c] * first)
        start(hop[g][h][1], is_mid)

    def mid_match(g):
        @pl.when(is_mid)
        def _():
            fhop[g][1].wait_recv()
            for c in range(2):
                km[g, 2, c] = 1.0 / (1.0 - b2r[g, 0, c] * b2s[g, 0, c])

    def mid_solve(g, h):
        @pl.when(is_mid)
        def _():
            hop[g][h][1].wait_recv()
            for i, c in pairs:
                s = 2 * h + i
                w_in = (m2r[g, h, i, c] + b2r[g, 0, c] * m2s[g, h, i, c]) * km[g, 2, c]
                first = tt[g, s, c] + km[g, 1, c] * w_in
                m3s[g, h, i, c] = first
                wab[g, i_in, s, c] = w_in
                wab[g, i_out, s, c] = m1r[g, h, i, c] + m0r[g, c] * first
        start(hop[g][h][2], is_mid)

    def end_solve(g, h):
        @pl.when(is_end)
        def _():
            hop[g][h][2].wait_recv()
            for i, c in pairs:
                wab[g, i_in, 2 * h + i, c] = m3r[g, h, i, c]
                wab[g, i_out, 2 * h + i, c] = jnp.zeros((16, 128), F32)

    def mid_extra(g):
        @pl.when(is_mid)
        def _():
            for c in range(2):
                b_out, b_in, q = m0r[g, c], b2r[g, 0, c], km[g, 0, c]
                s_oo, s_oi, s_io, s_ii = ss[g, i_oo, c], ss[g, i_oi, c], ss[g, i_io, c], ss[g, i_ii, c]
                g_mine, g_in, match = b2s[g, 1, c], b2r[g, 1, c], km[g, 2, c]
                r = 1.0 / (1.0 - s_ii * b_in)
                h = s_io * r
                b3s[g, 0, c] = s_oo + h * b_in * s_oi
                b3s[g, 1, c] = h
                b3s[g, 2, c] = h * g_in
                kx[g, 0, c] = match * b_in
                kx[g, 1, c] = match * b_in * g_mine
                kx[g, 2, c] = match
                kx[g, 3, c] = match * g_in
                kx[g, 4, c] = q
                kx[g, 5, c] = b_out * q
                kx[g, 6, c] = b_out * q * s_io
                kx[g, 7, c] = s_oi * b_out * q
                kx[g, 8, c] = h * b_in
        start(fhop[g][2], is_mid)

    def end_extra(g):
        @pl.when(is_end)
        def _():
            fhop[g][2].wait_recv()
            for c in range(2):
                c_in = b3r[g, 0, c]
                k = 1.0 / (1.0 - c_in * ss[g, i_ii, c])
                kx[g, 0, c] = k * c_in
                kx[g, 1, c] = k
                kx[g, 2, c] = k * b3r[g, 1, c]
                kx[g, 3, c] = k * b3r[g, 2, c]
                for i in range(4, 7):
                    kx[g, i, c] = jnp.zeros((16, 128), F32)

    def cross_send(g, h):
        for i, c in pairs:
            s = 2 * h + i
            ids[g, h, i, c] = ends[g, i_in, s, c] + kx[g, 7, c] * ends[g, i_out, s, c]
            ods[g, h, i, c] = ends[g, i_od, s, c] + kx[g, 8, c] * ends[g, i_in, s, c]
        for copy in cross(g, h):
            start(copy)

    def cross_solve(g, h):
        for at in range(3):
            remote(
                ids.at[g, h], xin.at[g, h, at], qs.at[g, h, 0], qr.at[g, h, at], far_mid
            ).wait_recv()
        for i, c in pairs:
            s = 2 * h + i
            near, r1, r2 = xin[g, h, 0, i, c], xin[g, h, 1, i, c], xin[g, h, 2, i, c]
            w_in = (kx[g, 0, c] * ids[g, h, i, c] + kx[g, 1, c] * near) + (
                kx[g, 2, c] * r1 + kx[g, 3, c] * r2
            )
            wab[g, i_in, s, c] = w_in
            wab[g, i_out, s, c] = (
                kx[g, 4, c] * near + kx[g, 5, c] * ends[g, i_out, s, c] + kx[g, 6, c] * w_in
            )

    def backward(t, g, h, emit, acc):
        def body(step, carry):
            z = 7 - step
            acc_s, acc_n, w_next = carry
            res = []
            for i in range(2):
                s = 2 * h + i
                k = s * 8 + z
                both = []
                for c in range(2):
                    w = fw[g, s, z, c] + g_r[g, z, c] * wab[g, 0, s, c] + (
                        rt_r[g, z, c] * w_next[2 * i + c]
                    )
                    res.append(w)
                    v = emit(s, z, c, w)
                    if g == 1:
                        xp[t + 1, 0, c, pl.ds(k, 1), :] = v[0:1]
                        xp[t + 1, 1, c, pl.ds(k, 1), :] = v[15:16]
                    both.append(v)
                acc_s = jnp.where(lane == k, roll(both[0], k, 1), acc_s)
                acc_n = jnp.where(lane == k, roll(both[1], k + 1, 1), acc_n)
            return acc_s, acc_n, tuple(res)

        first = tuple(wab[g, 1, 2 * h + i, c] for i in range(2) for c in range(2))
        return loop(8, body, acc + (first,))[:2]

    def pack_y(t, g, acc):
        yp[t + 1, g, 0], yp[t + 1, g, 1] = acc
        send_y(t + 1, g)

    def put(ref, g, s, z, c, v):
        if g == 0:
            ref[s, z, c, 8:24] = v
        else:
            ref[s, z, c, 0:8] = v[0:8]
            ref[s, z, c, 24:32] = v[8:16]

    def emit_first(g):
        def emit(s, z, c, w):
            put(fp, g, s, z, c, w)
            return w
        return emit

    def emit_relaxed(g):
        rows = (1, 2) if g == 0 else (0, 3)
        def emit(s, z, c, w):
            change = w - centre(g, fp[s, z, c])
            put(ch, g, s, z, c, change)
            for i in range(2):
                on[s, z, c, pl.ds(rows[i], 8, stride=4), :] = w[8 * i:8 * i + 8]
            return change
        return emit

    def load_pot(s, z, c):
        return jnp.concatenate([p_nat[s, z, c, pl.ds(j, 8, stride=4), :] for j in range(4)], 0)

    def load_first(s, z, c):
        return fp[s, z, c]

    empty = (jnp.zeros((16, 128), F32),) * 2

    wait_y(0, 0)
    pl.when(has_d)(to_above.wait_recv)
    pl.when(has_u)(to_below.wait_recv)
    setup(0)
    end_factor(0)
    for h in range(2):
        forward(0, 0, h, load_pot)
        end_send(0, h)
    wait_y(0, 1)
    wait_x(0)
    setup(1)
    end_factor(1)
    for h in range(2):
        forward(1, 0, h, load_pot)
        end_send(1, h)
    for g in range(2):
        mid_factor(g)
        for h in range(2):
            mid_forward(g, h)
    for g in range(2):
        mid_match(g)
        acc = empty
        for h in range(2):
            mid_solve(g, h)
        for h in range(2):
            end_solve(g, h)
            acc = backward(0, g, h, emit_first(g), acc)
        if g == 1:
            send_x(1)
        pack_y(0, g, acc)
    for g in range(2):
        mid_extra(g)

    @pl.when(is_end)
    def _():
        kx[:, 7:9] = jnp.zeros((2, 2, 2, 16, 128), F32)

    wait_y(1, 0)
    for h in range(2):
        forward(0, 1, h, load_first)
        cross_send(0, h)
    wait_y(1, 1)
    wait_x(1)
    for h in range(2):
        forward(1, 1, h, load_first)
        cross_send(1, h)
    for g in range(2):
        end_extra(g)
        acc = empty
        for h in range(2):
            cross_solve(g, h)
            acc = backward(1, g, h, emit_relaxed(g), acc)
        if g == 1:
            send_x(2)
        pack_y(1, g, acc)
    out_cp = [
        pltpu.make_async_copy(on.at[:, :, c], out.at[:, :, :, c * 128:(c + 1) * 128], loc.at[0, c])
        for c in range(2)
    ]
    for cp in out_cp:
        cp.start()

    pick = (
        lax.broadcasted_iota(jnp.int32, (256, 128), 0) // 2
        == lax.broadcasted_iota(jnp.int32, (256, 128), 1)
    ).astype(F32)

    def defect(g):
        def body(z, carry):
            rows = []
            for s in range(4):
                near = neighbours(g, 2, s * 8 + z, [ch[s, z, c] for c in range(2)])
                both = []
                for c in range(2):
                    here, w, e, so, no = near[c]
                    d = (lw_r[g, z, c] * w + le_r[g, z, c] * e) + (
                        ls_r[g, z, c] * so + ln_r[g, z, c] * no
                    )
                    if g == 0:
                        df[s, z, c] = d
                    else:
                        both.append(d + df[s, z, c])
                if g == 1:
                    rows.append(jnp.concatenate(both, 1))
            if g == 1:
                d = jnp.dot(
                    jnp.concatenate(rows, 0), pick,
                    precision=lax.Precision.HIGHEST, preferred_element_type=F32,
                )
                for s in range(4):
                    co[s, z, pl.ds(0, 8, stride=2), :] = d[16 * s:16 * s + 8]
                    co[s, z, pl.ds(1, 8, stride=2), :] = d[16 * s + 8:16 * s + 16]
            return carry

        loop(8, body, 0)

    wait_y(2, 0)
    defect(0)
    wait_y(2, 1)
    wait_x(2)
    defect(1)
    co_cp = pltpu.make_async_copy(co, coarse, loc.at[1, 0])
    co_cp.start()

    for copy, where in started:
        if where is None:
            copy.wait_send()
        else:
            pl.when(where)(copy.wait_send)
    for cp in out_cp:
        cp.wait()
    co_cp.wait()


def store_kernel(relaxed, restricted, out, coarse, held, held_coarse, sems):
    fetch = [pltpu.make_async_copy(restricted, held_coarse, sems.at[0, 4])] + [
        pltpu.make_async_copy(relaxed.at[s], held.at[s], sems.at[0, s]) for s in range(4)
    ]
    store = [pltpu.make_async_copy(held_coarse, coarse, sems.at[1, 4])] + [
        pltpu.make_async_copy(held.at[s], out.at[s], sems.at[1, s]) for s in range(4)
    ]
    for cp in fetch:
        cp.start()
    for cp, then in zip(fetch, store):
        cp.wait()
        then.start()
    for cp in store:
        cp.wait()


def solution(mesh):
    nz, nx, ny = mesh.shape["gz"], mesh.shape["gx"], mesh.shape["gy"]

    def body(potential, labels, conductivity, electrodes):
        coef = pltpu.VMEM((2, 8, 2, 16, 128), F32)
        field = pltpu.VMEM((4, 8, 2, 32, 128), F32)
        msg = pltpu.VMEM((2, 2, 2, 2, 16, 128), F32)
        part1 = pltpu.VMEM((2, 2, 16, 128), F32)
        part2 = pltpu.VMEM((2, 2, 2, 16, 128), F32)
        part3 = pltpu.VMEM((2, 3, 2, 16, 128), F32)
        dma = pltpu.SemaphoreType.DMA
        shapes = (
            jax.ShapeDtypeStruct((4, 8, 32, 256), F32),
            jax.ShapeDtypeStruct((4, 8, 16, 128), F32),
        )
        anywhere = pl.BlockSpec(memory_space=pl.ANY)
        results = pl.pallas_call(
            functools.partial(kernel, nz, nx, ny),
            out_shape=shapes,
            in_specs=[
                pl.BlockSpec(memory_space=pl.ANY),
                pl.BlockSpec(memory_space=pl.ANY),
                pl.BlockSpec(memory_space=pltpu.SMEM),
                pl.BlockSpec(memory_space=pltpu.SMEM),
            ],
            out_specs=(pl.BlockSpec(memory_space=pl.ANY), pl.BlockSpec(memory_space=pl.ANY)),
            scratch_shapes=[
                field,
                pltpu.VMEM((8, 2, 32, 128), jnp.int32),
                pltpu.VMEM((10, 2, 32, 128), F32),
                pltpu.VMEM((3, 2, 2, 40, 128), F32),
                pltpu.VMEM((3, 2, 2, 40, 128), F32),
                pltpu.VMEM((3, 2, 2, 16, 128), F32),
                pltpu.VMEM((3, 2, 2, 16, 128), F32),
                pltpu.VMEM((4, 2, 32, 128), F32),
                coef, coef, coef, coef, coef, coef, coef, coef, coef,
                pltpu.VMEM((2, 4, 2, 16, 128), F32),
                pltpu.VMEM((2, 4, 8, 2, 16, 128), F32),
                field, field, field,
                pltpu.VMEM((4, 8, 2, 16, 128), F32),
                pltpu.VMEM((4, 8, 16, 128), F32),
                pltpu.VMEM((2, 2, 4, 2, 16, 128), F32),
                pltpu.VMEM((2, 2, 4, 2, 16, 128), F32),
                pltpu.VMEM((2, 3, 2, 16, 128), F32),
                pltpu.VMEM((2, 4, 2, 16, 128), F32),
                part1, part1, msg, msg, msg, msg, part2, part2, msg, msg, part3, part3, msg, msg,
                pltpu.VMEM((2, 2, 3, 2, 2, 16, 128), F32),
                pltpu.VMEM((2, 9, 2, 16, 128), F32),
                dma((2, 2)), dma((2,)), dma((2,)),
                dma((3, 2)), dma((3, 2)), dma((3, 2, 2)), dma((3, 2, 2)),
                dma((2, 2, 3)), dma((2, 2, 3)), dma((2, 3)), dma((2, 3)),
                dma((2, 2, 3)), dma((2, 2, 3)),
            ],
            compiler_params=pltpu.CompilerParams(
                collective_id=0, has_side_effects=True, vmem_limit_bytes=60 * 1024 * 1024,
            ),
        )(potential, labels, conductivity, electrodes)
        return pl.pallas_call(
            store_kernel,
            out_shape=shapes,
            in_specs=[anywhere, anywhere],
            out_specs=(anywhere, anywhere),
            scratch_shapes=[
                pltpu.VMEM((4, 8, 32, 256), F32),
                pltpu.VMEM((4, 8, 16, 128), F32),
                pltpu.SemaphoreType.DMA((2, 5)),
            ],
        )(*results)

    return jax.shard_map(
        body,
        mesh=mesh,
        in_specs=(P(None, "gz", "gx", "gy"), P("gz", "gx", "gy"), P(), P()),
        out_specs=(P(None, "gz", "gx", "gy"), P(None, "gz", "gx", "gy")),
        check_vma=False,
    )
```

```python
import functools

import jax
import jax.numpy as jnp
from jax import lax
from jax.experimental import pallas as pl
from jax.experimental.pallas import tpu as pltpu
from jax.sharding import PartitionSpec as P

ASPECT = 128
MESH = pl.DeviceIdType.MESH
F32 = jnp.float32
UNROLL = True


def roll(v, shift, axis):
    return pltpu.roll(v, shift, axis)


def recip(v):
    return pltpu.reciprocal(v, approx=True)


def loop(count, body, init):
    if UNROLL:
        for i in range(count):
            init = body(i, init)
        return init
    return lax.fori_loop(0, count, body, init)


def kernel(
    nz, nx, ny,
    pot, lab, cond, elec, out, coarse,
    p_nat, l_nat, sg, xp, xh, yp, yh, src,
    lw_r, le_r, ls_r, ln_r, inv_r, e_r, rt_r, g_r, r_r, ss,
    fw, fp, ch, on, df, co, ends, wab, km, tt,
    m0s, m0r, m1s, m1r, m2s, m2r, b2s, b2r, m3s, m3r, b3s, b3r, ods, ids, xin, kx,
    loc, zs, zr, xs, xr, ys, yr, ms, mr, bs, br, qs, qr,
):
    p = lax.axis_index("gz")
    gx = lax.axis_index("gx")
    gy = lax.axis_index("gy")
    has_w, has_e = gx > 0, gx < nx - 1
    has_u, has_d = p > 0, p < nz - 1
    up = p < nz // 2
    is_end = (p == 0) | (p == nz - 1)
    is_mid = (p > 0) & (p < nz - 1)
    west, east = {"gx": gx - 1}, {"gx": gx + 1}
    south, north = {"gy": lax.rem(gy + ny - 1, ny)}, {"gy": lax.rem(gy + 1, ny)}
    above, below = {"gz": p - 1}, {"gz": p + 1}
    lane = lax.broadcasted_iota(jnp.int32, (16, 128), 1)
    lane32 = lax.broadcasted_iota(jnp.int32, (32, 128), 1)
    sub8 = lax.broadcasted_iota(jnp.int32, (8, 128), 0)
    row16 = lax.broadcasted_iota(jnp.int32, (16, 128), 0)

    lab_cp = [
        pltpu.make_async_copy(lab.at[:, :, c * 128:(c + 1) * 128], l_nat.at[:, c], loc.at[0, c])
        for c in range(2)
    ]
    pot_cp = [
        pltpu.make_async_copy(pot.at[:, :, :, c * 128:(c + 1) * 128], p_nat.at[:, :, c], loc.at[1, c])
        for c in range(2)
    ]
    for cp in lab_cp + pot_cp:
        cp.start()

    @pl.when(gx == 0)
    def _():
        xh[:, 0] = jnp.zeros((3, 2, 40, 128), F32)

    @pl.when(gx == nx - 1)
    def _():
        xh[:, 1] = jnp.zeros((3, 2, 40, 128), F32)

    barrier = pltpu.get_barrier_semaphore()

    def greet(device):
        pl.semaphore_signal(barrier, inc=1, device_id=device, device_id_type=MESH)

    greet(south)
    greet(north)
    for step in range(1, nz):
        greet({"gz": lax.rem(p + step, nz)})
    for cond_here, device in ((has_w, west), (has_e, east)):
        pl.when(cond_here)(functools.partial(greet, device))

    for cp in lab_cp:
        cp.wait()
    table = [cond[i] for i in range(16)]

    def lookup(z, carry):
        for c in range(2):
            l = jnp.concatenate([l_nat[z, c, pl.ds(j, 8, stride=4), :] for j in range(4)], 0)
            level = table
            for bit in range(4):
                on_bit = (l & (1 << bit)) != 0
                level = [
                    jnp.where(on_bit, level[2 * i + 1], level[2 * i]) for i in range(len(level) // 2)
                ]
            sg[z + 1, c] = recip(level[0])
        return carry

    loop(8, lookup, 0)

    @pl.when(p == 0)
    def _():
        sg[0] = sg[1]

    @pl.when(p == nz - 1)
    def _():
        sg[9] = sg[8]

    def remote(src_ref, dst_ref, send, recv, device):
        return pltpu.make_async_remote_copy(
            src_ref=src_ref, dst_ref=dst_ref, send_sem=send, recv_sem=recv,
            device_id=device, device_id_type=MESH,
        )

    started = []

    def start(copy, where=None):
        started.append((copy, where))
        if where is None:
            copy.start()
        else:
            pl.when(where)(copy.start)

    to_above = remote(sg.at[1], sg.at[9], zs.at[0], zr.at[1], above)
    to_below = remote(sg.at[8], sg.at[0], zs.at[1], zr.at[0], below)

    def lateral_copies(t):
        n = 40 if t == 0 else 32
        return (
            remote(xp.at[t, 0, :, 0:n], xh.at[t, 1, :, 0:n], xs.at[t, 0], xr.at[t, 1], west),
            remote(xp.at[t, 1, :, 0:n], xh.at[t, 0, :, 0:n], xs.at[t, 1], xr.at[t, 0], east),
        )

    def y_copies(t, g):
        return (
            remote(yp.at[t, g, 0], yh.at[t, g, 1], ys.at[t, g, 0], yr.at[t, g, 1], south),
            remote(yp.at[t, g, 1], yh.at[t, g, 0], ys.at[t, g, 1], yr.at[t, g, 0], north),
        )

    lat = [lateral_copies(t) for t in range(3)]
    laty = [[y_copies(t, g) for g in range(2)] for t in range(3)]

    def send_x(t):
        start(lat[t][0], has_w)
        start(lat[t][1], has_e)

    def send_y(t, g):
        for copy in laty[t][g]:
            start(copy)

    def wait_x(t):
        pl.when(has_e)(lat[t][0].wait_recv)
        pl.when(has_w)(lat[t][1].wait_recv)

    def wait_y(t, g):
        for copy in laty[t][g]:
            copy.wait_recv()

    def pack_sigma(z, acc):
        acc_s, acc_n = acc
        v0, v1 = sg[z + 1, 0], sg[z + 1, 1]
        acc_s = jnp.where(lane32 == 32 + z, roll(v0, 32 + z, 1), acc_s)
        acc_n = jnp.where(lane32 == 32 + z, roll(v1, 33 + z, 1), acc_n)
        for c, v in ((0, v0), (1, v1)):
            xp[0, 0, c, pl.ds(32 + z, 1), :] = v[0:1]
            xp[0, 1, c, pl.ds(32 + z, 1), :] = v[31:32]
        return acc_s, acc_n

    zero32 = jnp.zeros((32, 128), F32)
    acc = loop(8, pack_sigma, (zero32, zero32))
    for cp in pot_cp:
        cp.wait()

    def pack_pot(z, acc):
        acc_s, acc_n = acc
        for s in range(4):
            k = s * 8 + z
            v0, v1 = (
                jnp.concatenate([p_nat[s, z, c, pl.ds(j, 8, stride=4), :] for j in range(4)], 0)
                for c in range(2)
            )
            acc_s = jnp.where(lane32 == k, roll(v0, k, 1), acc_s)
            acc_n = jnp.where(lane32 == k, roll(v1, k + 1, 1), acc_n)
            for c in range(2):
                xp[0, 0, c, pl.ds(k, 1), :] = p_nat[s, z, c, 0:1, :]
                xp[0, 1, c, pl.ds(k, 1), :] = p_nat[s, z, c, 31:32, :]
        return acc_s, acc_n

    acc = loop(8, pack_pot, acc)
    for d in range(2):
        yp[0, 0, d] = acc[d][8:24]
        yp[0, 1, d] = jnp.concatenate([acc[d][0:8], acc[d][24:32]], 0)
    pl.semaphore_wait(
        barrier,
        nz + 1 + has_w.astype(jnp.int32) + has_e.astype(jnp.int32),
    )

    start(to_above, has_u)
    start(to_below, has_d)
    send_y(0, 0)
    send_y(0, 1)
    send_x(0)

    here = jnp.where(p == 0, 4.0 * ASPECT, 0.0).astype(F32)
    row32 = lax.broadcasted_iota(jnp.int32, (32, 128), 0)
    x_cell = gx * 32 + 4 * (row32 % 8) + row32 // 8
    for c in range(2):
        y_cell = gy * 256 + c * 128 + lane32
        for s in range(4):
            first = jnp.where((x_cell == elec[s, 0]) & (y_cell == elec[s, 1]), here, 0.0)
            second = jnp.where((x_cell == elec[s, 2]) & (y_cell == elec[s, 3]), here, 0.0)
            src[s, c] = first - second

    def centre(g, v):
        return v[8:24] if g == 0 else jnp.concatenate([v[0:8], v[24:32]], 0)

    def west_east(g, v, halo_w, halo_e):
        if g == 0:
            return v[0:16], v[16:32]
        w0 = jnp.where(sub8 == 0, halo_w(), roll(v[24:32], 1, 0))
        e3 = jnp.where(sub8 == 7, halo_e(), roll(v[0:8], 7, 0))
        return jnp.concatenate([w0, v[16:24]], 0), jnp.concatenate([v[8:16], e3], 0)

    def south_north(v0, v1, halo_s, halo_n):
        r0, r1, q0, q1 = roll(v0, 1, 1), roll(v1, 1, 1), roll(v0, 127, 1), roll(v1, 127, 1)
        return (
            (jnp.where(lane == 0, halo_s, r0), jnp.where(lane == 127, q1, q0)),
            (jnp.where(lane == 0, r0, r1), jnp.where(lane == 127, halo_n, q1)),
        )

    def neighbours(g, t, k, v):
        halo_s = roll(yh[t, g, 0], lax.rem(128 - k, 128), 1)
        halo_n = roll(yh[t, g, 1], 127 - k, 1)
        ctr = [centre(g, v[c]) for c in range(2)]
        sn = south_north(ctr[0], ctr[1], halo_s, halo_n)
        res = []
        for c in range(2):
            w, e = west_east(
                g, v[c],
                lambda: xh[t, 0, c, pl.ds(k, 1), :],
                lambda: xh[t, 1, c, pl.ds(k, 1), :],
            )
            res.append((ctr[c], w, e) + sn[c])
        return res

    one = jnp.ones((16, 128), F32)
    mask_w = jnp.where(row16 == 0, jnp.where(has_w, 1.0, 0.0).astype(F32), one)
    mask_e = jnp.where(row16 == 15, jnp.where(has_e, 1.0, 0.0).astype(F32), one)
    mask_s = jnp.where(lane == 0, jnp.where(gy > 0, 1.0, 0.0).astype(F32), one)
    mask_n = jnp.where(lane == 127, jnp.where(gy < ny - 1, 1.0, 0.0).astype(F32), one)
    depth2 = 2.0 * ASPECT * ASPECT

    def setup(g):
        top = jnp.where(has_u, depth2, 0.0).astype(F32)
        zero = jnp.zeros((16, 128), F32)
        init = tuple(
            (
                top * recip(centre(g, sg[0, c]) + centre(g, sg[1, c])),
                zero, one, one, zero,
            )
            for c in range(2)
        )

        def body(z, carry):
            near = neighbours(g, 0, 32 + z, [sg[z + 1, c] for c in range(2)])
            res = []
            for c in range(2):
                sh, ratio, gg, rr, s00 = carry[c]
                here, w, e, s, n = near[c]
                lw, le = 2.0 * recip(here + w), 2.0 * recip(here + e)
                ls, ln = 2.0 * recip(here + s), 2.0 * recip(here + n)
                if g == 1:
                    lw, le = lw * mask_w, le * mask_e
                if c == 0:
                    ls = ls * mask_s
                else:
                    ln = ln * mask_n
                dp = depth2 * recip(here + centre(g, sg[z + 2, c]))
                diag = sh + dp + lw + le + ls + ln
                inv = recip(diag - sh * ratio)
                ee = sh * inv
                ratio = dp * inv
                gg = ee * gg
                s00 = s00 + rr * gg
                lw_r[g, z, c], le_r[g, z, c], ls_r[g, z, c], ln_r[g, z, c] = lw, le, ls, ln
                inv_r[g, z, c], rt_r[g, z, c], g_r[g, z, c], r_r[g, z, c] = inv, ratio, gg, rr
                e_r[g, z, c] = jnp.where(z == 0, inv, ee)
                res.append((dp, ratio, gg, rr * ratio, s00))
            return tuple(res)

        last = loop(8, body, init)
        for c in range(2):
            ss[g, 0, c], ss[g, 1, c], ss[g, 2, c], ss[g, 3, c] = (
                last[c][4], last[c][2], last[c][3], last[c][1],
            )

    def forward(g, t, half, load):
        if True:
            def body(z, carry):
                res = []
                for i in range(2):
                    s = 2 * half + i
                    near = neighbours(g, t, s * 8 + z, [load(s, z, c) for c in range(2)])
                    for c in range(2):
                        f, first = carry[2 * i + c]
                        here, w, e, so, no = near[c]
                        rhs = (lw_r[g, z, c] * w + le_r[g, z, c] * e) + (
                            ls_r[g, z, c] * so + ln_r[g, z, c] * no
                        )
                        f = rhs * inv_r[g, z, c] + e_r[g, z, c] * f
                        fw[g, s, z, c] = f
                        res.append((f, first + r_r[g, z, c] * f))
                return tuple(res)

            zero = jnp.zeros((16, 128), F32)
            init = tuple(
                (centre(g, src[2 * half + i, c]), zero) for i in range(2) for c in range(2)
            )
            last = loop(8, body, init)
            for i in range(2):
                for c in range(2):
                    ends[g, 1, 2 * half + i, c], ends[g, 0, 2 * half + i, c] = last[2 * i + c]

    i_out, i_in = jnp.where(up, 0, 1), jnp.where(up, 1, 0)
    i_oo, i_oi = jnp.where(up, 0, 3), jnp.where(up, 1, 2)
    i_io, i_ii = jnp.where(up, 2, 1), jnp.where(up, 3, 0)
    end_of = {"gz": jnp.where(up, 0, nz - 1)}
    mid_of = {"gz": jnp.where(up, 1, nz - 2)}
    twin = {"gz": nz - 1 - p}
    mate = {"gz": jnp.where(lax.rem(p, 2) == 0, p + 1, p - 1)}
    far_mid = {"gz": jnp.where(up, nz - 2, 1)}
    far_end = {"gz": jnp.where(up, nz - 1, 0)}
    i_od = jnp.where(is_end, i_in, i_out)
    slot = jnp.where(is_end, 2, 1)

    def hops(g, h):
        return (
            remote(m1s.at[g, h], m1r.at[g, h], ms.at[g, h, 0], mr.at[g, h, 0], mid_of),
            remote(m2s.at[g, h], m2r.at[g, h], ms.at[g, h, 1], mr.at[g, h, 1], twin),
            remote(m3s.at[g, h], m3r.at[g, h], ms.at[g, h, 2], mr.at[g, h, 2], end_of),
        )

    def factor_hops(g):
        return (
            remote(m0s.at[g], m0r.at[g], bs.at[g, 0], br.at[g, 0], mid_of),
            remote(b2s.at[g], b2r.at[g], bs.at[g, 1], br.at[g, 1], twin),
            remote(b3s.at[g], b3r.at[g], bs.at[g, 2], br.at[g, 2], end_of),
        )

    def cross(g, h):
        def one_of(src_ref, at, i, device):
            return remote(src_ref.at[g, h], xin.at[g, h, at], qs.at[g, h, i], qr.at[g, h, at], device)
        return (
            one_of(ids, slot, 0, far_mid), one_of(ids, slot, 1, far_end), one_of(ods, 0, 2, mate),
        )

    hop = [[hops(g, h) for h in range(2)] for g in range(2)]
    fhop = [factor_hops(g) for g in range(2)]
    pairs = [(i, c) for i in range(2) for c in range(2)]

    def end_factor(g):
        @pl.when(is_end)
        def _():
            m0s[g] = ss[g, i_ii]
        start(fhop[g][0], is_end)

    def end_send(g, h):
        @pl.when(is_end)
        def _():
            for i, c in pairs:
                m1s[g, h, i, c] = ends[g, i_in, 2 * h + i, c]
        start(hop[g][h][0], is_end)

    def mid_factor(g):
        @pl.when(is_mid)
        def _():
            fhop[g][0].wait_recv()
            for c in range(2):
                b_out = m0r[g, c]
                q = 1.0 / (1.0 - ss[g, i_oo, c] * b_out)
                km[g, 0, c] = q
                km[g, 1, c] = q * ss[g, i_io, c]
                b2s[g, 0, c] = ss[g, i_ii, c] + ss[g, i_oi, c] * b_out * q * ss[g, i_io, c]
                b2s[g, 1, c] = ss[g, i_oi, c] * q
        start(fhop[g][1], is_mid)

    def mid_forward(g, h):
        @pl.when(is_mid)
        def _():
            hop[g][h][0].wait_recv()
            for i, c in pairs:
                s = 2 * h + i
                a_out = m1r[g, h, i, c]
                first = (ends[g, i_out, s, c] + ss[g, i_oo, c] * a_out) * km[g, 0, c]
                tt[g, s, c] = first
                m2s[g, h, i, c] = ends[g, i_in, s, c] + ss[g, i_oi, c] * (a_out + m0r[g, c] * first)
        start(hop[g][h][1], is_mid)

    def mid_match(g):
        @pl.when(is_mid)
        def _():
            fhop[g][1].wait_recv()
            for c in range(2):
                km[g, 2, c] = 1.0 / (1.0 - b2r[g, 0, c] * b2s[g, 0, c])

    def mid_solve(g, h):
        @pl.when(is_mid)
        def _():
            hop[g][h][1].wait_recv()
            for i, c in pairs:
                s = 2 * h + i
                w_in = (m2r[g, h, i, c] + b2r[g, 0, c] * m2s[g, h, i, c]) * km[g, 2, c]
                first = tt[g, s, c] + km[g, 1, c] * w_in
                m3s[g, h, i, c] = first
                wab[g, i_in, s, c] = w_in
                wab[g, i_out, s, c] = m1r[g, h, i, c] + m0r[g, c] * first
        start(hop[g][h][2], is_mid)

    def end_solve(g, h):
        @pl.when(is_end)
        def _():
            hop[g][h][2].wait_recv()
            for i, c in pairs:
                wab[g, i_in, 2 * h + i, c] = m3r[g, h, i, c]
                wab[g, i_out, 2 * h + i, c] = jnp.zeros((16, 128), F32)

    def mid_extra(g):
        @pl.when(is_mid)
        def _():
            for c in range(2):
                b_out, b_in, q = m0r[g, c], b2r[g, 0, c], km[g, 0, c]
                s_oo, s_oi, s_io, s_ii = ss[g, i_oo, c], ss[g, i_oi, c], ss[g, i_io, c], ss[g, i_ii, c]
                g_mine, g_in, match = b2s[g, 1, c], b2r[g, 1, c], km[g, 2, c]
                r = 1.0 / (1.0 - s_ii * b_in)
                h = s_io * r
                b3s[g, 0, c] = s_oo + h * b_in * s_oi
                b3s[g, 1, c] = h
                b3s[g, 2, c] = h * g_in
                kx[g, 0, c] = match * b_in
                kx[g, 1, c] = match * b_in * g_mine
                kx[g, 2, c] = match
                kx[g, 3, c] = match * g_in
                kx[g, 4, c] = q
                kx[g, 5, c] = b_out * q
                kx[g, 6, c] = b_out * q * s_io
                kx[g, 7, c] = s_oi * b_out * q
                kx[g, 8, c] = h * b_in
        start(fhop[g][2], is_mid)

    def end_extra(g):
        @pl.when(is_end)
        def _():
            fhop[g][2].wait_recv()
            for c in range(2):
                c_in = b3r[g, 0, c]
                k = 1.0 / (1.0 - c_in * ss[g, i_ii, c])
                kx[g, 0, c] = k * c_in
                kx[g, 1, c] = k
                kx[g, 2, c] = k * b3r[g, 1, c]
                kx[g, 3, c] = k * b3r[g, 2, c]
                for i in range(4, 7):
                    kx[g, i, c] = jnp.zeros((16, 128), F32)

    def cross_send(g, h):
        for i, c in pairs:
            s = 2 * h + i
            ids[g, h, i, c] = ends[g, i_in, s, c] + kx[g, 7, c] * ends[g, i_out, s, c]
            ods[g, h, i, c] = ends[g, i_od, s, c] + kx[g, 8, c] * ends[g, i_in, s, c]
        for copy in cross(g, h):
            start(copy)

    def cross_solve(g, h):
        for at in range(3):
            remote(
                ids.at[g, h], xin.at[g, h, at], qs.at[g, h, 0], qr.at[g, h, at], far_mid
            ).wait_recv()
        for i, c in pairs:
            s = 2 * h + i
            near, r1, r2 = xin[g, h, 0, i, c], xin[g, h, 1, i, c], xin[g, h, 2, i, c]
            w_in = (kx[g, 0, c] * ids[g, h, i, c] + kx[g, 1, c] * near) + (
                kx[g, 2, c] * r1 + kx[g, 3, c] * r2
            )
            wab[g, i_in, s, c] = w_in
            wab[g, i_out, s, c] = (
                kx[g, 4, c] * near + kx[g, 5, c] * ends[g, i_out, s, c] + kx[g, 6, c] * w_in
            )

    def backward(t, g, h, emit, acc):
        def body(step, carry):
            z = 7 - step
            acc_s, acc_n, w_next = carry
            res = []
            for i in range(2):
                s = 2 * h + i
                k = s * 8 + z
                both = []
                for c in range(2):
                    w = fw[g, s, z, c] + g_r[g, z, c] * wab[g, 0, s, c] + (
                        rt_r[g, z, c] * w_next[2 * i + c]
                    )
                    res.append(w)
                    v = emit(s, z, c, w)
                    if g == 1:
                        xp[t + 1, 0, c, pl.ds(k, 1), :] = v[0:1]
                        xp[t + 1, 1, c, pl.ds(k, 1), :] = v[15:16]
                    both.append(v)
                acc_s = jnp.where(lane == k, roll(both[0], k, 1), acc_s)
                acc_n = jnp.where(lane == k, roll(both[1], k + 1, 1), acc_n)
            return acc_s, acc_n, tuple(res)

        first = tuple(wab[g, 1, 2 * h + i, c] for i in range(2) for c in range(2))
        return loop(8, body, acc + (first,))[:2]

    def pack_y(t, g, acc):
        yp[t + 1, g, 0], yp[t + 1, g, 1] = acc
        send_y(t + 1, g)

    def put(ref, g, s, z, c, v):
        if g == 0:
            ref[s, z, c, 8:24] = v
        else:
            ref[s, z, c, 0:8] = v[0:8]
            ref[s, z, c, 24:32] = v[8:16]

    def emit_first(g):
        def emit(s, z, c, w):
            put(fp, g, s, z, c, w)
            return w
        return emit

    def emit_relaxed(g):
        rows = (1, 2) if g == 0 else (0, 3)
        def emit(s, z, c, w):
            change = w - centre(g, fp[s, z, c])
            put(ch, g, s, z, c, change)
            for i in range(2):
                on[s, z, c, pl.ds(rows[i], 8, stride=4), :] = w[8 * i:8 * i + 8]
            return change
        return emit

    def load_pot(s, z, c):
        return jnp.concatenate([p_nat[s, z, c, pl.ds(j, 8, stride=4), :] for j in range(4)], 0)

    def load_first(s, z, c):
        return fp[s, z, c]

    empty = (jnp.zeros((16, 128), F32),) * 2

    wait_y(0, 0)
    pl.when(has_d)(to_above.wait_recv)
    pl.when(has_u)(to_below.wait_recv)
    setup(0)
    end_factor(0)
    for h in range(2):
        forward(0, 0, h, load_pot)
        end_send(0, h)
    wait_y(0, 1)
    wait_x(0)
    setup(1)
    end_factor(1)
    for h in range(2):
        forward(1, 0, h, load_pot)
        end_send(1, h)
    for g in range(2):
        mid_factor(g)
        for h in range(2):
            mid_forward(g, h)
    for g in range(2):
        mid_match(g)
        for h in range(2):
            mid_solve(g, h)
    for g in range(2):
        acc = empty
        for h in range(2):
            end_solve(g, h)
            acc = backward(0, g, h, emit_first(g), acc)
        pack_y(0, g, acc)
        if g == 1:
            send_x(1)
    for g in range(2):
        mid_extra(g)

    @pl.when(is_end)
    def _():
        kx[:, 7:9] = jnp.zeros((2, 2, 2, 16, 128), F32)

    wait_y(1, 0)
    for h in range(2):
        forward(0, 1, h, load_first)
        cross_send(0, h)
    wait_y(1, 1)
    wait_x(1)
    for h in range(2):
        forward(1, 1, h, load_first)
        cross_send(1, h)
    for g in range(2):
        end_extra(g)
        acc = empty
        for h in range(2):
            cross_solve(g, h)
            acc = backward(1, g, h, emit_relaxed(g), acc)
        pack_y(1, g, acc)
        if g == 1:
            send_x(2)
    out_cp = [
        pltpu.make_async_copy(on.at[:, :, c], out.at[:, :, :, c * 128:(c + 1) * 128], loc.at[0, c])
        for c in range(2)
    ]
    for cp in out_cp:
        cp.start()

    pick = (
        lax.broadcasted_iota(jnp.int32, (256, 128), 0) // 2
        == lax.broadcasted_iota(jnp.int32, (256, 128), 1)
    ).astype(F32)

    def defect(g):
        def body(z, carry):
            rows = []
            for s in range(4):
                near = neighbours(g, 2, s * 8 + z, [ch[s, z, c] for c in range(2)])
                both = []
                for c in range(2):
                    here, w, e, so, no = near[c]
                    d = (lw_r[g, z, c] * w + le_r[g, z, c] * e) + (
                        ls_r[g, z, c] * so + ln_r[g, z, c] * no
                    )
                    if g == 0:
                        df[s, z, c] = d
                    else:
                        both.append(d + df[s, z, c])
                if g == 1:
                    rows.append(jnp.concatenate(both, 1))
            if g == 1:
                d = jnp.dot(
                    jnp.concatenate(rows, 0), pick,
                    precision=lax.Precision.HIGHEST, preferred_element_type=F32,
                )
                for s in range(4):
                    co[s, z, pl.ds(0, 8, stride=2), :] = d[16 * s:16 * s + 8]
                    co[s, z, pl.ds(1, 8, stride=2), :] = d[16 * s + 8:16 * s + 16]
            return carry

        loop(8, body, 0)

    wait_y(2, 0)
    defect(0)
    wait_y(2, 1)
    wait_x(2)
    defect(1)
    co_cp = pltpu.make_async_copy(co, coarse, loc.at[1, 0])
    co_cp.start()

    for copy, where in started:
        if where is None:
            copy.wait_send()
        else:
            pl.when(where)(copy.wait_send)
    for cp in out_cp:
        cp.wait()
    co_cp.wait()


def store_kernel(relaxed, restricted, out, coarse, held, held_coarse, sems):
    fetch = [pltpu.make_async_copy(restricted, held_coarse, sems.at[0, 4])] + [
        pltpu.make_async_copy(relaxed.at[s], held.at[s], sems.at[0, s]) for s in range(4)
    ]
    store = [pltpu.make_async_copy(held_coarse, coarse, sems.at[1, 4])] + [
        pltpu.make_async_copy(held.at[s], out.at[s], sems.at[1, s]) for s in range(4)
    ]
    for cp in fetch:
        cp.start()
    for cp, then in zip(fetch, store):
        cp.wait()
        then.start()
    for cp in store:
        cp.wait()


def solution(mesh):
    nz, nx, ny = mesh.shape["gz"], mesh.shape["gx"], mesh.shape["gy"]

    def body(potential, labels, conductivity, electrodes):
        coef = pltpu.VMEM((2, 8, 2, 16, 128), F32)
        field = pltpu.VMEM((4, 8, 2, 32, 128), F32)
        msg = pltpu.VMEM((2, 2, 2, 2, 16, 128), F32)
        part1 = pltpu.VMEM((2, 2, 16, 128), F32)
        part2 = pltpu.VMEM((2, 2, 2, 16, 128), F32)
        part3 = pltpu.VMEM((2, 3, 2, 16, 128), F32)
        dma = pltpu.SemaphoreType.DMA
        shapes = (
            jax.ShapeDtypeStruct((4, 8, 32, 256), F32),
            jax.ShapeDtypeStruct((4, 8, 16, 128), F32),
        )
        anywhere = pl.BlockSpec(memory_space=pl.ANY)
        results = pl.pallas_call(
            functools.partial(kernel, nz, nx, ny),
            out_shape=shapes,
            in_specs=[
                pl.BlockSpec(memory_space=pl.ANY),
                pl.BlockSpec(memory_space=pl.ANY),
                pl.BlockSpec(memory_space=pltpu.SMEM),
                pl.BlockSpec(memory_space=pltpu.SMEM),
            ],
            out_specs=(pl.BlockSpec(memory_space=pl.ANY), pl.BlockSpec(memory_space=pl.ANY)),
            scratch_shapes=[
                field,
                pltpu.VMEM((8, 2, 32, 128), jnp.int32),
                pltpu.VMEM((10, 2, 32, 128), F32),
                pltpu.VMEM((3, 2, 2, 40, 128), F32),
                pltpu.VMEM((3, 2, 2, 40, 128), F32),
                pltpu.VMEM((3, 2, 2, 16, 128), F32),
                pltpu.VMEM((3, 2, 2, 16, 128), F32),
                pltpu.VMEM((4, 2, 32, 128), F32),
                coef, coef, coef, coef, coef, coef, coef, coef, coef,
                pltpu.VMEM((2, 4, 2, 16, 128), F32),
                pltpu.VMEM((2, 4, 8, 2, 16, 128), F32),
                field, field, field,
                pltpu.VMEM((4, 8, 2, 16, 128), F32),
                pltpu.VMEM((4, 8, 16, 128), F32),
                pltpu.VMEM((2, 2, 4, 2, 16, 128), F32),
                pltpu.VMEM((2, 2, 4, 2, 16, 128), F32),
                pltpu.VMEM((2, 3, 2, 16, 128), F32),
                pltpu.VMEM((2, 4, 2, 16, 128), F32),
                part1, part1, msg, msg, msg, msg, part2, part2, msg, msg, part3, part3, msg, msg,
                pltpu.VMEM((2, 2, 3, 2, 2, 16, 128), F32),
                pltpu.VMEM((2, 9, 2, 16, 128), F32),
                dma((2, 2)), dma((2,)), dma((2,)),
                dma((3, 2)), dma((3, 2)), dma((3, 2, 2)), dma((3, 2, 2)),
                dma((2, 2, 3)), dma((2, 2, 3)), dma((2, 3)), dma((2, 3)),
                dma((2, 2, 3)), dma((2, 2, 3)),
            ],
            compiler_params=pltpu.CompilerParams(
                collective_id=0, has_side_effects=True, vmem_limit_bytes=60 * 1024 * 1024,
            ),
        )(potential, labels, conductivity, electrodes)
        return pl.pallas_call(
            store_kernel,
            out_shape=shapes,
            in_specs=[anywhere, anywhere],
            out_specs=(anywhere, anywhere),
            scratch_shapes=[
                pltpu.VMEM((4, 8, 32, 256), F32),
                pltpu.VMEM((4, 8, 16, 128), F32),
                pltpu.SemaphoreType.DMA((2, 5)),
            ],
        )(*results)

    return jax.shard_map(
        body,
        mesh=mesh,
        in_specs=(P(None, "gz", "gx", "gy"), P("gz", "gx", "gy"), P(), P()),
        out_specs=(P(None, "gz", "gx", "gy"), P(None, "gz", "gx", "gy")),
        check_vma=False,
    )
```
